128 devices in a mesh: gx: 8 (over x, core), gy: 16 (over y, z).
Axes of the slice: x: 4, y: 4, z: 4, core: 2. Of those that a mesh axis runs over, the one named last changes fastest.
Arguments:
- state_before: float32 [768, 5, 32768], P(('gx', 'gy')), as said below
- before_start: int32 [8, 16], replicated, may hold values from 0 to 61, as said below
- after_start: int32 [8, 16], replicated, may hold values from 0 to 61, as said below
- time_step: float32 [], replicated, may hold values from 0.02 to 0.03
Outputs:
- state_after: float32 [768, 5, 32768], P(('gx', 'gy'))
- added_mass: float32 [], replicated
The draws below stay inside these ranges and needn't reach their ends.
Inputs may be any that keep to these rules, and one draw needn't show every extreme that they name: state_before has density in 0.2 to 5, velocity components in -1 to 1 and pressure in 0.5 to 2; slots past an owner's blocks are read by no output. before_start[g, 0] = 0 and before_start[g, k] lies within 1 of k * 4; in every x-slab one entry is k * 4 + 1 and another k * 4 - 1; in x-slab 0 the last entry is (15) * 4 + 1. after_start[g, 0] = 0 and after_start[g, k] lies within 1 of k * 4; in every x-slab one entry is k * 4 + 1 and another k * 4 - 1; in x-slab 0 the last entry is (15) * 4 + 1.
All inputs are finite; a program needn't handle non-finite values.
Results may differ from the reference program's by a relative error of at most 0.0003.
Values sent between devices are 32-bit elements; how exact they have to be, the bound alone decides.
A program may use at most 128 MiB of HBM per device.

```python
import jax
import jax.numpy as jnp
import numpy as np
from jax import lax

NX = 512
NY = 512
NZ = 64
BS = 32
XB = 2
YB = 1
ZB = 2
TILE = 4
SLOTS = 6
HCAP = 1
BPS = 64
NBLK = 512
CELLS = 32768
N_GX = 8
N_GY = 16


GAMMA = 5.0 / 3.0


def boundary_starts(seed_key):
    key_one, key_two, key_three, key_four = jax.random.split(seed_key, 4)
    magnitude = jax.random.randint(key_one, (N_GX, N_GY), HCAP // 2, HCAP + 1)
    sign_flip = jax.random.randint(key_two, (N_GX, N_GY), 0, 2) * 2 - 1
    offsets = magnitude * sign_flip
    raised = jax.random.randint(key_three, (N_GX, 1), 1, N_GY)
    slab_row = jnp.arange(N_GX, dtype=jnp.int32)[:, None]
    raised = jnp.where(slab_row == 0, N_GY - 1, raised)
    lowered = (raised - 1 + jax.random.randint(key_four, (N_GX, 1), 1, N_GY - 1)) % (N_GY - 1) + 1
    column = jnp.arange(N_GY, dtype=jnp.int32)[None, :]
    offsets = jnp.where(column == raised, HCAP, offsets)
    offsets = jnp.where(column == lowered, -HCAP, offsets)
    offsets = jnp.where(column == 0, 0, offsets)
    return (column * TILE + offsets).astype(jnp.int32)


def draw_before_start(key, part):
    key = jax.random.fold_in(key, 11)
    return boundary_starts(key)


def draw_after_start(key, part):
    key = jax.random.fold_in(key, 23)
    return boundary_starts(key)


def draw_state_before(key, part):
    key = jax.random.fold_in(key, 5)
    key_one, key_two, key_three = jax.random.split(key, 3)
    field_shape = (N_GX * N_GY * SLOTS, BS * BS * BS)
    density = jnp.exp(jax.random.uniform(key_one, field_shape, jnp.float32, jnp.log(0.2), jnp.log(5.0)))
    velocity = jnp.clip(0.5 * jax.random.normal(key_two, (3,) + field_shape, jnp.float32), -1.0, 1.0)
    pressure = jnp.exp(jax.random.uniform(key_three, field_shape, jnp.float32, jnp.log(0.5), jnp.log(2.0)))
    momentum = density[None] * velocity
    energy = pressure / (GAMMA - 1.0) + 0.5 * density * jnp.sum(velocity * velocity, axis=0)
    fields = jnp.concatenate([density[None], momentum, energy[None]], axis=0)
    return jnp.transpose(fields, (1, 0, 2)).astype(jnp.float32)


def setup_inputs(seed: int = 0) -> dict:
    seeds = jax.random.split(jax.random.key(seed), 5)
    return {
        "state_before": draw_state_before(jax.random.fold_in(seeds[4], 71), 0),
        "before_start": draw_before_start(jax.random.fold_in(seeds[4], 71), 0),
        "after_start": draw_after_start(jax.random.fold_in(seeds[4], 71), 0),
        "time_step": jnp.clip(jax.random.uniform(seeds[3], (), jnp.float32, 0.02, 0.03), 0.02, 0.03),
    }


GAMMA = 5.0 / 3.0
FLOOR = 0.25

def block_order(extent_x, extent_y, extent_z):
    grid_x, grid_y, grid_z = np.meshgrid(np.arange(extent_x), np.arange(extent_y), np.arange(extent_z), indexing='ij')
    morton = np.zeros(grid_x.shape, np.int64)
    written = 0
    for depth_bit in range(max(extent_x, extent_y, extent_z).bit_length()):
        for coords, extent in ((grid_x, extent_x), (grid_y, extent_y), (grid_z, extent_z)):
            if extent - 1 >> depth_bit > 0:
                morton = morton | (coords >> depth_bit & 1) << written
                written += 1
    ranking = np.argsort(np.argsort(morton.reshape(-1), kind='stable'), kind='stable')
    return ranking.astype(np.int32)

def sine_table(length):
    indices = jnp.arange(1, length + 1, dtype=jnp.int32)
    product = indices[:, None] * indices[None, :] % (2 * (length + 1))
    return jnp.sin(jnp.pi * product.astype(jnp.float32) / (length + 1))

def eigenvalue(modes, length):
    return 2.0 * jnp.cos(jnp.pi * (modes + 1).astype(jnp.float32) / (length + 1)) - 2.0

def solve_columns(spectrum, eigen_x, eigen_y):
    depth = spectrum.shape[2]
    diagonal = jnp.broadcast_to((eigen_x[:, None] + eigen_y[None, :] - 2.0)[:, :, None], spectrum.shape).astype(spectrum.dtype)
    layers = jnp.arange(depth, dtype=jnp.int32)
    lower_band = jnp.broadcast_to(jnp.where(layers > 0, 1.0, 0.0).astype(spectrum.dtype), spectrum.shape)
    upper_band = jnp.broadcast_to(jnp.where(layers < depth - 1, 1.0, 0.0).astype(spectrum.dtype), spectrum.shape)
    return lax.linalg.tridiagonal_solve(lower_band, diagonal, upper_band, spectrum[..., None])[..., 0]

def primitive(conserved):
    density = conserved[0]
    velocity = conserved[1:4] / density
    kinetic = 0.5 * density * lax.optimization_barrier(jnp.sum(velocity * velocity, axis=0))
    pressure = (GAMMA - 1.0) * (conserved[4] - kinetic)
    return jnp.concatenate([density[None], velocity, pressure[None]], axis=0)

def limited(left_diff, right_diff):
    center = 0.5 * (left_diff + right_diff)
    magnitude = jnp.minimum(jnp.minimum(2.0 * jnp.abs(left_diff), 2.0 * jnp.abs(right_diff)), jnp.abs(center))
    return jnp.where(left_diff * right_diff > 0.0, jnp.sign(center) * magnitude, 0.0)

def euler_pieces(values, normal):
    density = values[0]
    velocity = values[1:4]
    pressure = values[4]
    normal_speed = velocity[normal]
    energy = pressure / (GAMMA - 1.0) + 0.5 * density * lax.optimization_barrier(jnp.sum(velocity * velocity, axis=0))
    conserved = jnp.concatenate([density[None], density * velocity, energy[None]], axis=0)
    fluxes = conserved * normal_speed
    fluxes = fluxes.at[1 + normal].add(pressure)
    fluxes = fluxes.at[4].add(pressure * normal_speed)
    sound_speed = jnp.sqrt(GAMMA * pressure / density)
    return (conserved, fluxes, normal_speed, sound_speed)

def hlle(left_state, right_state, normal):
    cons_left, flux_left, speed_left, sound_left = euler_pieces(left_state, normal)
    cons_right, flux_right, speed_right, sound_right = euler_pieces(right_state, normal)
    fastest = jnp.maximum(jnp.maximum(speed_left + sound_left, speed_right + sound_right), 0.0)
    slowest = jnp.minimum(jnp.minimum(speed_left - sound_left, speed_right - sound_right), 0.0)
    return (fastest * flux_left - slowest * flux_right + fastest * slowest * (cons_right - cons_left)) / (fastest - slowest)

def divergence(primitives, axis):
    cell_count = primitives.shape[axis] - 4

    def window(lower_edge, upper_edge):
        return lax.slice_in_dim(primitives, lower_edge, upper_edge, axis=axis)
    left_diff = window(1, cell_count + 3) - window(0, cell_count + 2)
    right_diff = window(2, cell_count + 4) - window(1, cell_count + 3)
    slopes = limited(left_diff, right_diff)
    middle = window(1, cell_count + 3)
    upper_face = middle + 0.5 * slopes
    lower_face = middle - 0.5 * slopes
    left_state = lax.slice_in_dim(upper_face, 0, cell_count + 1, axis=axis)
    right_state = lax.slice_in_dim(lower_face, 1, cell_count + 2, axis=axis)
    fluxes = hlle(left_state, right_state, axis - 1)
    return lax.slice_in_dim(fluxes, 1, cell_count + 1, axis=axis) - lax.slice_in_dim(fluxes, 0, cell_count, axis=axis)

def advance(planes, nearby, time_step):
    primitives = primitive(planes)
    change_x = divergence(primitives[:, :, 2:-2, 2:-2], 1)
    change_y = divergence(primitives[:, 2:-2, :, 2:-2], 2)
    change_z = divergence(primitives[:, 2:-2, 2:-2, :], 3)
    interior = planes[:, 2:-2, 2:-2, 2:-2]
    acceleration = jnp.stack([-0.5 * (nearby[2:, 1:-1, 1:-1] - nearby[:-2, 1:-1, 1:-1]), -0.5 * (nearby[1:-1, 2:, 1:-1] - nearby[1:-1, :-2, 1:-1]), -0.5 * (nearby[1:-1, 1:-1, 2:] - nearby[1:-1, 1:-1, :-2])], axis=0)
    gravity = jnp.concatenate([jnp.zeros_like(interior[:1]), interior[:1] * acceleration, lax.optimization_barrier(jnp.sum(interior[1:4] * acceleration, axis=0))[None]], axis=0)
    updated = interior - time_step * (change_x + change_y + change_z) + time_step * gravity
    density = jnp.maximum(updated[0], FLOOR)
    deficit = jnp.sum(density - updated[0])
    return (jnp.concatenate([density[None], updated[1:]], axis=0), deficit)

def sweep_blocks(state_pad, potential_pad, time_step, width):
    block_count = (state_pad.shape[1] - 4) // width

    def one_block(block_index):
        plane_start = block_index * width
        planes = lax.dynamic_slice_in_dim(state_pad, plane_start, width + 4, 1)
        nearby = lax.dynamic_slice_in_dim(potential_pad, plane_start, width + 2, 0)
        return advance(planes, nearby, time_step)
    pieces, deficits = lax.map(one_block, jnp.arange(block_count, dtype=jnp.int32))
    merged = jnp.transpose(pieces, (1, 0, 2, 3, 4))
    merged = merged.reshape((pieces.shape[1], block_count * width, pieces.shape[3], pieces.shape[4]))
    return (merged, jnp.sum(deficits))

def reference(state_before, before_start, after_start, time_step):
    ranking = jnp.asarray(block_order(XB, YB, ZB))
    inverse_rank = jnp.asarray(np.argsort(block_order(XB, YB, ZB)).astype(np.int32))
    positions = jnp.arange(BPS, dtype=jnp.int32)
    owner = lax.optimization_barrier(jnp.sum((before_start[:, None, :] <= positions[None, :, None]).astype(jnp.int32), axis=2)) - 1
    range_begin = jnp.take_along_axis(before_start, owner, axis=1)
    slab_ids = jnp.arange(N_GX, dtype=jnp.int32)[:, None]
    rows_before = (slab_ids * N_GY + owner) * SLOTS + positions[None, :] - range_begin
    blocks = jnp.take(state_before, rows_before.reshape(-1), axis=0)
    blocks = blocks.reshape((N_GX, N_GY, TILE, 5, CELLS))
    blocks = jnp.take(blocks, ranking, axis=2)
    blocks = blocks.reshape((N_GX, N_GY, XB, YB, ZB, 5, BS, BS, BS))
    state = jnp.transpose(blocks, (5, 0, 2, 6, 1, 3, 7, 4, 8)).reshape((5, NX, NY, NZ))
    source = 4.0 / NZ * state[0]
    sine_y = sine_table(NY)
    sine_x = sine_table(NX)
    along_y = jnp.einsum('ky,xyz->xkz', sine_y, source, precision=lax.Precision.HIGHEST)
    spectrum = jnp.einsum('kx,xyz->kyz', sine_x, along_y, precision=lax.Precision.HIGHEST)
    solved = solve_columns(spectrum, eigenvalue(jnp.arange(NX, dtype=jnp.int32), NX), eigenvalue(jnp.arange(NY, dtype=jnp.int32), NY))
    back_x = jnp.einsum('kx,kyz->xyz', sine_x, solved, precision=lax.Precision.HIGHEST) * (2.0 / (NX + 1))
    potential = jnp.einsum('ky,xkz->xyz', sine_y, back_x, precision=lax.Precision.HIGHEST) * (2.0 / (NY + 1))
    state_pad = jnp.pad(state, ((0, 0), (2, 2), (2, 2), (2, 2)), mode='edge')
    potential_pad = jnp.pad(potential, 1)
    new_state, deficit = sweep_blocks(state_pad, potential_pad, time_step, BS)
    added_mass = deficit / NBLK
    shaped = new_state.reshape((5, N_GX, XB, BS, N_GY, YB, BS, ZB, BS))
    shaped = jnp.transpose(shaped, (1, 4, 2, 5, 7, 0, 3, 6, 8)).reshape((N_GX, N_GY, TILE, 5, CELLS))
    shaped = jnp.take(shaped, inverse_rank, axis=2).reshape((N_GX * BPS, 5, CELLS))
    next_start = jnp.concatenate([after_start[:, 1:], jnp.full((N_GX, 1), BPS, jnp.int32)], axis=1)
    held = next_start - after_start
    slot_pos = jnp.arange(SLOTS, dtype=jnp.int32)
    wanted = jnp.minimum(after_start[:, :, None] + slot_pos[None, None, :], BPS - 1)
    flat_rows = (jnp.arange(N_GX, dtype=jnp.int32)[:, None, None] * BPS + wanted).reshape(-1)
    picked = jnp.take(shaped, flat_rows, axis=0).reshape((N_GX, N_GY, SLOTS, 5, CELLS))
    keep = slot_pos[None, None, :] < held[:, :, None]
    state_after = jnp.where(keep[:, :, :, None, None], picked, 0.0).reshape((N_GX * N_GY * SLOTS, 5, CELLS))
    return (state_after, added_mass)
```

```python
import jax
import jax.numpy as jnp
import numpy as np
from jax import lax
from jax.sharding import PartitionSpec as P

NX = 512
NY = 512
NZ = 64
BS = 32


GAMMA = 5.0 / 3.0
FLOOR = 0.25


def with_halo(block, sides, width):
    for axis, dim in sides:
        count = lax.axis_size(axis)
        forward = [(i, i + 1) for i in range(count - 1)]
        backward = [(target, source) for source, target in forward]
        low = lax.ppermute(
            lax.slice_in_dim(block, block.shape[dim] - width, None, axis=dim), axis, forward
        )
        high = lax.ppermute(lax.slice_in_dim(block, 0, width, axis=dim), axis, backward)
        block = jnp.concatenate([low, block, high], axis=dim)
    return block


def block_order(extent_x, extent_y, extent_z):
    grid_x, grid_y, grid_z = np.meshgrid(
        np.arange(extent_x), np.arange(extent_y), np.arange(extent_z), indexing="ij"
    )
    morton = np.zeros(grid_x.shape, np.int64)
    written = 0
    for depth_bit in range(max(extent_x, extent_y, extent_z).bit_length()):
        for coords, extent in ((grid_x, extent_x), (grid_y, extent_y), (grid_z, extent_z)):
            if extent - 1 >> depth_bit > 0:
                morton = morton | (coords >> depth_bit & 1) << written
                written += 1
    ranking = np.argsort(np.argsort(morton.reshape(-1), kind="stable"), kind="stable")
    return ranking.astype(np.int32)


def sine_table(length):
    indices = jnp.arange(1, length + 1, dtype=jnp.int32)
    product = indices[:, None] * indices[None, :] % (2 * (length + 1))
    return jnp.sin(jnp.pi * product.astype(jnp.float32) / (length + 1))


def eigenvalue(modes, length):
    return 2.0 * jnp.cos(jnp.pi * (modes + 1).astype(jnp.float32) / (length + 1)) - 2.0


def solve_columns(spectrum, eigen_x, eigen_y):
    depth = spectrum.shape[2]
    sine_z = sine_table(depth)
    eigen_z = eigenvalue(jnp.arange(depth, dtype=jnp.int32), depth)
    modes = jnp.einsum("xyz,zk->xyk", spectrum, sine_z, precision=lax.Precision.HIGHEST)
    modes = modes / (eigen_x[:, None, None] + eigen_y[None, :, None] + eigen_z[None, None, :])
    return jnp.einsum("xyk,kz->xyz", modes, sine_z, precision=lax.Precision.HIGHEST) * (2.0 / (depth + 1))


def primitive(conserved):
    density = conserved[0]
    velocity = conserved[1:4] / density
    kinetic = 0.5 * density * jnp.sum(velocity * velocity, axis=0)
    pressure = (GAMMA - 1.0) * (conserved[4] - kinetic)
    return jnp.concatenate([density[None], velocity, pressure[None]], axis=0)


def limited(left_diff, right_diff):
    center = 0.5 * (left_diff + right_diff)
    magnitude = jnp.minimum(
        jnp.minimum(2.0 * jnp.abs(left_diff), 2.0 * jnp.abs(right_diff)), jnp.abs(center)
    )
    return jnp.where(left_diff * right_diff > 0.0, jnp.sign(center) * magnitude, 0.0)


def euler_pieces(values, normal):
    density = values[0]
    velocity = values[1:4]
    pressure = values[4]
    normal_speed = velocity[normal]
    energy = pressure / (GAMMA - 1.0) + 0.5 * density * jnp.sum(velocity * velocity, axis=0)
    conserved = jnp.concatenate([density[None], density * velocity, energy[None]], axis=0)
    fluxes = conserved * normal_speed
    fluxes = fluxes.at[1 + normal].add(pressure)
    fluxes = fluxes.at[4].add(pressure * normal_speed)
    sound_speed = jnp.sqrt(GAMMA * pressure / density)
    return (conserved, fluxes, normal_speed, sound_speed)


def hlle(left_state, right_state, normal):
    cons_left, flux_left, speed_left, sound_left = euler_pieces(left_state, normal)
    cons_right, flux_right, speed_right, sound_right = euler_pieces(right_state, normal)
    fastest = jnp.maximum(jnp.maximum(speed_left + sound_left, speed_right + sound_right), 0.0)
    slowest = jnp.minimum(jnp.minimum(speed_left - sound_left, speed_right - sound_right), 0.0)
    return (
        fastest * flux_left - slowest * flux_right + fastest * slowest * (cons_right - cons_left)
    ) / (fastest - slowest)


def divergence(primitives, axis):
    cell_count = primitives.shape[axis] - 4

    def window(lower_edge, upper_edge):
        return lax.slice_in_dim(primitives, lower_edge, upper_edge, axis=axis)

    left_diff = window(1, cell_count + 3) - window(0, cell_count + 2)
    right_diff = window(2, cell_count + 4) - window(1, cell_count + 3)
    slopes = limited(left_diff, right_diff)
    middle = window(1, cell_count + 3)
    upper_face = middle + 0.5 * slopes
    lower_face = middle - 0.5 * slopes
    left_state = lax.slice_in_dim(upper_face, 0, cell_count + 1, axis=axis)
    right_state = lax.slice_in_dim(lower_face, 1, cell_count + 2, axis=axis)
    fluxes = hlle(left_state, right_state, axis - 1)
    return lax.slice_in_dim(fluxes, 1, cell_count + 1, axis=axis) - lax.slice_in_dim(
        fluxes, 0, cell_count, axis=axis
    )


def advance(planes, nearby, time_step):
    primitives = primitive(planes)
    change_x = divergence(primitives[:, :, 2:-2, 2:-2], 1)
    change_y = divergence(primitives[:, 2:-2, :, 2:-2], 2)
    change_z = divergence(primitives[:, 2:-2, 2:-2, :], 3)
    interior = planes[:, 2:-2, 2:-2, 2:-2]
    acceleration = jnp.stack(
        [
            -0.5 * (nearby[2:, 1:-1, 1:-1] - nearby[:-2, 1:-1, 1:-1]),
            -0.5 * (nearby[1:-1, 2:, 1:-1] - nearby[1:-1, :-2, 1:-1]),
            -0.5 * (nearby[1:-1, 1:-1, 2:] - nearby[1:-1, 1:-1, :-2]),
        ],
        axis=0,
    )
    gravity = jnp.concatenate(
        [
            jnp.zeros_like(interior[:1]),
            interior[:1] * acceleration,
            jnp.sum(interior[1:4] * acceleration, axis=0)[None],
        ],
        axis=0,
    )
    updated = interior - time_step * (change_x + change_y + change_z) + time_step * gravity
    density = jnp.maximum(updated[0], FLOOR)
    deficit = jnp.sum(density - updated[0])
    return (jnp.concatenate([density[None], updated[1:]], axis=0), deficit)


def sweep_blocks(state_pad, potential_pad, time_step, width):
    block_count = (state_pad.shape[1] - 4) // width

    def one_block(block_index):
        plane_start = block_index * width
        planes = lax.dynamic_slice_in_dim(state_pad, plane_start, width + 4, 1)
        nearby = lax.dynamic_slice_in_dim(potential_pad, plane_start, width + 2, 0)
        return advance(planes, nearby, time_step)

    pieces, deficits = lax.map(one_block, jnp.arange(block_count, dtype=jnp.int32))
    merged = jnp.transpose(pieces, (1, 0, 2, 3, 4))
    merged = merged.reshape(
        (pieces.shape[1], block_count * width, pieces.shape[3], pieces.shape[4])
    )
    return (merged, jnp.sum(deficits))


def to_tile(blocks, extent_x, extent_y, extent_z):
    ranking = jnp.asarray(block_order(extent_x, extent_y, extent_z))
    ordered = jnp.take(blocks, ranking, axis=0)
    field_count = blocks.shape[1]
    shaped = ordered.reshape((extent_x, extent_y, extent_z, field_count, BS, BS, BS))
    shaped = jnp.transpose(shaped, (3, 0, 4, 1, 5, 2, 6))
    return shaped.reshape((field_count, extent_x * BS, extent_y * BS, extent_z * BS))


def to_blocks(tile_cells, extent_x, extent_y, extent_z):
    inverse_rank = jnp.asarray(
        np.argsort(block_order(extent_x, extent_y, extent_z)).astype(np.int32)
    )
    field_count = tile_cells.shape[0]
    shaped = tile_cells.reshape((field_count, extent_x, BS, extent_y, BS, extent_z, BS))
    shaped = jnp.transpose(shaped, (1, 3, 5, 0, 2, 4, 6))
    shaped = shaped.reshape((extent_x * extent_y * extent_z, field_count, BS * BS * BS))
    return jnp.take(shaped, inverse_rank, axis=0)


def own_range(start_table, slab_index, column_index, inner_count, tile_blocks):
    row_starts = lax.dynamic_index_in_dim(start_table, slab_index, 0, keepdims=False)
    range_begin = lax.dynamic_index_in_dim(row_starts, column_index, 0, keepdims=False)
    next_begin = lax.dynamic_index_in_dim(
        row_starts, jnp.minimum(column_index + 1, inner_count - 1), 0, keepdims=False
    )
    range_end = jnp.where(column_index + 1 < inner_count, next_begin, tile_blocks * inner_count)
    return (
        range_begin - column_index * tile_blocks,
        range_end - (column_index + 1) * tile_blocks,
        range_end - range_begin,
    )


def swap_edges(send_rows, margin):
    return with_halo(send_rows, (("gy", 0),), margin)


def columns(field_rows):
    return lax.all_to_all(field_rows, "gy", split_axis=0, concat_axis=1, tiled=True)


def across(field_rows):
    return lax.all_to_all(field_rows, ("gx", "gy"), split_axis=1, concat_axis=0, tiled=True)


def outflow(padded, index_here, extent, axis):
    length = padded.shape[axis]
    low_plane = lax.slice_in_dim(padded, 2, 3, axis=axis)
    high_plane = lax.slice_in_dim(padded, length - 3, length - 2, axis=axis)
    line_shape = tuple((length if which == axis else 1 for which in range(padded.ndim)))
    cell_place = jnp.arange(length, dtype=jnp.int32).reshape(line_shape)
    replaced = jnp.where((cell_place < 2) & (index_here == 0), low_plane, padded)
    return jnp.where((cell_place >= length - 2) & (index_here == extent - 1), high_plane, replaced)


def per_device(state_before, before_start, after_start, time_step):
    outer_count = lax.axis_size("gx")
    inner_count = lax.axis_size("gy")
    slab_index = lax.axis_index("gx")
    column_index = lax.axis_index("gy")
    slot_count = state_before.shape[0]
    field_count = state_before.shape[1]
    tile_x = NX // outer_count
    tile_y = NY // inner_count
    blocks_x = tile_x // BS
    blocks_y = tile_y // BS
    blocks_z = NZ // BS
    tile_blocks = blocks_x * blocks_y * blocks_z
    margin = tile_blocks // 4
    lead, trail, held = own_range(before_start, slab_index, column_index, inner_count, tile_blocks)
    head_part = state_before[:margin]
    tail_part = lax.dynamic_slice_in_dim(state_before, held - margin, margin, 0)
    received = swap_edges(jnp.concatenate([head_part, tail_part], axis=0), margin)
    from_prev = received[:margin]
    from_next = received[3 * margin :]
    joined = jnp.concatenate([from_prev, state_before], axis=0)
    own_part = lax.dynamic_slice_in_dim(joined, margin - lead, tile_blocks, 0)
    spare = jnp.concatenate(
        [jnp.zeros((tile_blocks,) + state_before.shape[1:], jnp.float32), from_next], axis=0
    )
    next_part = lax.dynamic_slice_in_dim(spare, jnp.maximum(-trail, 0), tile_blocks, 0)
    position = jnp.arange(tile_blocks, dtype=jnp.int32)
    blocks = jnp.where((position >= tile_blocks + trail)[:, None, None], next_part, own_part)
    tile_cells = to_tile(blocks, blocks_x, blocks_y, blocks_z)
    source = 4.0 / NZ * tile_cells[0]
    sine_y = sine_table(NY)
    sine_x = sine_table(NX)
    spread = columns(source)
    along_y = jnp.einsum("ky,xyz->xkz", sine_y, spread, precision=lax.Precision.HIGHEST)
    whole_x = across(along_y)
    spectrum = jnp.einsum("kx,xyz->kyz", sine_x, whole_x, precision=lax.Precision.HIGHEST)
    row_count = spectrum.shape[1]
    first_mode = (slab_index * inner_count + column_index) * row_count
    modes_y = first_mode + jnp.arange(row_count, dtype=jnp.int32)
    solved = solve_columns(
        spectrum, eigenvalue(jnp.arange(NX, dtype=jnp.int32), NX), eigenvalue(modes_y, NY)
    )
    back_x = jnp.einsum("kx,kyz->yxz", sine_x, solved, precision=lax.Precision.HIGHEST) * (
        2.0 / (NX + 1)
    )
    whole_y = across(back_x)
    potential_rows = jnp.einsum("ky,kxz->yxz", sine_y, whole_y, precision=lax.Precision.HIGHEST) * (
        2.0 / (NY + 1)
    )
    potential = jnp.transpose(columns(potential_rows), (1, 0, 2))
    fields = jnp.concatenate([tile_cells, potential[None]], axis=0)
    ghosted = with_halo(fields, (("gx", 1), ("gy", 2)), 2)
    state_pad = outflow(ghosted[:field_count], slab_index, outer_count, 1)
    state_pad = outflow(state_pad, column_index, inner_count, 2)
    state_pad = jnp.pad(state_pad, ((0, 0), (0, 0), (0, 0), (2, 2)), mode="edge")
    potential_pad = jnp.pad(ghosted[field_count, 1:-1, 1:-1, :], ((0, 0), (0, 0), (1, 1)))
    new_tile, deficit = sweep_blocks(state_pad, potential_pad, time_step, BS)
    total_deficit = lax.psum(deficit, ("gx", "gy"))
    added_mass = total_deficit / (tile_blocks * inner_count * outer_count)
    new_blocks = to_blocks(new_tile, blocks_x, blocks_y, blocks_z)
    returned = swap_edges(
        jnp.concatenate([new_blocks[:margin], new_blocks[tile_blocks - margin :]], axis=0), margin
    )
    lead_after, trail_after, held_after = own_range(
        after_start, slab_index, column_index, inner_count, tile_blocks
    )
    extended = jnp.concatenate(
        [
            returned[:margin],
            new_blocks,
            returned[3 * margin :],
            jnp.zeros((slot_count,) + new_blocks.shape[1:], jnp.float32),
        ],
        axis=0,
    )
    chosen = lax.dynamic_slice_in_dim(extended, margin + lead_after, slot_count, 0)
    keep = jnp.arange(slot_count, dtype=jnp.int32) < held_after
    state_after = jnp.where(keep[:, None, None], chosen, 0.0)
    return (state_after, added_mass)


def solution(mesh):
    placed = (P(("gx", "gy"), None, None), P(), P(), P())
    return jax.shard_map(
        per_device,
        mesh=mesh,
        in_specs=placed,
        out_specs=(P(("gx", "gy"), None, None), P()),
        check_vma=False,
    )
```

```python
import jax
import jax.numpy as jnp
import numpy as np
from jax import lax
from jax.experimental import pallas as pl
from jax.experimental.pallas import tpu as pltpu
from jax.sharding import PartitionSpec as P

GAMMA = 5.0 / 3.0
FLOOR = 0.25
MESH = pl.DeviceIdType.MESH
HIGHEST = lax.Precision.HIGHEST

NK, NG = 16, 8


def tables():
    def sine(n):
        i = np.arange(1, n + 1)
        return np.sin(np.pi * ((i[:, None] * i[None, :]) % (2 * (n + 1))) / (n + 1))

    sine_y, sine_z = sine(512), sine(64)
    forward = np.zeros((16, 2, 4, 2, 64))
    for u in range(2):
        forward[:, u, :, u, :] = sine_z.reshape(16, 4, 64)
    forward = forward.reshape(128, 128)
    order = np.arange(512).reshape(16, 8, 4).transpose(0, 2, 1).reshape(512)
    ordered = sine_y[order]
    modes_y = 2 - 2 * np.cos(np.pi * np.arange(1, 513) / 513)
    modes_z = 2 - 2 * np.cos(np.pi * np.arange(1, 65) / 65)
    h = 0.5 * (modes_z[:, None] + modes_y[None, :])
    root = np.sqrt(h * (h + 2))
    lam = 1 / (1 + h + root)
    gain = -0.5 / root

    def rows(values):
        return np.broadcast_to(values.reshape(16, 1, 4, 512), (16, 2, 4, 512)).reshape(16, 8, 512)

    table = np.stack([rows(lam), rows(gain)], axis=1)
    f32 = np.float32
    return (
        (forward * (4.0 / 64)).astype(f32),
        (forward * (2.0 / 65)).astype(f32),
        ordered.astype(f32),
        np.ascontiguousarray(ordered.T * (2.0 / 513)).astype(f32),
        table.astype(f32),
    )


def lanes():
    return lax.broadcasted_iota(jnp.int32, (8, 128), 1)


def swap4(parts):
    group = lanes() // 32
    low, even = group < 2, group % 2 == 0
    a, b, c, d = parts
    a, c = jnp.where(low, a, pltpu.roll(c, 64, 1)), jnp.where(low, pltpu.roll(a, 64, 1), c)
    b, d = jnp.where(low, b, pltpu.roll(d, 64, 1)), jnp.where(low, pltpu.roll(b, 64, 1), d)
    a, b = jnp.where(even, a, pltpu.roll(b, 32, 1)), jnp.where(even, pltpu.roll(a, 96, 1), b)
    c, d = jnp.where(even, c, pltpu.roll(d, 32, 1)), jnp.where(even, pltpu.roll(c, 96, 1), d)
    return a, b, c, d


def half_slope(down, up):
    quarter = 0.25 * (down + up)
    low = jnp.minimum(jnp.maximum(down, up), 0.0)
    high = jnp.maximum(jnp.minimum(down, up), 0.0)
    return jnp.minimum(jnp.maximum(quarter, low), high)


def face_flux(left, right, normal):
    def side(w):
        rho, vx, vy, vz, p = w
        gp = GAMMA * p
        return gp * lax.rsqrt(gp * rho), 0.5 * (vx * vx + vy * vy + vz * vz)

    sound_l, half_l = side(left)
    sound_r, half_r = side(right)
    ul, ur = left[1 + normal], right[1 + normal]
    fast = jnp.maximum(jnp.maximum(ul + sound_l, ur + sound_r), 0.0)
    slow = jnp.minimum(jnp.minimum(ul - sound_l, ur - sound_r), 0.0)
    inverse = 1.0 / (fast - slow)
    a, b = fast * inverse, slow * inverse
    d = fast * b
    kl, kr = a * ul - d, d - b * ur
    gl, gr = left[0] * kl, right[0] * kr
    apl, bpr = a * left[4], b * right[4]
    out = [gl + gr]
    for i in range(3):
        term = gl * left[1 + i] + gr * right[1 + i]
        out.append(term + (apl - bpr) if i == normal else term)
    out.append(
        1.5 * (left[4] * kl + right[4] * kr) + (gl * half_l + gr * half_r) + (apl * ul - bpr * ur)
    )
    return out


def cell_flux(w, normal):
    rho, p, u = w[0], w[4], w[1 + normal]
    mass = rho * u
    out = [mass]
    for i in range(3):
        out.append(mass * w[1 + i] + p if i == normal else mass * w[1 + i])
    half = 0.5 * (w[1] * w[1] + w[2] * w[2] + w[3] * w[3])
    out.append(2.5 * p * u + mass * half)
    return out


def at8(row):
    return pl.ds(pl.multiple_of(row, 8), 8)


EDGE, REST, HALO, PHI, AFTER, A2A, BACK, MOM, DEF_Y, DEF_X, N_SEM = (
    0, 2, 4, 8, 12, 14, 30, 46, 54, 70, 78,
)


def step_kernel(
    st, before, dt_ref, bz_h, bzi_h, sf_h, si_h, tab_h,
    nb, added,
    raw, tmp, dense, tail, next_head, prev_tail, cons, prim, acc, pot, pot0,
    xs, xr, ys, yr, pxs, pxr, pys, pyr,
    spec_t, spec_r, lines, trans, vsol, back_t, back_r, mom, defs, dgx,
    bz, bzi, sf, si, tab, load_sem, ss, rs,
):
    g, k = lax.axis_index("gx"), lax.axis_index("gy")
    k_up, k_dn = (k + 1) % NK, (k + NK - 1) % NK
    g_up, g_dn = (g + 1) % NG, (g + NG - 1) % NG
    dt = dt_ref[0, 0]
    lane = lanes()
    sub = lax.broadcasted_iota(jnp.int32, (8, 128), 0)
    zed = lane % 64

    loads = [pltpu.make_async_copy(st.at[f], raw.at[f], load_sem.at[f]) for f in range(5)]
    consts = [(bz_h, bz), (sf_h, sf), (tab_h.at[k], tab), (si_h, si), (bzi_h, bzi)]
    const_loads = [
        pltpu.make_async_copy(a, b, load_sem.at[5 + i]) for i, (a, b) in enumerate(consts)
    ]
    for c in loads + const_loads:
        c.start()

    barrier = pltpu.get_barrier_semaphore()

    def greet_y(o, _):
        pl.semaphore_signal(barrier, inc=1, device_id={"gy": (k + o) % NK}, device_id_type=MESH)
        return 0

    def greet_x(o, _):
        pl.semaphore_signal(barrier, inc=1, device_id={"gx": (g + o) % NG}, device_id_type=MESH)
        return 0

    lax.fori_loop(1, NK, greet_y, 0)
    lax.fori_loop(1, NG, greet_x, 0)

    def send(src, dst, sem, device, rsem=None):
        return pltpu.make_async_remote_copy(
            src_ref=src, dst_ref=dst, send_sem=ss.at[sem], recv_sem=rs.at[sem if rsem is None else rsem],
            device_id=device, device_id_type=MESH,
        )

    begin = before[g, k]
    end = jnp.where(k < NK - 1, before[g, jnp.minimum(k + 1, NK - 1)], 4 * NK)
    lead, trail = jnp.clip(begin - 4 * k, -1, 1), jnp.clip(end - 4 * (k + 1), -1, 1)
    last = jnp.clip(end - begin - 1, 0, 5)

    def spread(f):
        def body(x4, _):
            for i4 in range(4):
                x = x4 * 4 + i4
                v = raw[f, :, pl.ds(pl.multiple_of(x * 1024, 1024), 1024)]
                for s in range(8):
                    tmp[i4, 8 * s : 8 * s + 6, :] = v[:, 128 * s : 128 * s + 128]
                for slot in range(6):
                    dense[slot, f, x] = tmp[i4, pl.ds(slot, 8, stride=8), :]
            return 0

        lax.fori_loop(0, 8, body, 0)

        def tails(x4, _):
            for i4 in range(4):
                tail[f, x4 * 4 + i4] = dense[last, f, x4 * 4 + i4]
            return 0

        lax.fori_loop(0, 8, tails, 0)

    def assemble(f):
        def body(x, _):
            q0 = jnp.where(lead > 0, prev_tail[f, x], dense[jnp.maximum(-lead, 0), f, x])
            q1 = dense[1 - lead, f, x]
            q2 = dense[2 - lead, f, x]
            q3 = jnp.where(trail < 0, next_head[f, x], dense[3 - lead, f, x])
            for j, v in enumerate(swap4((q0, q2, q1, q3))):
                cons[f, at8(x * 32 + 8 * j), :] = v
            return 0

        lax.fori_loop(0, 32, body, 0, unroll=2)

    loads[0].wait()
    spread(0)
    pl.semaphore_wait(barrier, NK + NG - 2)
    edges = [
        send(dense.at[0, 0], next_head.at[0], EDGE, {"gy": k_dn}),
        send(tail.at[0], prev_tail.at[0], EDGE + 1, {"gy": k_up}),
    ]
    for c in edges:
        c.start()
    for f in range(1, 5):
        loads[f].wait()
        spread(f)
    for c in edges:
        c.wait_recv()
    assemble(0)
    for c in const_loads:
        c.wait()

    spec_t[...] = lax.dot_general(
        bz[...], cons[0], (((1,), (1,)), ((), ())),
        precision=HIGHEST, preferred_element_type=jnp.float32,
    )

    def a2a_copy(peer, source):
        return send(
            spec_t.at[at8(8 * peer), :], spec_r.at[source], A2A + peer, {"gy": peer}, A2A + source
        )

    def start_a2a(o, _):
        a2a_copy((k + o) % NK, k).start()
        return 0

    lax.fori_loop(1, NK, start_a2a, 0)
    spec_r[k] = spec_t[at8(8 * k), :]

    rest = [
        send(dense.at[0, pl.ds(1, 4)], next_head.at[pl.ds(1, 4)], REST, {"gy": k_dn}),
        send(tail.at[pl.ds(1, 4)], prev_tail.at[pl.ds(1, 4)], REST + 1, {"gy": k_up}),
    ]
    for c in rest:
        c.start()

    def wait_a2a(o, _):
        source = (k + NK - o) % NK
        a2a_copy(source, source).wait_recv()
        return 0

    lax.fori_loop(1, NK, wait_a2a, 0)

    def to_lines(x4, _):
        for m in range(4):
            parts = [
                spec_r[4 * m + b, :, pl.ds(pl.multiple_of(x4 * 128, 128), 128)] for b in range(4)
            ]
            for i, v in enumerate(swap4(parts)):
                lines[at8(x4 * 32 + 8 * i), 128 * m : 128 * m + 128] = v
        return 0

    lax.fori_loop(0, 8, to_lines, 0)
    trans[...] = jnp.dot(
        lines[...], sf[...], precision=HIGHEST, preferred_element_type=jnp.float32
    )

    lam, gain = tab[0], tab[1]
    lam2 = lam * lam
    lam4 = lam2 * lam2
    lam8 = lam4 * lam4
    lam16 = lam8 * lam8
    lam32 = lam16 * lam16
    lam64 = lam32 * lam32

    def sums(i, carry):
        u, v = carry
        return trans[at8(8 * i), :] + lam * u, trans[at8(8 * (31 - i)), :] + lam * v

    zero = jnp.zeros((8, 512), jnp.float32)
    up_sum, down_sum = lax.fori_loop(0, 32, sums, (zero, zero))
    upper = lax.broadcasted_iota(jnp.int32, (8, 512), 0) >= 4
    up_roll, down_roll = pltpu.roll(up_sum, 4, 0), pltpu.roll(down_sum, 4, 0)
    mom[g] = jnp.where(upper, up_sum + lam32 * up_roll, down_sum + lam32 * down_roll)

    def mom_copy(peer, source):
        return send(mom.at[source], mom.at[source], MOM + peer, {"gx": peer}, MOM + source)

    def start_mom(o, _):
        mom_copy((g + o) % NG, g).start()
        return 0

    lax.fori_loop(1, NG, start_mom, 0)

    for c in rest:
        c.wait_recv()
    for f in range(1, 5):
        assemble(f)

    def primitives(x, _):
        for j in range(4):
            rho, mx, my, mz, energy = [cons[f, at8(x * 32 + 8 * j), :] for f in range(5)]
            inverse = 1.0 / rho
            vx, vy, vz = mx * inverse, my * inverse, mz * inverse
            p = (GAMMA - 1.0) * (energy - 0.5 * rho * (vx * vx + vy * vy + vz * vz))
            for f, v in enumerate((rho, vx, vy, vz, p)):
                prim[f, at8((x + 2) * 64 + (j + 2) * 8), :] = v
        return 0

    lax.fori_loop(0, 32, primitives, 0)

    for f in range(5):
        for r in range(2):
            for j in range(4):
                row = f * 64 + r * 32 + j * 8
                xs[0, row : row + 8, :] = prim[f, (2 + r) * 64 + (j + 2) * 8 : (2 + r) * 64 + (j + 3) * 8, :]
                xs[1, row : row + 8, :] = prim[f, (32 + r) * 64 + (j + 2) * 8 : (32 + r) * 64 + (j + 3) * 8, :]
            for q in range(4):
                row = f * 64 + r * 32 + q * 8
                ys[0, row : row + 8, :] = prim[f, pl.ds((2 + 8 * q) * 64 + (2 + r) * 8, 8, stride=64), :]
                ys[1, row : row + 8, :] = prim[f, pl.ds((2 + 8 * q) * 64 + (4 + r) * 8 + 7, 8, stride=64), :]
    halo = [
        send(xs.at[0], xr.at[1], HALO, {"gx": g_dn}),
        send(xs.at[1], xr.at[0], HALO + 1, {"gx": g_up}),
        send(ys.at[0], yr.at[1], HALO + 2, {"gy": k_dn}),
        send(ys.at[1], yr.at[0], HALO + 3, {"gy": k_up}),
    ]
    for c in halo:
        c.start()

    def wait_mom(o, _):
        source = (g + NG - o) % NG
        mom_copy(source, source).wait_recv()
        return 0

    lax.fori_loop(1, NG, wait_mom, 0)
    from_low, from_high, at_start, at_end = zero, zero, zero, zero
    power_low, power_high = zero + 1.0, zero + 1.0
    for i in range(NG):
        m_up, m_dn = mom[i], mom[NG - 1 - i]
        ups = jnp.where(upper, m_up, pltpu.roll(m_up, 4, 0))
        downs = jnp.where(upper, pltpu.roll(m_dn, 4, 0), m_dn)
        from_low = jnp.where(i < g, from_low * lam64 + ups, from_low)
        from_high = jnp.where(NG - 1 - i > g, from_high * lam64 + downs, from_high)
        at_end = at_end * lam64 + ups
        at_start = at_start * lam64 + downs
        power_low = jnp.where(i < g, power_low * lam64, power_low)
        power_high = jnp.where(NG - 1 - i > g, power_high * lam64, power_high)
    lam128 = lam64 * lam64
    lam256 = lam128 * lam128
    whole = lam256 * lam256 * lam
    at_start, at_end = lam * at_start, lam * at_end
    scale = 1.0 / (1.0 - whole * whole)
    from_low = from_low - (at_start - whole * at_end) * scale * power_low
    from_high = from_high - (at_end - whole * at_start) * scale * power_high
    first_u = jnp.where(upper, up_roll + lam32 * from_low, from_low)
    first_v = jnp.where(upper, from_high, down_roll + lam32 * from_high)

    def downward(i, v):
        v = trans[at8(8 * (31 - i)), :] + lam * v
        vsol[at8(8 * (31 - i)), :] = v
        return v

    lax.fori_loop(0, 32, downward, first_v)

    def upward(i, u):
        carried = lam * u
        f = trans[at8(8 * i), :]
        trans[at8(8 * i), :] = gain * (carried + vsol[at8(8 * i), :])
        return f + carried

    lax.fori_loop(0, 32, upward, first_u)
    lines[...] = jnp.dot(
        trans[...], si[...], precision=HIGHEST, preferred_element_type=jnp.float32
    )

    def from_lines(x4, _):
        for m in range(4):
            parts = [lines[at8(x4 * 32 + 8 * i), 128 * m : 128 * m + 128] for i in range(4)]
            for b, v in enumerate(swap4(parts)):
                back_t[4 * m + b, :, pl.ds(pl.multiple_of(x4 * 128, 128), 128)] = v
        return 0

    lax.fori_loop(0, 8, from_lines, 0)

    def back_copy(peer, source):
        return send(
            back_t.at[peer], back_r.at[at8(8 * source), :], BACK + peer, {"gy": peer}, BACK + source
        )

    def start_back(o, _):
        back_copy((k + o) % NK, k).start()
        return 0

    lax.fori_loop(1, NK, start_back, 0)
    back_r[at8(8 * k), :] = back_t[k]

    def sweep_z(x, _):
        for j in range(4):
            w = [prim[f, at8((x + 2) * 64 + (j + 2) * 8), :] for f in range(5)]
            left, right = [], []
            for v in w:
                down = jnp.where(zed == 0, 0.0, v - pltpu.roll(v, 1, 1))
                up = jnp.where(zed == 63, 0.0, pltpu.roll(down, 127, 1))
                h = half_slope(down, up)
                left.append(v + h)
                lower = v - h
                right.append(jnp.where(zed == 63, lower, pltpu.roll(lower, 127, 1)))
            high = face_flux(left, right, 2)
            wall = cell_flux(w, 2)
            for f in range(5):
                low = jnp.where(zed == 0, wall[f], pltpu.roll(high[f], 1, 1))
                acc[f, at8((x + 1) * 32 + 8 * j), :] = high[f] - low
        return 0

    lax.fori_loop(0, 32, sweep_z, 0)

    for c in halo:
        c.wait_recv()

    for f in range(5):
        for r in range(2):
            for j in range(4):
                row = f * 64 + r * 32 + j * 8
                e = (j + 2) * 8

                def plane(xx):
                    return prim[f, (xx + 2) * 64 + e : (xx + 2) * 64 + e + 8, :]

                low = pltpu.roll(jnp.where(lane >= 64, xr[0, row : row + 8, :], plane(30 + r)), 64, 1)
                low = jnp.where((lane < 64) & (g == 0), plane(0), low)
                prim[f, r * 64 + e : r * 64 + e + 8, :] = low
                high = pltpu.roll(jnp.where(lane < 64, xr[1, row : row + 8, :], plane(r)), 64, 1)
                high = jnp.where((lane >= 64) & (g == NG - 1), plane(31), high)
                prim[f, (34 + r) * 64 + e : (34 + r) * 64 + e + 8, :] = high

    def place_y(x, _):
        base = (x + 2) * 64
        for f in range(5):
            rows = [prim[f, at8(base + 16 + 8 * j), :] for j in range(4)]
            first = jnp.broadcast_to(rows[0][0:1, :], (8, 128))
            final = jnp.broadcast_to(rows[3][7:8, :], (8, 128))
            for r in range(2):
                row = f * 64 + r * 32 + x
                low = jnp.where(k == 0, first, jnp.broadcast_to(yr[0, pl.ds(row, 1), :], (8, 128)))
                prim[f, at8(base + 8 * r), :] = jnp.where(sub == 0, low, pltpu.roll(rows[2 + r], 1, 0))
                high = jnp.where(k == NK - 1, final, jnp.broadcast_to(yr[1, pl.ds(row, 1), :], (8, 128)))
                prim[f, at8(base + 48 + 8 * r), :] = jnp.where(sub == 7, high, pltpu.roll(rows[r], 7, 0))
        return 0

    lax.fori_loop(0, 32, place_y, 0)

    def sweep_y(x, _):
        base = (x + 2) * 64
        previous_left, previous_flux = None, None
        for e in range(1, 7):
            left, right = [], []
            for f in range(5):
                v = prim[f, at8(base + 8 * e), :]
                down = v - prim[f, at8(base + 8 * e - 8), :]
                up = prim[f, at8(base + 8 * e + 8), :] - v
                h = half_slope(down, up)
                left.append(v + h)
                right.append(v - h)
            if previous_left is not None:
                flux = face_flux(previous_left, right, 1)
                if previous_flux is not None:
                    for f in range(5):
                        row = at8((x + 1) * 32 + 8 * (e - 3))
                        acc[f, row, :] = acc[f, row, :] + (flux[f] - previous_flux[f])
                previous_flux = flux
            previous_left = left
        return 0

    lax.fori_loop(0, 32, sweep_y, 0)

    def sweep_x(j, _):
        e = (j + 2) * 8

        def cell(f, i):
            return prim[f, at8((i + 2) * 64 + e), :]

        def body(i, carry):
            value, down, left, flux = carry
            new_value, new_down, new_left, right = [], [], [], []
            for f in range(5):
                v = cell(f, i + 1)
                up = v - value[f]
                h = half_slope(down[f], up)
                right.append(value[f] - h)
                new_left.append(value[f] + h)
                new_value.append(v)
                new_down.append(up)
            new_flux = face_flux(left, right, 0)
            for f in range(5):
                row = at8(i * 32 + 8 * j)
                acc[f, row, :] = acc[f, row, :] + (new_flux[f] - flux[f])
            return new_value, new_down, new_left, new_flux

        value, down, left, flux = [], [], [], []
        for f in range(5):
            a, b, c = cell(f, -2), cell(f, -1), cell(f, 0)
            left.append(b + half_slope(b - a, c - b))
            value.append(c)
            down.append(c - b)
            flux.append(jnp.zeros((8, 128), jnp.float32))
        lax.fori_loop(0, 33, body, (value, down, left, flux))
        return 0

    for f in range(5):
        acc[f, 0:32, :] = jnp.zeros((32, 128), jnp.float32)
    lax.fori_loop(0, 4, sweep_x, 0)

    def deficit(x, total):
        for j in range(4):
            new = cons[0, at8(x * 32 + 8 * j), :] - dt * acc[0, at8((x + 1) * 32 + 8 * j), :]
            total = total + (jnp.maximum(new, FLOOR) - new)
        return total

    defs[k] = lax.fori_loop(0, 32, deficit, jnp.zeros((8, 128), jnp.float32))

    def def_copy(peer, source):
        return send(defs.at[source], defs.at[source], DEF_Y + peer, {"gy": peer}, DEF_Y + source)

    def start_def(o, _):
        def_copy((k + o) % NK, k).start()
        return 0

    lax.fori_loop(1, NK, start_def, 0)

    def wait_back(o, _):
        source = (k + NK - o) % NK
        back_copy(source, source).wait_recv()
        return 0

    lax.fori_loop(1, NK, wait_back, 0)
    pot0[...] = lax.dot_general(
        back_r[...], bzi[...], (((0,), (0,)), ((), ())),
        precision=HIGHEST, preferred_element_type=jnp.float32,
    )
    pxs[0] = pot0[0:32, :]
    pxs[1] = pot0[31 * 32 : 32 * 32, :]
    for q in range(4):
        pys[0, 8 * q : 8 * q + 8, :] = pot0[pl.ds(8 * q * 32, 8, stride=32), :]
        pys[1, 8 * q : 8 * q + 8, :] = pot0[pl.ds(8 * q * 32 + 31, 8, stride=32), :]
    phi_halo = [
        send(pxs.at[0], pxr.at[1], PHI, {"gx": g_dn}),
        send(pxs.at[1], pxr.at[0], PHI + 1, {"gx": g_up}),
        send(pys.at[0], pyr.at[1], PHI + 2, {"gy": k_dn}),
        send(pys.at[1], pyr.at[0], PHI + 3, {"gy": k_up}),
    ]
    for c in phi_halo:
        c.start()

    def wait_def(o, _):
        source = (k + NK - o) % NK
        def_copy(source, source).wait_recv()
        return 0

    lax.fori_loop(1, NK, wait_def, 0)
    dgx[g] = jnp.sum(defs[...], axis=0)

    def dgx_copy(peer, source):
        return send(dgx.at[source], dgx.at[source], DEF_X + peer, {"gx": peer}, DEF_X + source)

    def start_dgx(o, _):
        dgx_copy((g + o) % NG, g).start()
        return 0

    lax.fori_loop(1, NG, start_dgx, 0)

    for c in phi_halo:
        c.wait_recv()
    for j in range(4):
        low = pltpu.roll(
            jnp.where(lane >= 64, pxr[0, 8 * j : 8 * j + 8, :], pot0[31 * 32 + 8 * j : 31 * 32 + 8 * j + 8, :]), 64, 1
        )
        pot[8 + 8 * j : 16 + 8 * j, :] = jnp.where((lane < 64) & (g == 0), 0.0, low)
        high = pltpu.roll(jnp.where(lane < 64, pxr[1, 8 * j : 8 * j + 8, :], pot0[8 * j : 8 * j + 8, :]), 64, 1)
        pot[33 * 48 + 8 + 8 * j : 33 * 48 + 16 + 8 * j, :] = jnp.where((lane >= 64) & (g == NG - 1), 0.0, high)

    def place_pot(x, _):
        base = (x + 1) * 48
        rows = [pot0[at8(x * 32 + 8 * j), :] for j in range(4)]
        for j in range(4):
            pot[at8(base + 8 + 8 * j), :] = rows[j]
        low = jnp.where(k == 0, 0.0, jnp.broadcast_to(pyr[0, pl.ds(x, 1), :], (8, 128)))
        pot[at8(base), :] = jnp.where(sub == 0, low, pltpu.roll(rows[3], 1, 0))
        high = jnp.where(k == NK - 1, 0.0, jnp.broadcast_to(pyr[1, pl.ds(x, 1), :], (8, 128)))
        pot[at8(base + 40), :] = jnp.where(sub == 7, high, pltpu.roll(rows[0], 7, 0))
        return 0

    lax.fori_loop(0, 32, place_pot, 0)

    def finish(x, _):
        base = (x + 1) * 48 + 8
        new = [[None] * 4 for _ in range(5)]
        for j in range(4):
            here = pot[at8(base + 8 * j), :]
            half = -0.5 * dt
            ax = half * (pot[at8(base + 48 + 8 * j), :] - pot[at8(base - 48 + 8 * j), :])
            ay = half * (pot[at8(base + 8 + 8 * j), :] - pot[at8(base - 8 + 8 * j), :])
            az = half * (
                jnp.where(zed == 63, 0.0, pltpu.roll(here, 127, 1))
                - jnp.where(zed == 0, 0.0, pltpu.roll(here, 1, 1))
            )
            u = [cons[f, at8(x * 32 + 8 * j), :] for f in range(5)]
            change = [acc[f, at8((x + 1) * 32 + 8 * j), :] for f in range(5)]
            new[0][j] = jnp.maximum(u[0] - dt * change[0], FLOOR)
            for i, a in enumerate((ax, ay, az)):
                new[1 + i][j] = u[1 + i] - dt * change[1 + i] + u[0] * a
            new[4][j] = u[4] - dt * change[4] + (u[1] * ax + u[2] * ay + u[3] * az)
        for f in range(5):
            b0, b2, b1, b3 = swap4(new[f])
            for q, v in enumerate((b0, b1, b2, b3)):
                nb[1 + q, f, x] = v
        return 0

    lax.fori_loop(0, 32, finish, 0)
    after = [
        send(nb.at[1], nb.at[5], AFTER, {"gy": k_dn}),
        send(nb.at[4], nb.at[0], AFTER + 1, {"gy": k_up}),
    ]
    for c in after:
        c.start()

    def wait_dgx(o, _):
        source = (g + NG - o) % NG
        dgx_copy(source, source).wait_recv()
        return 0

    lax.fori_loop(1, NG, wait_dgx, 0)
    added[0, 0] = jnp.sum(jnp.sum(dgx[...], axis=0)) * (1.0 / 512)

    for c in edges + rest + halo + phi_halo:
        c.wait_send()

    def sent_y(o, _):
        peer = (k + o) % NK
        a2a_copy(peer, k).wait_send()
        back_copy(peer, k).wait_send()
        def_copy(peer, k).wait_send()
        return 0

    def sent_x(o, _):
        peer = (g + o) % NG
        mom_copy(peer, g).wait_send()
        dgx_copy(peer, g).wait_send()
        return 0

    lax.fori_loop(1, NK, sent_y, 0)
    lax.fori_loop(1, NG, sent_x, 0)
    for c in after:
        c.wait()


def place_kernel(after, where, nb, out, tmp):
    g, k = where[0], where[1]
    begin = after[g, k]
    end = jnp.where(k < NK - 1, after[g, jnp.minimum(k + 1, NK - 1)], 4 * NK)
    lead, held = jnp.clip(begin - 4 * k, -1, 1), end - begin

    def body(x4, _):
        for i4 in range(4):
            x = x4 * 4 + i4
            for slot in range(6):
                index = jnp.minimum(slot + lead + 1, 5)
                v = jnp.where(slot < held, nb[index, 0, x], 0.0)
                tmp[i4, pl.ds(slot, 8, stride=8), :] = v
            for s in range(8):
                out[0, :, pl.ds(pl.multiple_of(x * 1024 + 128 * s, 128), 128)] = tmp[i4, 8 * s : 8 * s + 6, :]
        return 0

    lax.fori_loop(0, 8, body, 0)


def per_device(consts, state_before, before_start, after_start, time_step):
    f32 = jnp.float32
    st = jnp.transpose(state_before, (1, 0, 2))
    any_spec = pl.BlockSpec(memory_space=pl.ANY)
    smem = pl.BlockSpec(memory_space=pltpu.SMEM)
    vmem = pl.BlockSpec(memory_space=pltpu.VMEM)
    block = (5, 32, 8, 128)

    def scratch(*shape):
        return pltpu.VMEM(shape, f32)

    nb, added = pl.pallas_call(
        step_kernel,
        out_shape=(jax.ShapeDtypeStruct((6,) + block, f32), jax.ShapeDtypeStruct((1, 1), f32)),
        in_specs=[any_spec, smem, smem] + [any_spec] * 5,
        out_specs=(vmem, smem),
        scratch_shapes=[
            scratch(5, 6, 32768),
            scratch(4, 64, 128),
            scratch(6, *block),
            scratch(*block),
            scratch(*block),
            scratch(*block),
            scratch(5, 1024, 128),
            scratch(5, 36 * 64, 128),
            scratch(5, 33 * 32, 128),
            scratch(34 * 48, 128),
            scratch(1024, 128),
            scratch(2, 320, 128), scratch(2, 320, 128), scratch(2, 320, 128), scratch(2, 320, 128),
            scratch(2, 32, 128), scratch(2, 32, 128), scratch(2, 32, 128), scratch(2, 32, 128),
            scratch(128, 1024),
            scratch(16, 8, 1024),
            scratch(256, 512),
            scratch(256, 512),
            scratch(256, 512),
            scratch(16, 8, 1024),
            scratch(128, 1024),
            scratch(8, 8, 512),
            scratch(16, 8, 128),
            scratch(8, 8, 128),
            scratch(128, 128), scratch(128, 128), scratch(512, 512), scratch(512, 512),
            scratch(2, 8, 512),
            pltpu.SemaphoreType.DMA((10,)),
            pltpu.SemaphoreType.DMA((N_SEM,)),
            pltpu.SemaphoreType.DMA((N_SEM,)),
        ],
        compiler_params=pltpu.CompilerParams(
            collective_id=0, has_side_effects=True, vmem_limit_bytes=56 * 1024 * 1024
        ),
        name="step",
    )(st, before_start, time_step.reshape(1, 1), *consts)

    where = jnp.stack([lax.axis_index("gx"), lax.axis_index("gy")]).astype(jnp.int32)
    out = pl.pallas_call(
        place_kernel,
        out_shape=jax.ShapeDtypeStruct((5, 6, 32768), f32),
        grid=(5,),
        in_specs=[smem, smem, pl.BlockSpec((6, 1, 32, 8, 128), lambda f: (0, f, 0, 0, 0))],
        out_specs=pl.BlockSpec((1, 6, 32768), lambda f: (f, 0, 0)),
        scratch_shapes=[scratch(4, 64, 128)],
        compiler_params=pltpu.CompilerParams(vmem_limit_bytes=32 * 1024 * 1024),
        name="place",
    )(after_start, where, nb)
    return jnp.transpose(out, (1, 0, 2)), added.reshape(())


def solution(mesh):
    consts = tables()

    def run(*args):
        return per_device([jnp.asarray(c) for c in consts], *args)

    placed = (P(("gx", "gy"), None, None), P(), P(), P())
    return jax.shard_map(
        run,
        mesh=mesh,
        in_specs=placed,
        out_specs=(P(("gx", "gy"), None, None), P()),
        check_vma=False,
    )
```

```python
import jax
import jax.numpy as jnp
import numpy as np
from jax import lax
from jax.experimental import pallas as pl
from jax.experimental.pallas import tpu as pltpu
from jax.sharding import PartitionSpec as P

GAMMA = 5.0 / 3.0
FLOOR = 0.25
MESH = pl.DeviceIdType.MESH
HIGHEST = lax.Precision.HIGHEST

NK, NG, PART = 16, 8, 8
Z_FIRST = 24


def tables():
    def sine(n):
        i = np.arange(1, n + 1)
        return np.sin(np.pi * ((i[:, None] * i[None, :]) % (2 * (n + 1))) / (n + 1))

    sine_y, sine_z = sine(512), sine(64)
    forward = np.zeros((16, 2, 4, 2, 64))
    for u in range(2):
        forward[:, u, :, u, :] = sine_z.reshape(16, 4, 64)
    forward = forward.reshape(128, 128)
    backward = forward * (2.0 / 65)
    padded = np.pad(backward.reshape(128, 2, 64), ((0, 0), (0, 0), (1, 1)))
    slope = (padded[:, :, 2:] - padded[:, :, :-2]).reshape(128, 128)
    order = np.arange(512).reshape(16, 8, 4).transpose(0, 2, 1).reshape(512)
    ordered = sine_y[order]
    modes_y = 2 - 2 * np.cos(np.pi * np.arange(1, 513) / 513)
    modes_z = 2 - 2 * np.cos(np.pi * np.arange(1, 65) / 65)
    h = 0.5 * (modes_z[:, None] + modes_y[None, :])
    root = np.sqrt(h * (h + 2))
    lam = 1 / (1 + h + root)
    gain = -0.5 / root

    def rows(values):
        return np.broadcast_to(values.reshape(16, 1, 4, 512), (16, 2, 4, 512)).reshape(16, 8, 512)

    table = np.stack([rows(lam), rows(gain)], axis=1)
    cell = np.arange(128)
    down = (cell[:, None] == cell - (cell % 64 > 0)).astype(np.float32)
    up = (cell[:, None] == cell + (cell % 64 < 63)).astype(np.float32)
    f32 = np.float32
    return (
        (forward * (4.0 / 64)).astype(f32),
        np.concatenate([backward, slope], axis=1).astype(f32),
        ordered.astype(f32),
        np.ascontiguousarray(ordered.T * (2.0 / 513)).astype(f32),
        table.astype(f32),
        np.tile(np.concatenate([down, up], axis=1), (2, 1)),
    )


def lanes():
    return lax.broadcasted_iota(jnp.int32, (8, 128), 1)


def swap4(parts):
    group = lanes() // 32
    low, even = group < 2, group % 2 == 0

    def pick(order):
        return jnp.where(low, jnp.where(even, order[0], order[1]), jnp.where(even, order[2], order[3]))

    turned = []
    for r in range(4):
        mixed = pick([parts[(i + r) % 4] for i in range(4)])
        turned.append(pltpu.roll(mixed, 32 * r, 1) if r else mixed)
    return [pick([turned[(b - j) % 4] for b in range(4)]) for j in range(4)]


def half_slope(down, up):
    quarter = 0.25 * (down + up)
    low = jnp.minimum(jnp.maximum(down, up), 0.0)
    high = jnp.maximum(jnp.minimum(down, up), 0.0)
    return jnp.minimum(jnp.maximum(quarter, low), high)


def face_flux(left, right, normal):
    def side(w):
        rho, vx, vy, vz, p = w
        gp = GAMMA * p
        return gp * lax.rsqrt(gp * rho), 0.5 * (vx * vx + vy * vy + vz * vz)

    sound_l, half_l = side(left)
    sound_r, half_r = side(right)
    ul, ur = left[1 + normal], right[1 + normal]
    fast = jnp.maximum(jnp.maximum(ul + sound_l, ur + sound_r), 0.0)
    slow = jnp.minimum(jnp.minimum(ul - sound_l, ur - sound_r), 0.0)
    inverse = 1.0 / (fast - slow)
    a, b = fast * inverse, slow * inverse
    d = fast * b
    kl, kr = a * ul - d, d - b * ur
    gl, gr = left[0] * kl, right[0] * kr
    apl, bpr = a * left[4], b * right[4]
    out = [gl + gr]
    for i in range(3):
        term = gl * left[1 + i] + gr * right[1 + i]
        out.append(term + (apl - bpr) if i == normal else term)
    out.append(
        1.5 * (left[4] * kl + right[4] * kr) + (gl * half_l + gr * half_r) + (apl * ul - bpr * ur)
    )
    return out


def cell_flux(w, normal):
    rho, p, u = w[0], w[4], w[1 + normal]
    mass = rho * u
    out = [mass]
    for i in range(3):
        out.append(mass * w[1 + i] + p if i == normal else mass * w[1 + i])
    half = 0.5 * (w[1] * w[1] + w[2] * w[2] + w[3] * w[3])
    out.append(2.5 * p * u + mass * half)
    return out


def at8(row):
    return pl.ds(pl.multiple_of(row, 8), 8)


EDGE, REST, HALO, PHI, AFTER, A2A, BACK, MOM, DEF_Y, DEF_X, N_SEM = (
    0, 2, 8, 12, 16, 24, 40, 56, 64, 80, 88,
)


def step_kernel(
    st, before, dt_ref, bz_h, bzi_h, sf_h, si_h, tab_h, move_h,
    nb, added,
    raw, tmp, dense, tail, next_head, prev_tail, cons, prim, acc, below, above, pot, pot0, potz,
    xs, xr, ys, yr, pxs, pxr, pys, pyr,
    spec_t, spec_r, lines, trans, vsol, back_t, back_r, mom, defs, dgx,
    bz, bzi, sf, si, tab, move, load_sem, ss, rs,
):
    g, k = lax.axis_index("gx"), lax.axis_index("gy")
    k_up, k_dn = (k + 1) % NK, (k + NK - 1) % NK
    g_up, g_dn = (g + 1) % NG, (g + NG - 1) % NG
    dt = dt_ref[0, 0]
    lane = lanes()
    sub = lax.broadcasted_iota(jnp.int32, (8, 128), 0)
    zed = lane % 64

    loads = [pltpu.make_async_copy(st.at[f], raw.at[f], load_sem.at[f]) for f in range(5)]
    consts = [(bz_h, bz), (sf_h, sf), (tab_h.at[k], tab), (si_h, si), (bzi_h, bzi), (move_h, move)]
    const_loads = [
        pltpu.make_async_copy(a, b, load_sem.at[5 + i]) for i, (a, b) in enumerate(consts)
    ]
    for c in loads + const_loads:
        c.start()

    barrier = pltpu.get_barrier_semaphore()

    def greet_y(o, _):
        pl.semaphore_signal(barrier, inc=1, device_id={"gy": (k + o) % NK}, device_id_type=MESH)
        return 0

    def greet_x(o, _):
        pl.semaphore_signal(barrier, inc=1, device_id={"gx": (g + o) % NG}, device_id_type=MESH)
        return 0

    lax.fori_loop(1, NK, greet_y, 0)
    lax.fori_loop(1, NG, greet_x, 0)

    def send(src, dst, sem, device, rsem=None):
        return pltpu.make_async_remote_copy(
            src_ref=src, dst_ref=dst, send_sem=ss.at[sem], recv_sem=rs.at[sem if rsem is None else rsem],
            device_id=device, device_id_type=MESH,
        )

    begin = before[g, k]
    end = jnp.where(k < NK - 1, before[g, jnp.minimum(k + 1, NK - 1)], 4 * NK)
    lead, trail = jnp.clip(begin - 4 * k, -1, 1), jnp.clip(end - 4 * (k + 1), -1, 1)
    last = jnp.clip(end - begin - 1, 0, 5)

    def spread(f):
        def body(x4, _):
            for i4 in range(4):
                x = x4 * 4 + i4
                v = raw[f, :, pl.ds(pl.multiple_of(x * 1024, 1024), 1024)]
                for s in range(8):
                    tmp[i4, 8 * s : 8 * s + 6, :] = v[:, 128 * s : 128 * s + 128]
                for slot in range(6):
                    dense[slot, f, x] = tmp[i4, pl.ds(slot, 8, stride=8), :]
            return 0

        lax.fori_loop(0, 8, body, 0)

        def tails(x4, _):
            for i4 in range(4):
                tail[f, x4 * 4 + i4] = dense[last, f, x4 * 4 + i4]
            return 0

        lax.fori_loop(0, 8, tails, 0)

    def assemble(f):
        def body(x4, _):
            for i4 in range(4):
                x = x4 * 4 + i4
                q0 = jnp.where(lead > 0, prev_tail[f, x], dense[jnp.maximum(-lead, 0), f, x])
                q1 = dense[1 - lead, f, x]
                q2 = dense[2 - lead, f, x]
                q3 = jnp.where(trail < 0, next_head[f, x], dense[3 - lead, f, x])
                for j, v in enumerate(swap4((q0, q2, q1, q3))):
                    cons[f, at8(x * 32 + 8 * j), :] = v
            return 0

        lax.fori_loop(0, 8, body, 0)

    for f in range(5):
        loads[f].wait()
        spread(f)
    pl.semaphore_wait(barrier, NK + NG - 2)
    edges = [
        send(dense.at[0, 0], next_head.at[0], EDGE, {"gy": k_dn}),
        send(tail.at[0], prev_tail.at[0], EDGE + 1, {"gy": k_up}),
    ]
    rest = [
        [
            send(dense.at[0, span], next_head.at[span], REST + 2 * i, {"gy": k_dn}),
            send(tail.at[span], prev_tail.at[span], REST + 2 * i + 1, {"gy": k_up}),
        ]
        for i, span in enumerate((pl.ds(1, 1), pl.ds(2, 1), pl.ds(3, 2)))
    ]
    for c in edges + rest[0]:
        c.start()
    for c in edges:
        c.wait_recv()
    assemble(0)
    for c in const_loads:
        c.wait()

    spec_t[...] = lax.dot_general(
        bz[...], cons[0], (((1,), (1,)), ((), ())),
        precision=HIGHEST, preferred_element_type=jnp.float32,
    )

    def a2a_copy(peer, source):
        return send(
            spec_t.at[at8(8 * peer), :], spec_r.at[source], A2A + peer, {"gy": peer}, A2A + source
        )

    def start_a2a(o, _):
        a2a_copy((k + o) % NK, k).start()
        return 0

    lax.fori_loop(1, NK, start_a2a, 0)
    for c in rest[1]:
        c.start()
    spec_r[k] = spec_t[at8(8 * k), :]
    for c in rest[0]:
        c.wait_recv()
    assemble(1)

    def wait_a2a(o, _):
        source = (k + NK - o) % NK
        a2a_copy(source, source).wait_recv()
        return 0

    lax.fori_loop(1, NK, wait_a2a, 0)

    def to_lines(x4, _):
        for m in range(4):
            parts = [
                spec_r[4 * m + b, :, pl.ds(pl.multiple_of(x4 * 128, 128), 128)] for b in range(4)
            ]
            for i, v in enumerate(swap4(parts)):
                lines[at8(x4 * 32 + 8 * i), 128 * m : 128 * m + 128] = v
        return 0

    lax.fori_loop(0, 8, to_lines, 0)
    trans[...] = jnp.dot(
        lines[...], sf[...], precision=HIGHEST, preferred_element_type=jnp.float32
    )

    lam, gain = tab[0], tab[1]
    lam2 = lam * lam
    lam4 = lam2 * lam2
    lam8 = lam4 * lam4
    lam16 = lam8 * lam8
    lam32 = lam16 * lam16
    lam64 = lam32 * lam32

    def sums(i, carry):
        u, v = carry
        return trans[at8(8 * i), :] + lam * u, trans[at8(8 * (31 - i)), :] + lam * v

    zero = jnp.zeros((8, 512), jnp.float32)
    up_sum, down_sum = lax.fori_loop(0, 32, sums, (zero, zero))
    upper = lax.broadcasted_iota(jnp.int32, (8, 512), 0) >= 4
    up_roll, down_roll = pltpu.roll(up_sum, 4, 0), pltpu.roll(down_sum, 4, 0)
    mom[g] = jnp.where(upper, up_sum + lam32 * up_roll, down_sum + lam32 * down_roll)

    def mom_copy(peer, source):
        return send(mom.at[source], mom.at[source], MOM + peer, {"gx": peer}, MOM + source)

    def start_mom(o, _):
        mom_copy((g + o) % NG, g).start()
        return 0

    lax.fori_loop(1, NG, start_mom, 0)
    for c in rest[2]:
        c.start()

    def wait_mom(o, _):
        source = (g + NG - o) % NG
        mom_copy(source, source).wait_recv()
        return 0

    lax.fori_loop(1, NG, wait_mom, 0)
    from_low, from_high, at_start, at_end = zero, zero, zero, zero
    power_low, power_high = zero + 1.0, zero + 1.0
    for i in range(NG):
        m_up, m_dn = mom[i], mom[NG - 1 - i]
        ups = jnp.where(upper, m_up, pltpu.roll(m_up, 4, 0))
        downs = jnp.where(upper, pltpu.roll(m_dn, 4, 0), m_dn)
        from_low = jnp.where(i < g, from_low * lam64 + ups, from_low)
        from_high = jnp.where(NG - 1 - i > g, from_high * lam64 + downs, from_high)
        at_end = at_end * lam64 + ups
        at_start = at_start * lam64 + downs
        power_low = jnp.where(i < g, power_low * lam64, power_low)
        power_high = jnp.where(NG - 1 - i > g, power_high * lam64, power_high)
    lam128 = lam64 * lam64
    lam256 = lam128 * lam128
    whole = lam256 * lam256 * lam
    at_start, at_end = lam * at_start, lam * at_end
    scale = 1.0 / (1.0 - whole * whole)
    from_low = from_low - (at_start - whole * at_end) * scale * power_low
    from_high = from_high - (at_end - whole * at_start) * scale * power_high
    first_u = jnp.where(upper, up_roll + lam32 * from_low, from_low)
    first_v = jnp.where(upper, from_high, down_roll + lam32 * from_high)

    def downward(i, v):
        v = trans[at8(8 * (31 - i)), :] + lam * v
        vsol[at8(8 * (31 - i)), :] = v
        return v

    lax.fori_loop(0, 32, downward, first_v)

    def upward(i, u):
        carried = lam * u
        f = trans[at8(8 * i), :]
        trans[at8(8 * i), :] = gain * (carried + vsol[at8(8 * i), :])
        return f + carried

    lax.fori_loop(0, 32, upward, first_u)
    lines[...] = jnp.dot(
        trans[...], si[...], precision=HIGHEST, preferred_element_type=jnp.float32
    )

    def from_lines(x4, _):
        for m in range(4):
            parts = [lines[at8(x4 * 32 + 8 * i), 128 * m : 128 * m + 128] for i in range(4)]
            for b, v in enumerate(swap4(parts)):
                back_t[4 * m + b, :, pl.ds(pl.multiple_of(x4 * 128, 128), 128)] = v
        return 0

    lax.fori_loop(0, 8, from_lines, 0)

    def back_copy(peer, source):
        return send(
            back_t.at[peer], back_r.at[at8(8 * source), :], BACK + peer, {"gy": peer}, BACK + source
        )

    def start_back(o, _):
        back_copy((k + o) % NK, k).start()
        return 0

    lax.fori_loop(1, NK, start_back, 0)
    back_r[at8(8 * k), :] = back_t[k]

    for c in rest[1] + rest[2]:
        c.wait_recv()
    for f in range(2, 5):
        assemble(f)

    def primitives(x, _):
        for j in range(4):
            rho, mx, my, mz, energy = [cons[f, at8(x * 32 + 8 * j), :] for f in range(5)]
            inverse = 1.0 / rho
            vx, vy, vz = mx * inverse, my * inverse, mz * inverse
            p = (GAMMA - 1.0) * (energy - 0.5 * rho * (vx * vx + vy * vy + vz * vz))
            for f, v in enumerate((rho, vx, vy, vz, p)):
                prim[f, at8((x + 2) * 64 + (j + 2) * 8), :] = v
        return 0

    lax.fori_loop(0, 32, primitives, 0)

    for f in range(5):
        for r in range(2):
            for j in range(4):
                row = f * 64 + r * 32 + j * 8
                xs[0, row : row + 8, :] = prim[f, (2 + r) * 64 + (j + 2) * 8 : (2 + r) * 64 + (j + 3) * 8, :]
                xs[1, row : row + 8, :] = prim[f, (32 + r) * 64 + (j + 2) * 8 : (32 + r) * 64 + (j + 3) * 8, :]
            for q in range(4):
                row = f * 64 + r * 32 + q * 8
                ys[0, row : row + 8, :] = prim[f, pl.ds((2 + 8 * q) * 64 + (2 + r) * 8, 8, stride=64), :]
                ys[1, row : row + 8, :] = prim[f, pl.ds((2 + 8 * q) * 64 + (4 + r) * 8 + 7, 8, stride=64), :]
    halo = [
        send(xs.at[0], xr.at[1], HALO, {"gx": g_dn}),
        send(xs.at[1], xr.at[0], HALO + 1, {"gx": g_up}),
        send(ys.at[0], yr.at[1], HALO + 2, {"gy": k_dn}),
        send(ys.at[1], yr.at[0], HALO + 3, {"gy": k_up}),
    ]
    for c in halo:
        c.start()

    def neighbours_z(x8, _):
        for f in range(5):
            v = jnp.concatenate(
                [prim[f, pl.ds(pl.multiple_of((x8 * 8 + i + 2) * 64 + 16, 16), 32), :] for i in range(8)]
            )
            upper_half = v.astype(jnp.bfloat16)
            lower_half = (v - upper_half.astype(jnp.float32)).astype(jnp.bfloat16)
            both = jnp.dot(
                jnp.concatenate([upper_half, lower_half], axis=1), move[...],
                preferred_element_type=jnp.float32,
            )
            rows = pl.ds(pl.multiple_of(x8 * 256, 256), 256)
            below[f, rows, :] = both[:, 0:128]
            above[f, rows, :] = both[:, 128:256]
        return 0

    lax.fori_loop(0, 4, neighbours_z, 0)

    def sweep_z(x, _):
        for j in range(4):
            row = at8(x * 32 + 8 * j)
            w = [prim[f, at8((x + 2) * 64 + (j + 2) * 8), :] for f in range(5)]
            left, right = [], []
            for f, v in enumerate(w):
                h = half_slope(v - below[f, row, :], above[f, row, :] - v)
                left.append(v + h)
                lower = v - h
                right.append(jnp.where(zed == 63, lower, pltpu.roll(lower, 127, 1)))
            high = face_flux(left, right, 2)
            wall = cell_flux(w, 2)
            for f in range(5):
                low = jnp.where(zed == 0, wall[f], pltpu.roll(high[f], 1, 1))
                acc[f, row, :] = high[f] - low
        return 0

    lax.fori_loop(0, Z_FIRST, sweep_z, 0)

    def wait_back(o, _):
        source = (k + NK - o) % NK
        back_copy(source, source).wait_recv()
        return 0

    lax.fori_loop(1, NK, wait_back, 0)
    both = lax.dot_general(
        back_r[...], bzi[...], (((0,), (0,)), ((), ())),
        precision=HIGHEST, preferred_element_type=jnp.float32,
    )
    pot0[...] = both[:, 0:128]
    potz[...] = both[:, 128:256]
    pxs[0] = pot0[0:32, :]
    pxs[1] = pot0[31 * 32 : 32 * 32, :]
    for q in range(4):
        pys[0, 8 * q : 8 * q + 8, :] = pot0[pl.ds(8 * q * 32, 8, stride=32), :]
        pys[1, 8 * q : 8 * q + 8, :] = pot0[pl.ds(8 * q * 32 + 31, 8, stride=32), :]
    phi_halo = [
        send(pxs.at[0], pxr.at[1], PHI, {"gx": g_dn}),
        send(pxs.at[1], pxr.at[0], PHI + 1, {"gx": g_up}),
        send(pys.at[0], pyr.at[1], PHI + 2, {"gy": k_dn}),
        send(pys.at[1], pyr.at[0], PHI + 3, {"gy": k_up}),
    ]
    for c in phi_halo:
        c.start()

    lax.fori_loop(Z_FIRST, 32, sweep_z, 0)

    for c in halo:
        c.wait_recv()

    for f in range(5):
        for r in range(2):
            for j in range(4):
                row = f * 64 + r * 32 + j * 8
                e = (j + 2) * 8

                def plane(xx):
                    return prim[f, (xx + 2) * 64 + e : (xx + 2) * 64 + e + 8, :]

                low = pltpu.roll(jnp.where(lane >= 64, xr[0, row : row + 8, :], plane(30 + r)), 64, 1)
                low = jnp.where((lane < 64) & (g == 0), plane(0), low)
                prim[f, r * 64 + e : r * 64 + e + 8, :] = low
                high = pltpu.roll(jnp.where(lane < 64, xr[1, row : row + 8, :], plane(r)), 64, 1)
                high = jnp.where((lane >= 64) & (g == NG - 1), plane(31), high)
                prim[f, (34 + r) * 64 + e : (34 + r) * 64 + e + 8, :] = high

    def place_y(x, _):
        base = (x + 2) * 64
        for f in range(5):
            rows = [prim[f, at8(base + 16 + 8 * j), :] for j in range(4)]
            first = jnp.broadcast_to(rows[0][0:1, :], (8, 128))
            final = jnp.broadcast_to(rows[3][7:8, :], (8, 128))
            for r in range(2):
                row = f * 64 + r * 32 + x
                low = jnp.where(k == 0, first, jnp.broadcast_to(yr[0, pl.ds(row, 1), :], (8, 128)))
                prim[f, at8(base + 8 * r), :] = jnp.where(sub == 0, low, pltpu.roll(rows[2 + r], 1, 0))
                high = jnp.where(k == NK - 1, final, jnp.broadcast_to(yr[1, pl.ds(row, 1), :], (8, 128)))
                prim[f, at8(base + 48 + 8 * r), :] = jnp.where(sub == 7, high, pltpu.roll(rows[r], 7, 0))
        return 0

    lax.fori_loop(0, 32, place_y, 0)

    def sweep_row(cell, count, normal, target):
        before_left, before_flux = None, None
        for i in range(-1, count + 1):
            left, right = [], []
            for f in range(5):
                v = cell(f, i)
                h = half_slope(v - cell(f, i - 1), cell(f, i + 1) - v)
                left.append(v + h)
                right.append(v - h)
            if before_left is not None:
                flux = face_flux(before_left, right, normal)
                if before_flux is not None:
                    for f in range(5):
                        row = target(i - 1)
                        acc[f, row, :] = acc[f, row, :] + (flux[f] - before_flux[f])
                before_flux = flux
            before_left = left

    def hydro(part):
        def sweep_y(i, _):
            x = part * PART + i
            base = (x + 2) * 64 + 16
            sweep_row(
                lambda f, e: prim[f, at8(base + 8 * e), :], 4, 1, lambda e: at8(x * 32 + 8 * e)
            )
            return 0

        lax.fori_loop(0, PART, sweep_y, 0)

        def sweep_x(j, _):
            base = (part * PART + 2) * 64 + 16 + 8 * j
            sweep_row(
                lambda f, i: prim[f, at8(base + 64 * i), :], PART, 0,
                lambda i: at8((part * PART + i) * 32 + 8 * j),
            )
            return 0

        lax.fori_loop(0, 4, sweep_x, 0)

    def finish(part):
        def body(i, _):
            x = part * PART + i
            base = (x + 1) * 48 + 8
            new = [[None] * 4 for _ in range(5)]
            half = -0.5 * dt
            for j in range(4):
                ax = half * (pot[at8(base + 48 + 8 * j), :] - pot[at8(base - 48 + 8 * j), :])
                ay = half * (pot[at8(base + 8 + 8 * j), :] - pot[at8(base - 8 + 8 * j), :])
                az = half * potz[at8(x * 32 + 8 * j), :]
                u = [cons[f, at8(x * 32 + 8 * j), :] for f in range(5)]
                change = [acc[f, at8(x * 32 + 8 * j), :] for f in range(5)]
                new[0][j] = jnp.maximum(u[0] - dt * change[0], FLOOR)
                for i3, a in enumerate((ax, ay, az)):
                    new[1 + i3][j] = u[1 + i3] - dt * change[1 + i3] + u[0] * a
                new[4][j] = u[4] - dt * change[4] + (u[1] * ax + u[2] * ay + u[3] * az)
            for f in range(5):
                b0, b2, b1, b3 = swap4(new[f])
                for q, v in enumerate((b0, b1, b2, b3)):
                    nb[1 + q, f, x] = v
            return 0

        lax.fori_loop(0, PART, body, 0)

    def after_copies(part):
        span = pl.ds(part * PART, PART)
        return [
            send(nb.at[1, :, span], nb.at[5, :, span], AFTER + part, {"gy": k_dn}),
            send(nb.at[4, :, span], nb.at[0, :, span], AFTER + 4 + part, {"gy": k_up}),
        ]

    def emit(part):
        for c in after_copies(part):
            c.start()

    def hydro_part(part, _):
        hydro(part)
        return 0

    lax.fori_loop(0, 32 // PART, hydro_part, 0)

    def deficit(x, total):
        for j in range(4):
            row = at8(x * 32 + 8 * j)
            density = cons[0, row, :] - dt * acc[0, row, :]
            total = total + (jnp.maximum(density, FLOOR) - density)
        return total

    defs[k] = lax.fori_loop(0, 32, deficit, jnp.zeros((8, 128), jnp.float32))

    def def_copy(peer, source):
        return send(defs.at[source], defs.at[source], DEF_Y + peer, {"gy": peer}, DEF_Y + source)

    def start_def(o, _):
        def_copy((k + o) % NK, k).start()
        return 0

    def wait_def(o, _):
        source = (k + NK - o) % NK
        def_copy(source, source).wait_recv()
        return 0

    lax.fori_loop(1, NK, start_def, 0)

    for c in phi_halo:
        c.wait_recv()
    for j in range(4):
        low = pltpu.roll(
            jnp.where(lane >= 64, pxr[0, 8 * j : 8 * j + 8, :], pot0[31 * 32 + 8 * j : 31 * 32 + 8 * j + 8, :]), 64, 1
        )
        pot[8 + 8 * j : 16 + 8 * j, :] = jnp.where((lane < 64) & (g == 0), 0.0, low)
        high = pltpu.roll(jnp.where(lane < 64, pxr[1, 8 * j : 8 * j + 8, :], pot0[8 * j : 8 * j + 8, :]), 64, 1)
        pot[33 * 48 + 8 + 8 * j : 33 * 48 + 16 + 8 * j, :] = jnp.where((lane >= 64) & (g == NG - 1), 0.0, high)

    def place_pot(x, _):
        base = (x + 1) * 48
        rows = [pot0[at8(x * 32 + 8 * j), :] for j in range(4)]
        for j in range(4):
            pot[at8(base + 8 + 8 * j), :] = rows[j]
        low = jnp.where(k == 0, 0.0, jnp.broadcast_to(pyr[0, pl.ds(x, 1), :], (8, 128)))
        pot[at8(base), :] = jnp.where(sub == 0, low, pltpu.roll(rows[3], 1, 0))
        high = jnp.where(k == NK - 1, 0.0, jnp.broadcast_to(pyr[1, pl.ds(x, 1), :], (8, 128)))
        pot[at8(base + 40), :] = jnp.where(sub == 7, high, pltpu.roll(rows[0], 7, 0))
        return 0

    lax.fori_loop(0, 32, place_pot, 0)
    def one_part(part, _):
        finish(part)
        emit(part)
        return 0

    lax.fori_loop(0, 2, one_part, 0)
    lax.fori_loop(1, NK, wait_def, 0)
    dgx[g] = jnp.sum(defs[...], axis=0)

    def dgx_copy(peer, source):
        return send(dgx.at[source], dgx.at[source], DEF_X + peer, {"gx": peer}, DEF_X + source)

    def start_dgx(o, _):
        dgx_copy((g + o) % NG, g).start()
        return 0

    def wait_dgx(o, _):
        source = (g + NG - o) % NG
        dgx_copy(source, source).wait_recv()
        return 0

    lax.fori_loop(1, NG, start_dgx, 0)
    lax.fori_loop(2, 4, one_part, 0)
    lax.fori_loop(1, NG, wait_dgx, 0)
    added[0, 0] = jnp.sum(jnp.sum(dgx[...], axis=0)) * (1.0 / 512)

    for c in edges + rest[0] + rest[1] + rest[2] + halo + phi_halo:
        c.wait_send()

    def sent_y(o, _):
        peer = (k + o) % NK
        a2a_copy(peer, k).wait_send()
        back_copy(peer, k).wait_send()
        def_copy(peer, k).wait_send()
        return 0

    def sent_x(o, _):
        peer = (g + o) % NG
        mom_copy(peer, g).wait_send()
        dgx_copy(peer, g).wait_send()
        return 0

    lax.fori_loop(1, NK, sent_y, 0)
    lax.fori_loop(1, NG, sent_x, 0)
    for part in range(32 // PART):
        for c in after_copies(part):
            c.wait()


def place_kernel(after, where, nb, out, tmp, ready, sem):
    g, k = where[0], where[1]
    begin = after[g, k]
    end = jnp.where(k < NK - 1, after[g, jnp.minimum(k + 1, NK - 1)], 4 * NK)
    lead, held = jnp.clip(begin - 4 * k, -1, 1), end - begin
    writes = [pltpu.make_async_copy(ready.at[f], out.at[f], sem.at[f]) for f in range(5)]
    for f in range(5):

        def body(x4, _):
            for i4 in range(4):
                x = x4 * 4 + i4
                for slot in range(6):
                    index = jnp.minimum(slot + lead + 1, 5)
                    v = jnp.where(slot < held, nb[index, f, x], 0.0)
                    tmp[i4, pl.ds(slot, 8, stride=8), :] = v
                for s in range(8):
                    ready[f, :, pl.ds(pl.multiple_of(x * 1024 + 128 * s, 128), 128)] = tmp[i4, 8 * s : 8 * s + 6, :]
            return 0

        lax.fori_loop(0, 8, body, 0)
        writes[f].start()
    for c in writes:
        c.wait()


def per_device(consts, state_before, before_start, after_start, time_step):
    f32 = jnp.float32
    st = jnp.transpose(state_before, (1, 0, 2))
    any_spec = pl.BlockSpec(memory_space=pl.ANY)
    smem = pl.BlockSpec(memory_space=pltpu.SMEM)
    vmem = pl.BlockSpec(memory_space=pltpu.VMEM)
    block = (5, 32, 8, 128)

    def scratch(*shape):
        return pltpu.VMEM(shape, f32)

    nb, added = pl.pallas_call(
        step_kernel,
        out_shape=(pltpu.VMEM((6,) + block, f32), jax.ShapeDtypeStruct((1, 1), f32)),
        in_specs=[any_spec, smem, smem] + [any_spec] * 6,
        out_specs=(vmem, smem),
        scratch_shapes=[
            scratch(5, 6, 32768),
            scratch(4, 64, 128),
            scratch(6, *block),
            scratch(*block),
            scratch(*block),
            scratch(*block),
            scratch(5, 1024, 128),
            scratch(5, 36 * 64, 128),
            scratch(5, 1024, 128),
            scratch(5, 1024, 128), scratch(5, 1024, 128),
            scratch(34 * 48, 128),
            scratch(1024, 128),
            scratch(1024, 128),
            scratch(2, 320, 128), scratch(2, 320, 128), scratch(2, 320, 128), scratch(2, 320, 128),
            scratch(2, 32, 128), scratch(2, 32, 128), scratch(2, 32, 128), scratch(2, 32, 128),
            scratch(128, 1024),
            scratch(16, 8, 1024),
            scratch(256, 512),
            scratch(256, 512),
            scratch(256, 512),
            scratch(16, 8, 1024),
            scratch(128, 1024),
            scratch(8, 8, 512),
            scratch(16, 8, 128),
            scratch(8, 8, 128),
            scratch(128, 128), scratch(128, 256), scratch(512, 512), scratch(512, 512),
            scratch(2, 8, 512),
            pltpu.VMEM((256, 256), jnp.bfloat16),
            pltpu.SemaphoreType.DMA((11,)),
            pltpu.SemaphoreType.DMA((N_SEM,)),
            pltpu.SemaphoreType.DMA((N_SEM,)),
        ],
        compiler_params=pltpu.CompilerParams(
            collective_id=0, has_side_effects=True, vmem_limit_bytes=58 * 1024 * 1024
        ),
        name="step",
    )(st, before_start, time_step.reshape(1, 1), *consts)

    where = jnp.stack([lax.axis_index("gx"), lax.axis_index("gy")]).astype(jnp.int32)
    out = pl.pallas_call(
        place_kernel,
        out_shape=jax.ShapeDtypeStruct((5, 6, 32768), f32),
        in_specs=[smem, smem, vmem],
        out_specs=any_spec,
        scratch_shapes=[
            scratch(4, 64, 128), scratch(5, 6, 32768), pltpu.SemaphoreType.DMA((5,)),
        ],
        compiler_params=pltpu.CompilerParams(vmem_limit_bytes=32 * 1024 * 1024),
        name="place",
    )(after_start, where, nb)
    return jnp.transpose(out, (1, 0, 2)), added.reshape(())


def solution(mesh):
    consts = tables()

    def run(*args):
        return per_device([jnp.asarray(c) for c in consts[:-1]] + [jnp.asarray(consts[-1], jnp.bfloat16)], *args)

    placed = (P(("gx", "gy"), None, None), P(), P(), P())
    return jax.shard_map(
        run,
        mesh=mesh,
        in_specs=placed,
        out_specs=(P(("gx", "gy"), None, None), P()),
        check_vma=False,
    )
```

```python
import jax
import jax.numpy as jnp
import numpy as np
from jax import lax
from jax.experimental import pallas as pl
from jax.experimental.pallas import tpu as pltpu
from jax.sharding import PartitionSpec as P

GAMMA = 5.0 / 3.0
FLOOR = 0.25
MESH = pl.DeviceIdType.MESH
HIGHEST = lax.Precision.HIGHEST

NK, NG, PART = 16, 8, 8


def tables():
    def sine(n):
        i = np.arange(1, n + 1)
        return np.sin(np.pi * ((i[:, None] * i[None, :]) % (2 * (n + 1))) / (n + 1))

    sine_x, sine_z = sine(512), sine(64)
    forward = np.zeros((8, 2, 8, 2, 64))
    for u in range(2):
        forward[:, u, :, u, :] = sine_z.reshape(8, 8, 64)
    forward = forward.reshape(128, 128)
    backward = forward * (2.0 / 65)
    padded = np.pad(backward.reshape(128, 2, 64), ((0, 0), (0, 0), (1, 1)))
    slope = (padded[:, :, 2:] - padded[:, :, :-2]).reshape(128, 128)
    order = np.arange(512).reshape(8, 2, 8, 4).transpose(0, 1, 3, 2).reshape(512)
    ordered = sine_x[order]
    modes_x = 2 - 2 * np.cos(np.pi * np.arange(1, 513) / 513)
    modes_z = 2 - 2 * np.cos(np.pi * np.arange(1, 65) / 65)
    h = 0.5 * (modes_z[:, None] + modes_x[None, :])
    root = np.sqrt(h * (h + 2))
    lam = 1 / (1 + h + root)
    gain = -0.5 / root

    table = np.stack([lam.reshape(8, 8, 512), gain.reshape(8, 8, 512)], axis=1)
    cell = np.arange(128)
    down = (cell[:, None] == cell - (cell % 64 > 0)).astype(np.float32)
    up = (cell[:, None] == cell + (cell % 64 < 63)).astype(np.float32)
    f32 = np.float32
    return (
        (forward * (4.0 / 64)).astype(f32),
        np.concatenate([backward, slope], axis=1).astype(f32),
        ordered.astype(f32),
        (ordered * (2.0 / 513)).astype(f32),
        table.astype(f32),
        np.tile(np.concatenate([down, up], axis=1), (2, 1)),
    )


def lanes():
    return lax.broadcasted_iota(jnp.int32, (8, 128), 1)


def swap4(parts):
    group = lanes() // 32
    low, even = group < 2, group % 2 == 0

    def pick(order):
        return jnp.where(low, jnp.where(even, order[0], order[1]), jnp.where(even, order[2], order[3]))

    turned = []
    for r in range(4):
        mixed = pick([parts[(i + r) % 4] for i in range(4)])
        turned.append(pltpu.roll(mixed, 32 * r, 1) if r else mixed)
    return [pick([turned[(b - j) % 4] for b in range(4)]) for j in range(4)]


def half_slope(down, up):
    quarter = 0.25 * (down + up)
    low = jnp.minimum(jnp.maximum(down, up), 0.0)
    high = jnp.maximum(jnp.minimum(down, up), 0.0)
    return jnp.minimum(jnp.maximum(quarter, low), high)


def face_flux(left, right, normal):
    def side(w):
        rho, vx, vy, vz, p = w
        gp = GAMMA * p
        return gp * lax.rsqrt(gp * rho), 0.5 * (vx * vx + vy * vy + vz * vz)

    sound_l, half_l = side(left)
    sound_r, half_r = side(right)
    ul, ur = left[1 + normal], right[1 + normal]
    fast = jnp.maximum(jnp.maximum(ul + sound_l, ur + sound_r), 0.0)
    slow = jnp.minimum(jnp.minimum(ul - sound_l, ur - sound_r), 0.0)
    inverse = 1.0 / (fast - slow)
    a, b = fast * inverse, slow * inverse
    d = fast * b
    kl, kr = a * ul - d, d - b * ur
    gl, gr = left[0] * kl, right[0] * kr
    apl, bpr = a * left[4], b * right[4]
    out = [gl + gr]
    for i in range(3):
        term = gl * left[1 + i] + gr * right[1 + i]
        out.append(term + (apl - bpr) if i == normal else term)
    out.append(
        1.5 * (left[4] * kl + right[4] * kr) + (gl * half_l + gr * half_r) + (apl * ul - bpr * ur)
    )
    return out


def cell_flux(w, normal):
    rho, p, u = w[0], w[4], w[1 + normal]
    mass = rho * u
    out = [mass]
    for i in range(3):
        out.append(mass * w[1 + i] + p if i == normal else mass * w[1 + i])
    half = 0.5 * (w[1] * w[1] + w[2] * w[2] + w[3] * w[3])
    out.append(2.5 * p * u + mass * half)
    return out


def at8(row):
    return pl.ds(pl.multiple_of(row, 8), 8)


EDGE, REST, HALO, PHI, AFTER, A2A, BACK, MOM_Z, MOM_Y, DEF_Y, DEF_X, DENSITY, N_SEM = (
    0, 2, 10, 20, 24, 32, 40, 48, 52, 56, 72, 80, 88,
)


def step_kernel(
    st, before, dt_ref, bz_h, bzi_h, sf_h, si_h, tab_h, move_h,
    nb, added,
    raw, tmp, dense, tail, next_head, prev_tail, cons, prim, acc, below, above, pot, pot0, potz,
    xs, xr, ys, yr, pxs, pxr, pys, pyr,
    spec_t, spec_r, lines, trans, held, vsol, back_t, back_r, mom_z, mom_y, defs, dgx,
    bz, bzi, sf, si, tab, move, load_sem, ss, rs,
):
    g, k = lax.axis_index("gx"), lax.axis_index("gy")
    k_up, k_dn = (k + 1) % NK, (k + NK - 1) % NK
    g_up, g_dn = (g + 1) % NG, (g + NG - 1) % NG
    dt = dt_ref[0, 0]
    lane = lanes()
    sub = lax.broadcasted_iota(jnp.int32, (8, 128), 0)
    zed = lane % 64

    loads = [pltpu.make_async_copy(st.at[f], raw.at[f], load_sem.at[f]) for f in range(5)]
    consts = [(bz_h, bz), (sf_h, sf), (tab_h.at[g], tab), (si_h, si), (bzi_h, bzi), (move_h, move)]
    const_loads = [
        pltpu.make_async_copy(a, b, load_sem.at[5 + i]) for i, (a, b) in enumerate(consts)
    ]
    for c in loads + const_loads:
        c.start()

    barrier = pltpu.get_barrier_semaphore()

    def greet_y(o, _):
        pl.semaphore_signal(barrier, inc=1, device_id={"gy": (k + o) % NK}, device_id_type=MESH)
        return 0

    def greet_x(o, _):
        pl.semaphore_signal(barrier, inc=1, device_id={"gx": (g + o) % NG}, device_id_type=MESH)
        return 0

    lax.fori_loop(1, NK, greet_y, 0)
    lax.fori_loop(1, NG, greet_x, 0)

    def send(src, dst, sem, device, rsem=None):
        return pltpu.make_async_remote_copy(
            src_ref=src, dst_ref=dst, send_sem=ss.at[sem], recv_sem=rs.at[sem if rsem is None else rsem],
            device_id=device, device_id_type=MESH,
        )

    begin = before[g, k]
    end = jnp.where(k < NK - 1, before[g, jnp.minimum(k + 1, NK - 1)], 4 * NK)
    lead, trail = jnp.clip(begin - 4 * k, -1, 1), jnp.clip(end - 4 * (k + 1), -1, 1)
    last = jnp.clip(end - begin - 1, 0, 5)

    def spread(f):
        def body(x4, _):
            for i4 in range(4):
                x = x4 * 4 + i4
                v = raw[f, :, pl.ds(pl.multiple_of(x * 1024, 1024), 1024)]
                for s in range(8):
                    tmp[i4, 8 * s : 8 * s + 6, :] = v[:, 128 * s : 128 * s + 128]
                for slot in range(6):
                    dense[slot, f, x] = tmp[i4, pl.ds(slot, 8, stride=8), :]
            return 0

        lax.fori_loop(0, 8, body, 0)

        def tails(x4, _):
            for i4 in range(4):
                tail[f, x4 * 4 + i4] = dense[last, f, x4 * 4 + i4]
            return 0

        lax.fori_loop(0, 8, tails, 0)

    def assemble(fields, first, count, step):
        def body(i, _):
            for f in fields:
                for i4 in range(step):
                    x = first + i * step + i4
                    q0 = jnp.where(lead > 0, prev_tail[f, x], dense[jnp.maximum(-lead, 0), f, x])
                    q1 = dense[1 - lead, f, x]
                    q2 = dense[2 - lead, f, x]
                    q3 = jnp.where(trail < 0, next_head[f, x], dense[3 - lead, f, x])
                    for j, v in enumerate(swap4((q0, q2, q1, q3))):
                        cons[f, at8(x * 32 + 8 * j), :] = v
            return 0

        lax.fori_loop(0, count // step, body, 0)

    loads[0].wait()
    spread(0)
    pl.semaphore_wait(barrier, NK + NG - 2)
    edges = [
        send(dense.at[0, 0], next_head.at[0], EDGE, {"gy": k_dn}),
        send(tail.at[0], prev_tail.at[0], EDGE + 1, {"gy": k_up}),
    ]
    rest = [
        [
            send(dense.at[0, pl.ds(1, 4), span], next_head.at[pl.ds(1, 4), span], REST + 2 * i, {"gy": k_dn}),
            send(tail.at[pl.ds(1, 4), span], prev_tail.at[pl.ds(1, 4), span], REST + 2 * i + 1, {"gy": k_up}),
        ]
        for i, span in enumerate(pl.ds(PART * i, PART) for i in range(32 // PART))
    ]
    for c in edges:
        c.start()
    for f in range(1, 5):
        loads[f].wait()
        spread(f)
    for c in rest[0]:
        c.start()
    for c in edges:
        c.wait_recv()
    assemble((0,), 0, 32, 4)
    for c in const_loads:
        c.wait()

    def primitives(x, _):
        for j in range(4):
            rho, mx, my, mz, energy = [cons[f, at8(x * 32 + 8 * j), :] for f in range(5)]
            inverse = 1.0 / rho
            vx, vy, vz = mx * inverse, my * inverse, mz * inverse
            p = (GAMMA - 1.0) * (energy - 0.5 * rho * (vx * vx + vy * vy + vz * vz))
            for f, v in enumerate((rho, vx, vy, vz, p)):
                prim[f, at8((x + 2) * 64 + (j + 2) * 8), :] = v
        return 0

    def neighbours_z(x8, _):
        for f in range(5):
            v = jnp.concatenate(
                [prim[f, pl.ds(pl.multiple_of((x8 * 8 + i + 2) * 64 + 16, 16), 32), :] for i in range(8)]
            )
            upper_half = v.astype(jnp.bfloat16)
            lower_half = (v - upper_half.astype(jnp.float32)).astype(jnp.bfloat16)
            both = jnp.dot(
                jnp.concatenate([upper_half, lower_half], axis=1), move[...],
                preferred_element_type=jnp.float32,
            )
            rows = pl.ds(pl.multiple_of(x8 * 256, 256), 256)
            below[f, rows, :] = both[:, 0:128]
            above[f, rows, :] = both[:, 128:256]
        return 0

    def sweep_z(x, _):
        for j in range(4):
            row = at8(x * 32 + 8 * j)
            w = [prim[f, at8((x + 2) * 64 + (j + 2) * 8), :] for f in range(5)]
            left, right = [], []
            for f, v in enumerate(w):
                h = half_slope(v - below[f, row, :], above[f, row, :] - v)
                left.append(v + h)
                lower = v - h
                right.append(jnp.where(zed == 63, lower, pltpu.roll(lower, 127, 1)))
            high = face_flux(left, right, 2)
            wall = cell_flux(w, 2)
            for f in range(5):
                low = jnp.where(zed == 0, wall[f], pltpu.roll(high[f], 1, 1))
                acc[f, row, :] = high[f] - low
        return 0

    def halo_y(part):
        span = pl.ds(80 * part, 80)
        return [
            send(ys.at[0, span], yr.at[1, span], HALO + 2 * part, {"gy": k_dn}),
            send(ys.at[1, span], yr.at[0, span], HALO + 2 * part + 1, {"gy": k_up}),
        ]

    halo_x = [
        send(xs.at[0], xr.at[1], HALO + 8, {"gx": g_dn}),
        send(xs.at[1], xr.at[0], HALO + 9, {"gx": g_up}),
    ]

    def halo_copies(part):
        return halo_y(part) + (halo_x[:1] if part == 0 else halo_x[1:] if part == 3 else [])

    def send_halo(part):
        for f in range(5):
            for r in range(2):
                row = part * 80 + f * 16 + r * 8
                base = (2 + PART * part) * 64 + r * 8
                ys[0, row : row + 8, :] = prim[f, pl.ds(base + 16, 8, stride=64), :]
                ys[1, row : row + 8, :] = prim[f, pl.ds(base + 39, 8, stride=64), :]
                for side, at in ((0, 0), (1, 3)):
                    if part == at:
                        row, base = f * 64 + r * 32, (2 + 30 * side + r) * 64 + 16
                        xs[side, row : row + 32, :] = prim[f, base : base + 32, :]
        return halo_copies(part)

    def start_part(part):
        for c in rest[part]:
            c.wait_recv()
        first = part * PART
        assemble((1, 2, 3, 4), first, PART, 2)
        lax.fori_loop(first, first + PART, primitives, 0)
        for c in send_halo(part):
            c.start()
        neighbours_z(part, 0)
        lax.fori_loop(first, first + PART, sweep_z, 0)

    modes = lax.dot_general(
        bz[...], cons[0], (((1,), (1,)), ((), ())),
        precision=HIGHEST, preferred_element_type=jnp.float32,
    )
    for r in range(16):
        for c in range(8):
            spec_t[r, 8 * c : 8 * c + 8, :] = modes[8 * r : 8 * r + 8, 128 * c : 128 * c + 128]

    def a2a_copy(peer, source):
        return send(
            spec_t.at[pl.ds(2 * peer, 2)], spec_r.at[pl.ds(2 * source, 2)],
            A2A + peer, {"gx": peer}, A2A + source,
        )

    def start_a2a(o, _):
        a2a_copy((g + o) % NG, g).start()
        return 0

    lax.fori_loop(1, NG, start_a2a, 0)
    for c in rest[1]:
        c.start()
    spec_r[pl.ds(2 * g, 2)] = spec_t[pl.ds(2 * g, 2)]
    start_part(0)
    for c in rest[2]:
        c.start()
    start_part(1)

    def wait_a2a(o, _):
        source = (g + NG - o) % NG
        a2a_copy(source, source).wait_recv()
        return 0

    lax.fori_loop(1, NG, wait_a2a, 0)
    for c in rest[3]:
        c.start()

    def to_lines(r, _):
        for q in range(2):
            parts = [spec_r[r, pl.ds(4 * q + b, 8, stride=8), :] for b in range(4)]
            for i, v in enumerate(swap4(parts)):
                lines[at8(r * 32 + 8 * i), 128 * q : 128 * q + 128] = v
        return 0

    lax.fori_loop(0, 16, to_lines, 0)
    lined = lax.dot_general(
        lines[...], sf[...], (((0,), (0,)), ((), ())),
        precision=HIGHEST, preferred_element_type=jnp.float32,
    )
    for t in range(4):
        trans[t] = lined[:, 128 * t : 128 * t + 128]

    k_four, k_in = k // 4, k % 4
    lam, gain = tab[0], tab[1]
    lam2 = lam * lam
    lam4 = lam2 * lam2
    lam8 = lam4 * lam4
    lam16 = lam8 * lam8
    lam32 = lam16 * lam16
    lam64 = lam32 * lam32
    lam128 = lam64 * lam64

    def line_rows(y):
        return pl.ds((y % 4) * 8 + y // 4, 8, stride=32)

    def line(y):
        return jnp.concatenate([trans[t, line_rows(y), :] for t in range(4)], axis=1)

    def sums(i, carry):
        u, v = carry
        low, high = line(i), line(31 - i)
        held[i] = low
        return low + lam * u, high + lam * v

    zero = jnp.zeros((8, 512), jnp.float32)
    up_sum, down_sum = lax.fori_loop(0, 32, sums, (zero, zero))
    mom_z[k_in, 0:8, :] = up_sum
    mom_z[k_in, 8:16, :] = down_sum

    def mom_z_copy(peer, source):
        return send(
            mom_z.at[source], mom_z.at[source], MOM_Z + peer, {"gy": 4 * k_four + peer}, MOM_Z + source
        )

    def mom_y_copy(peer, source):
        return send(
            mom_y.at[source], mom_y.at[source], MOM_Y + peer, {"gy": 4 * peer + k_in}, MOM_Y + source
        )

    for o in range(1, 4):
        mom_z_copy((k_in + o) % 4, k_in).start()
    start_part(2)
    for o in range(1, 4):
        source = (k_in + 4 - o) % 4
        mom_z_copy(source, source).wait_recv()
    from_low, from_high, four_up, four_down = zero, zero, zero, zero
    power_low, power_high = zero + 1.0, zero + 1.0
    for i in range(4):
        ups, downs = mom_z[i, 0:8, :], mom_z[3 - i, 8:16, :]
        four_up = four_up * lam32 + ups
        four_down = four_down * lam32 + downs
        from_low = jnp.where(i < k_in, from_low * lam32 + ups, from_low)
        from_high = jnp.where(3 - i > k_in, from_high * lam32 + downs, from_high)
        power_low = jnp.where(i < k_in, power_low * lam32, power_low)
        power_high = jnp.where(3 - i > k_in, power_high * lam32, power_high)
    mom_y[k_four, 0:8, :] = four_up
    mom_y[k_four, 8:16, :] = four_down
    for o in range(1, 4):
        mom_y_copy((k_four + o) % 4, k_four).start()
    start_part(3)
    for o in range(1, 4):
        source = (k_four + 4 - o) % 4
        mom_y_copy(source, source).wait_recv()

    far_low, far_high, at_start, at_end = zero, zero, zero, zero
    far_power_low, far_power_high = zero + 1.0, zero + 1.0
    for i in range(4):
        ups, downs = mom_y[i, 0:8, :], mom_y[3 - i, 8:16, :]
        at_end = at_end * lam128 + ups
        at_start = at_start * lam128 + downs
        far_low = jnp.where(i < k_four, far_low * lam128 + ups, far_low)
        far_high = jnp.where(3 - i > k_four, far_high * lam128 + downs, far_high)
        far_power_low = jnp.where(i < k_four, far_power_low * lam128, far_power_low)
        far_power_high = jnp.where(3 - i > k_four, far_power_high * lam128, far_power_high)
    lam256 = lam128 * lam128
    whole = lam256 * lam256 * lam
    at_start, at_end = lam * at_start, lam * at_end
    scale = 1.0 / (1.0 - whole * whole)
    low_image = (at_start - whole * at_end) * scale * far_power_low
    high_image = (at_end - whole * at_start) * scale * far_power_high
    first_u = from_low + power_low * (far_low - low_image)
    first_v = from_high + power_high * (far_high - high_image)

    def downward(i, v):
        v = held[31 - i] + lam * v
        vsol[31 - i] = v
        return v

    lax.fori_loop(0, 32, downward, first_v)

    def upward(i, u):
        carried = lam * u
        f = held[i]
        value = gain * (carried + vsol[i])
        for t in range(4):
            trans[t, line_rows(i), :] = value[:, 128 * t : 128 * t + 128]
        return f + carried

    lax.fori_loop(0, 32, upward, first_u)
    lines[...] = lax.dot_general(
        si[...], jnp.concatenate([trans[t] for t in range(4)], axis=1), (((1,), (1,)), ((), ())),
        precision=HIGHEST, preferred_element_type=jnp.float32,
    )

    def from_lines(r, _):
        for q in range(2):
            parts = [lines[at8(r * 32 + 8 * i), 128 * q : 128 * q + 128] for i in range(4)]
            for b, v in enumerate(swap4(parts)):
                back_t[r, pl.ds(4 * q + b, 8, stride=8), :] = v
        return 0

    lax.fori_loop(0, 16, from_lines, 0)

    def back_copy(peer, source):
        return send(
            back_t.at[pl.ds(2 * peer, 2)], back_r.at[pl.ds(2 * source, 2)],
            BACK + peer, {"gx": peer}, BACK + source,
        )

    def start_back(o, _):
        back_copy((g + o) % NG, g).start()
        return 0

    lax.fori_loop(1, NG, start_back, 0)
    back_r[pl.ds(2 * g, 2)] = back_t[pl.ds(2 * g, 2)]


    def place_halo_x():
        for c in halo_x:
            c.wait_recv()
        for f in range(5):
            for r in range(2):
                for j in range(4):
                    row = f * 64 + r * 32 + j * 8
                    e = (j + 2) * 8

                    def plane(xx):
                        return prim[f, (xx + 2) * 64 + e : (xx + 2) * 64 + e + 8, :]

                    low = pltpu.roll(jnp.where(lane >= 64, xr[0, row : row + 8, :], plane(30 + r)), 64, 1)
                    low = jnp.where((lane < 64) & (g == 0), plane(0), low)
                    prim[f, r * 64 + e : r * 64 + e + 8, :] = low
                    high = pltpu.roll(jnp.where(lane < 64, xr[1, row : row + 8, :], plane(r)), 64, 1)
                    high = jnp.where((lane >= 64) & (g == NG - 1), plane(31), high)
                    prim[f, (34 + r) * 64 + e : (34 + r) * 64 + e + 8, :] = high

    def place_y(x, _):
        base = (x + 2) * 64
        for f in range(5):
            rows = [prim[f, at8(base + 16 + 8 * j), :] for j in range(4)]
            first = jnp.broadcast_to(rows[0][0:1, :], (8, 128))
            final = jnp.broadcast_to(rows[3][7:8, :], (8, 128))
            for r in range(2):
                row = (x // PART) * 80 + f * 16 + r * 8 + x % PART
                low = jnp.where(k == 0, first, jnp.broadcast_to(yr[0, pl.ds(row, 1), :], (8, 128)))
                prim[f, at8(base + 8 * r), :] = jnp.where(sub == 0, low, pltpu.roll(rows[2 + r], 1, 0))
                high = jnp.where(k == NK - 1, final, jnp.broadcast_to(yr[1, pl.ds(row, 1), :], (8, 128)))
                prim[f, at8(base + 48 + 8 * r), :] = jnp.where(sub == 7, high, pltpu.roll(rows[r], 7, 0))
        return 0

    def place_halo_y(part):
        for c in halo_y(part):
            c.wait_recv()
        lax.fori_loop(PART * part, PART * part + PART, place_y, 0)

    def sweep_row(cell, count, normal, target):
        before_left, before_flux = None, None
        for i in range(-1, count + 1):
            left, right = [], []
            for f in range(5):
                v = cell(f, i)
                h = half_slope(v - cell(f, i - 1), cell(f, i + 1) - v)
                left.append(v + h)
                right.append(v - h)
            if before_left is not None:
                flux = face_flux(before_left, right, normal)
                if before_flux is not None:
                    for f in range(5):
                        row = target(i - 1)
                        acc[f, row, :] = acc[f, row, :] + (flux[f] - before_flux[f])
                before_flux = flux
            before_left = left

    def hydro(part):
        def sweep_y(i, _):
            x = part * PART + i
            base = (x + 2) * 64 + 16
            sweep_row(
                lambda f, e: prim[f, at8(base + 8 * e), :], 4, 1, lambda e: at8(x * 32 + 8 * e)
            )
            return 0

        lax.fori_loop(0, PART, sweep_y, 0)

        def sweep_x(j, _):
            base = (part * PART + 2) * 64 + 16 + 8 * j
            sweep_row(
                lambda f, i: prim[f, at8(base + 64 * i), :], PART, 0,
                lambda i: at8((part * PART + i) * 32 + 8 * j),
            )
            return 0

        lax.fori_loop(0, 4, sweep_x, 0)

    def finish(part):
        def body(i, _):
            x = part * PART + i
            base = (x + 1) * 48 + 8
            new = [[None] * 4 for _ in range(4)]
            half = -0.5 * dt
            for j in range(4):
                ax = half * (pot[at8(base + 48 + 8 * j), :] - pot[at8(base - 48 + 8 * j), :])
                ay = half * (pot[at8(base + 8 + 8 * j), :] - pot[at8(base - 8 + 8 * j), :])
                az = half * potz[at8(x * 32 + 8 * j), :]
                u = [cons[f, at8(x * 32 + 8 * j), :] for f in range(5)]
                change = [acc[f, at8(x * 32 + 8 * j), :] for f in range(5)]
                for i3, a in enumerate((ax, ay, az)):
                    new[i3][j] = u[1 + i3] - dt * change[1 + i3] + u[0] * a
                new[3][j] = u[4] - dt * change[4] + (u[1] * ax + u[2] * ay + u[3] * az)
            for f in range(4):
                b0, b2, b1, b3 = swap4(new[f])
                for q, v in enumerate((b0, b1, b2, b3)):
                    nb[1 + q, 1 + f, x] = v
            return 0

        lax.fori_loop(0, PART, body, 0)

    def after_copies(part):
        fields, span = pl.ds(1, 4), pl.ds(part * PART, PART)
        return [
            send(nb.at[1, fields, span], nb.at[5, fields, span], AFTER + part, {"gy": k_dn}),
            send(nb.at[4, fields, span], nb.at[0, fields, span], AFTER + 4 + part, {"gy": k_up}),
        ]

    def emit(part):
        for c in after_copies(part):
            c.start()

    def deficit(x, total):
        for j in range(4):
            row = at8(x * 32 + 8 * j)
            density = cons[0, row, :] - dt * acc[0, row, :]
            total = total + (jnp.maximum(density, FLOOR) - density)
        return total

    def def_copy(peer, source):
        return send(defs.at[source], defs.at[source], DEF_Y + peer, {"gy": peer}, DEF_Y + source)

    def start_def(o, _):
        def_copy((k + o) % NK, k).start()
        return 0

    def wait_def(o, _):
        source = (k + NK - o) % NK
        def_copy(source, source).wait_recv()
        return 0

    def density_copies(part):
        span = pl.ds(part * PART, PART)
        return [
            send(nb.at[1, 0, span], nb.at[5, 0, span], DENSITY + part, {"gy": k_dn}),
            send(nb.at[4, 0, span], nb.at[0, 0, span], DENSITY + 4 + part, {"gy": k_up}),
        ]

    def finish_density(part):
        def body(i2, _):
            for i in range(2):
                x = part * PART + i2 * 2 + i
                new = []
                for j in range(4):
                    row = at8(x * 32 + 8 * j)
                    new.append(jnp.maximum(cons[0, row, :] - dt * acc[0, row, :], FLOOR))
                b0, b2, b1, b3 = swap4(new)
                for q, v in enumerate((b0, b1, b2, b3)):
                    nb[1 + q, 0, x] = v
            return 0

        lax.fori_loop(0, PART // 2, body, 0)
        for c in density_copies(part):
            c.start()

    place_halo_y(1)
    hydro(1)
    finish_density(1)
    place_halo_y(2)
    hydro(2)
    finish_density(2)

    def wait_back(o, _):
        source = (g + NG - o) % NG
        back_copy(source, source).wait_recv()
        return 0

    lax.fori_loop(1, NG, wait_back, 0)
    both = lax.dot_general(
        jnp.concatenate(
            [
                jnp.concatenate([back_r[r, 8 * c : 8 * c + 8, :] for c in range(8)], axis=1)
                for r in range(16)
            ]
        ),
        bzi[...], (((0,), (0,)), ((), ())),
        precision=HIGHEST, preferred_element_type=jnp.float32,
    )
    pot0[...] = both[:, 0:128]
    potz[...] = both[:, 128:256]
    pxs[0] = pot0[0:32, :]
    pxs[1] = pot0[31 * 32 : 32 * 32, :]
    for q in range(4):
        pys[0, 8 * q : 8 * q + 8, :] = pot0[pl.ds(8 * q * 32, 8, stride=32), :]
        pys[1, 8 * q : 8 * q + 8, :] = pot0[pl.ds(8 * q * 32 + 31, 8, stride=32), :]
    phi_halo = [
        send(pxs.at[0], pxr.at[1], PHI, {"gx": g_dn}),
        send(pxs.at[1], pxr.at[0], PHI + 1, {"gx": g_up}),
        send(pys.at[0], pyr.at[1], PHI + 2, {"gy": k_dn}),
        send(pys.at[1], pyr.at[0], PHI + 3, {"gy": k_up}),
    ]
    for c in phi_halo:
        c.start()

    place_halo_x()
    place_halo_y(0)
    place_halo_y(3)
    hydro(0)
    hydro(3)
    defs[k] = lax.fori_loop(0, 32, deficit, jnp.zeros((8, 128), jnp.float32))
    lax.fori_loop(1, NK, start_def, 0)
    finish_density(0)
    finish_density(3)
    for c in phi_halo:
        c.wait_recv()
    for j in range(4):
        low = pltpu.roll(
            jnp.where(lane >= 64, pxr[0, 8 * j : 8 * j + 8, :], pot0[31 * 32 + 8 * j : 31 * 32 + 8 * j + 8, :]), 64, 1
        )
        pot[8 + 8 * j : 16 + 8 * j, :] = jnp.where((lane < 64) & (g == 0), 0.0, low)
        high = pltpu.roll(jnp.where(lane < 64, pxr[1, 8 * j : 8 * j + 8, :], pot0[8 * j : 8 * j + 8, :]), 64, 1)
        pot[33 * 48 + 8 + 8 * j : 33 * 48 + 16 + 8 * j, :] = jnp.where((lane >= 64) & (g == NG - 1), 0.0, high)

    def place_pot(x, _):
        base = (x + 1) * 48
        rows = [pot0[at8(x * 32 + 8 * j), :] for j in range(4)]
        for j in range(4):
            pot[at8(base + 8 + 8 * j), :] = rows[j]
        low = jnp.where(k == 0, 0.0, jnp.broadcast_to(pyr[0, pl.ds(x, 1), :], (8, 128)))
        pot[at8(base), :] = jnp.where(sub == 0, low, pltpu.roll(rows[3], 1, 0))
        high = jnp.where(k == NK - 1, 0.0, jnp.broadcast_to(pyr[1, pl.ds(x, 1), :], (8, 128)))
        pot[at8(base + 40), :] = jnp.where(sub == 7, high, pltpu.roll(rows[0], 7, 0))
        return 0

    lax.fori_loop(0, 32, place_pot, 0)
    def finish_part(part):
        finish(part)
        emit(part)

    finish_part(1)
    finish_part(2)
    lax.fori_loop(1, NK, wait_def, 0)
    dgx[g] = jnp.sum(defs[...], axis=0)

    def dgx_copy(peer, source):
        return send(dgx.at[source], dgx.at[source], DEF_X + peer, {"gx": peer}, DEF_X + source)

    def start_dgx(o, _):
        dgx_copy((g + o) % NG, g).start()
        return 0

    def wait_dgx(o, _):
        source = (g + NG - o) % NG
        dgx_copy(source, source).wait_recv()
        return 0

    lax.fori_loop(1, NG, start_dgx, 0)
    for part in (0, 3):
        finish_part(part)
    lax.fori_loop(1, NG, wait_dgx, 0)
    added[0, 0] = jnp.sum(jnp.sum(dgx[...], axis=0)) * (1.0 / 512)

    halo = sum([halo_copies(part) for part in range(32 // PART)], [])
    for c in edges + sum(rest, []) + halo + phi_halo:
        c.wait_send()

    def sent_y(o, _):
        def_copy((k + o) % NK, k).wait_send()
        return 0

    def sent_x(o, _):
        peer = (g + o) % NG
        a2a_copy(peer, g).wait_send()
        back_copy(peer, g).wait_send()
        dgx_copy(peer, g).wait_send()
        return 0

    for o in range(1, 4):
        mom_z_copy((k_in + o) % 4, k_in).wait_send()
        mom_y_copy((k_four + o) % 4, k_four).wait_send()
    lax.fori_loop(1, NK, sent_y, 0)
    lax.fori_loop(1, NG, sent_x, 0)
    for part in range(32 // PART):
        for c in density_copies(part) + after_copies(part):
            c.wait()


def place_kernel(after, where, nb, out, tmp, ready, sem):
    g, k = where[0], where[1]
    begin = after[g, k]
    end = jnp.where(k < NK - 1, after[g, jnp.minimum(k + 1, NK - 1)], 4 * NK)
    lead, held = jnp.clip(begin - 4 * k, -1, 1), end - begin
    writes = [pltpu.make_async_copy(ready.at[f], out.at[f], sem.at[f]) for f in range(5)]
    for f in range(5):

        def body(x4, _):
            for i4 in range(4):
                x = x4 * 4 + i4
                for slot in range(6):
                    index = jnp.minimum(slot + lead + 1, 5)
                    v = jnp.where(slot < held, nb[index, f, x], 0.0)
                    tmp[i4, pl.ds(slot, 8, stride=8), :] = v
                for s in range(8):
                    ready[f, :, pl.ds(pl.multiple_of(x * 1024 + 128 * s, 128), 128)] = tmp[i4, 8 * s : 8 * s + 6, :]
            return 0

        lax.fori_loop(0, 8, body, 0)
        writes[f].start()
    for c in writes:
        c.wait()


def per_device(consts, state_before, before_start, after_start, time_step):
    f32 = jnp.float32
    st = jnp.transpose(state_before, (1, 0, 2))
    any_spec = pl.BlockSpec(memory_space=pl.ANY)
    smem = pl.BlockSpec(memory_space=pltpu.SMEM)
    vmem = pl.BlockSpec(memory_space=pltpu.VMEM)
    block = (5, 32, 8, 128)

    def scratch(*shape):
        return pltpu.VMEM(shape, f32)

    nb, added = pl.pallas_call(
        step_kernel,
        out_shape=(pltpu.VMEM((6,) + block, f32), jax.ShapeDtypeStruct((1, 1), f32)),
        in_specs=[any_spec, smem, smem] + [any_spec] * 6,
        out_specs=(vmem, smem),
        scratch_shapes=[
            scratch(5, 6, 32768),
            scratch(4, 64, 128),
            scratch(6, *block),
            scratch(*block),
            scratch(*block),
            scratch(*block),
            scratch(5, 1024, 128),
            scratch(5, 36 * 64, 128),
            scratch(5, 1024, 128),
            scratch(5, 1024, 128), scratch(5, 1024, 128),
            scratch(34 * 48, 128),
            scratch(1024, 128),
            scratch(1024, 128),
            scratch(2, 320, 128), scratch(2, 320, 128), scratch(2, 320, 128), scratch(2, 320, 128),
            scratch(2, 32, 128), scratch(2, 32, 128), scratch(2, 32, 128), scratch(2, 32, 128),
            scratch(16, 64, 128),
            scratch(16, 64, 128),
            scratch(512, 256),
            scratch(4, 256, 128),
            scratch(32, 8, 512),
            scratch(32, 8, 512),
            scratch(16, 64, 128),
            scratch(16, 64, 128),
            scratch(4, 16, 512),
            scratch(4, 16, 512),
            scratch(16, 8, 128),
            scratch(8, 8, 128),
            scratch(128, 128), scratch(128, 256), scratch(512, 512), scratch(512, 512),
            scratch(2, 8, 512),
            pltpu.VMEM((256, 256), jnp.bfloat16),
            pltpu.SemaphoreType.DMA((11,)),
            pltpu.SemaphoreType.DMA((N_SEM,)),
            pltpu.SemaphoreType.DMA((N_SEM,)),
        ],
        compiler_params=pltpu.CompilerParams(
            collective_id=0, has_side_effects=True, vmem_limit_bytes=58 * 1024 * 1024
        ),
        name="step",
    )(st, before_start, time_step.reshape(1, 1), *consts)

    where = jnp.stack([lax.axis_index("gx"), lax.axis_index("gy")]).astype(jnp.int32)
    out = pl.pallas_call(
        place_kernel,
        out_shape=jax.ShapeDtypeStruct((5, 6, 32768), f32),
        in_specs=[smem, smem, vmem],
        out_specs=any_spec,
        scratch_shapes=[
            scratch(4, 64, 128), scratch(5, 6, 32768), pltpu.SemaphoreType.DMA((5,)),
        ],
        compiler_params=pltpu.CompilerParams(vmem_limit_bytes=32 * 1024 * 1024),
        name="place",
    )(after_start, where, nb)
    return jnp.transpose(out, (1, 0, 2)), added.reshape(())


def solution(mesh):
    consts = tables()

    def run(*args):
        return per_device([jnp.asarray(c) for c in consts[:-1]] + [jnp.asarray(consts[-1], jnp.bfloat16)], *args)

    placed = (P(("gx", "gy"), None, None), P(), P(), P())
    return jax.shard_map(
        run,
        mesh=mesh,
        in_specs=placed,
        out_specs=(P(("gx", "gy"), None, None), P()),
        check_vma=False,
    )
```

```python
import jax
import jax.numpy as jnp
import numpy as np
from jax import lax
from jax.experimental import pallas as pl
from jax.experimental.pallas import tpu as pltpu
from jax.sharding import PartitionSpec as P

GAMMA = 5.0 / 3.0
FLOOR = 0.25
MESH = pl.DeviceIdType.MESH
HIGHEST = lax.Precision.HIGHEST

NK, NG, PART = 16, 8, 8


def tables():
    def sine(n):
        i = np.arange(1, n + 1)
        return np.sin(np.pi * ((i[:, None] * i[None, :]) % (2 * (n + 1))) / (n + 1))

    sine_x, sine_z = sine(512), sine(64)
    forward = np.zeros((8, 2, 8, 2, 64))
    for u in range(2):
        forward[:, u, :, u, :] = sine_z.reshape(8, 8, 64)
    forward = forward.reshape(128, 128)
    backward = forward * (2.0 / 65)
    padded = np.pad(backward.reshape(128, 2, 64), ((0, 0), (0, 0), (1, 1)))
    slope = (padded[:, :, 2:] - padded[:, :, :-2]).reshape(128, 128)
    order = np.arange(512).reshape(8, 2, 8, 4).transpose(0, 1, 3, 2).reshape(512)
    ordered = sine_x[order]
    modes_x = 2 - 2 * np.cos(np.pi * np.arange(1, 513) / 513)
    modes_z = 2 - 2 * np.cos(np.pi * np.arange(1, 65) / 65)
    h = 0.5 * (modes_z[:, None] + modes_x[None, :])
    root = np.sqrt(h * (h + 2))
    lam = 1 / (1 + h + root)
    gain = -0.5 / root

    table = np.stack([lam.reshape(8, 8, 512), gain.reshape(8, 8, 512)], axis=1)
    cell = np.arange(128)
    down = (cell[:, None] == cell - (cell % 64 > 0)).astype(np.float32)
    up = (cell[:, None] == cell + (cell % 64 < 63)).astype(np.float32)
    f32 = np.float32
    return (
        (forward * (4.0 / 64)).astype(f32),
        np.concatenate([backward, slope], axis=1).astype(f32),
        ordered.astype(f32),
        (ordered * (2.0 / 513)).astype(f32),
        table.astype(f32),
        np.tile(np.concatenate([down, up], axis=1), (2, 1)),
    )


def lanes():
    return lax.broadcasted_iota(jnp.int32, (8, 128), 1)


def swap4(parts):
    group = lanes() // 32
    low, even = group < 2, group % 2 == 0

    def pick(order):
        return jnp.where(low, jnp.where(even, order[0], order[1]), jnp.where(even, order[2], order[3]))

    turned = []
    for r in range(4):
        mixed = pick([parts[(i + r) % 4] for i in range(4)])
        turned.append(pltpu.roll(mixed, 32 * r, 1) if r else mixed)
    return [pick([turned[(b - j) % 4] for b in range(4)]) for j in range(4)]


def half_slope(down, up):
    quarter = 0.25 * (down + up)
    low = jnp.minimum(jnp.maximum(down, up), 0.0)
    high = jnp.maximum(jnp.minimum(down, up), 0.0)
    return jnp.minimum(jnp.maximum(quarter, low), high)


def face_flux(left, right, normal):
    def side(w):
        rho, vx, vy, vz, p = w
        gp = GAMMA * p
        return gp * lax.rsqrt(gp * rho), 0.5 * (vx * vx + vy * vy + vz * vz)

    sound_l, half_l = side(left)
    sound_r, half_r = side(right)
    ul, ur = left[1 + normal], right[1 + normal]
    fast = jnp.maximum(jnp.maximum(ul + sound_l, ur + sound_r), 0.0)
    slow = jnp.minimum(jnp.minimum(ul - sound_l, ur - sound_r), 0.0)
    inverse = 1.0 / (fast - slow)
    a, b = fast * inverse, slow * inverse
    d = fast * b
    kl, kr = a * ul - d, d - b * ur
    gl, gr = left[0] * kl, right[0] * kr
    apl, bpr = a * left[4], b * right[4]
    out = [gl + gr]
    for i in range(3):
        term = gl * left[1 + i] + gr * right[1 + i]
        out.append(term + (apl - bpr) if i == normal else term)
    out.append(
        1.5 * (left[4] * kl + right[4] * kr) + (gl * half_l + gr * half_r) + (apl * ul - bpr * ur)
    )
    return out


def cell_flux(w, normal):
    rho, p, u = w[0], w[4], w[1 + normal]
    mass = rho * u
    out = [mass]
    for i in range(3):
        out.append(mass * w[1 + i] + p if i == normal else mass * w[1 + i])
    half = 0.5 * (w[1] * w[1] + w[2] * w[2] + w[3] * w[3])
    out.append(2.5 * p * u + mass * half)
    return out


def at8(row):
    return pl.ds(pl.multiple_of(row, 8), 8)


EDGE, REST, HALO, PHI, AFTER, A2A, BACK, MOM_Z, MOM_Y, DEF_Y, DEF_X, DENSITY, N_SEM = (
    0, 2, 10, 20, 24, 32, 40, 48, 52, 56, 72, 80, 88,
)


def step_kernel(
    st, before, dt_ref, bz_h, bzi_h, sf_h, si_h, tab_h, move_h,
    nb, added,
    raw, tmp, dense, tail, next_head, prev_tail, cons, prim, acc, below, above, pot, pot0, potz,
    xs, xr, ys, yr, pxs, pxr, pys, pyr,
    spec_t, spec_r, lines, trans, held, vsol, back_t, back_r, mom_z, mom_y, defs, dgx,
    bz, bzi, sf, si, tab, move, load_sem, ss, rs,
):
    g, k = lax.axis_index("gx"), lax.axis_index("gy")
    k_up, k_dn = (k + 1) % NK, (k + NK - 1) % NK
    g_up, g_dn = (g + 1) % NG, (g + NG - 1) % NG
    dt = dt_ref[0, 0]
    lane = lanes()
    sub = lax.broadcasted_iota(jnp.int32, (8, 128), 0)
    zed = lane % 64

    loads = [pltpu.make_async_copy(st.at[f], raw.at[f], load_sem.at[f]) for f in range(5)]
    consts = [(bz_h, bz), (sf_h, sf), (tab_h.at[g], tab), (si_h, si), (bzi_h, bzi), (move_h, move)]
    const_loads = [
        pltpu.make_async_copy(a, b, load_sem.at[5 + i]) for i, (a, b) in enumerate(consts)
    ]
    for c in loads + const_loads:
        c.start()

    barrier = pltpu.get_barrier_semaphore()

    def greet_y(o, _):
        pl.semaphore_signal(barrier, inc=1, device_id={"gy": (k + o) % NK}, device_id_type=MESH)
        return 0

    def greet_x(o, _):
        pl.semaphore_signal(barrier, inc=1, device_id={"gx": (g + o) % NG}, device_id_type=MESH)
        return 0

    lax.fori_loop(1, NK, greet_y, 0)
    lax.fori_loop(1, NG, greet_x, 0)

    def send(src, dst, sem, device, rsem=None):
        return pltpu.make_async_remote_copy(
            src_ref=src, dst_ref=dst, send_sem=ss.at[sem], recv_sem=rs.at[sem if rsem is None else rsem],
            device_id=device, device_id_type=MESH,
        )

    begin = before[g, k]
    end = jnp.where(k < NK - 1, before[g, jnp.minimum(k + 1, NK - 1)], 4 * NK)
    lead, trail = jnp.clip(begin - 4 * k, -1, 1), jnp.clip(end - 4 * (k + 1), -1, 1)
    last = jnp.clip(end - begin - 1, 0, 5)

    def spread(f):
        def body(x4, _):
            for i4 in range(4):
                x = x4 * 4 + i4
                v = raw[f, :, pl.ds(pl.multiple_of(x * 1024, 1024), 1024)]
                for s in range(8):
                    tmp[i4, 8 * s : 8 * s + 6, :] = v[:, 128 * s : 128 * s + 128]
                for slot in range(6):
                    dense[slot, f, x] = tmp[i4, pl.ds(slot, 8, stride=8), :]
            return 0

        lax.fori_loop(0, 8, body, 0)

        def tails(x4, _):
            for i4 in range(4):
                tail[f, x4 * 4 + i4] = dense[last, f, x4 * 4 + i4]
            return 0

        lax.fori_loop(0, 8, tails, 0)

    def assemble(fields, first, count, step):
        def body(i, _):
            for f in fields:
                for i4 in range(step):
                    x = first + i * step + i4
                    q0 = jnp.where(lead > 0, prev_tail[f, x], dense[jnp.maximum(-lead, 0), f, x])
                    q1 = dense[1 - lead, f, x]
                    q2 = dense[2 - lead, f, x]
                    q3 = jnp.where(trail < 0, next_head[f, x], dense[3 - lead, f, x])
                    for j, v in enumerate(swap4((q0, q2, q1, q3))):
                        cons[f, at8(x * 32 + 8 * j), :] = v
            return 0

        lax.fori_loop(0, count // step, body, 0)

    loads[0].wait()
    spread(0)
    pl.semaphore_wait(barrier, NK + NG - 2)
    edges = [
        send(dense.at[0, 0], next_head.at[0], EDGE, {"gy": k_dn}),
        send(tail.at[0], prev_tail.at[0], EDGE + 1, {"gy": k_up}),
    ]
    rest = [
        [
            send(dense.at[0, pl.ds(1, 4), span], next_head.at[pl.ds(1, 4), span], REST + 2 * i, {"gy": k_dn}),
            send(tail.at[pl.ds(1, 4), span], prev_tail.at[pl.ds(1, 4), span], REST + 2 * i + 1, {"gy": k_up}),
        ]
        for i, span in enumerate(pl.ds(PART * i, PART) for i in range(32 // PART))
    ]
    for c in edges:
        c.start()
    for f in range(1, 5):
        loads[f].wait()
        spread(f)
    for c in rest[0]:
        c.start()
    for c in edges:
        c.wait_recv()
    assemble((0,), 0, 32, 4)
    for c in const_loads:
        c.wait()

    def primitives(x, _):
        for j in range(4):
            rho, mx, my, mz, energy = [cons[f, at8(x * 32 + 8 * j), :] for f in range(5)]
            inverse = 1.0 / rho
            vx, vy, vz = mx * inverse, my * inverse, mz * inverse
            p = (GAMMA - 1.0) * (energy - 0.5 * rho * (vx * vx + vy * vy + vz * vz))
            for f, v in enumerate((rho, vx, vy, vz, p)):
                prim[f, at8((x + 2) * 64 + (j + 2) * 8), :] = v
        return 0

    def neighbours_z(x8, _):
        for f in range(5):
            v = jnp.concatenate(
                [prim[f, pl.ds(pl.multiple_of((x8 * 8 + i + 2) * 64 + 16, 16), 32), :] for i in range(8)]
            )
            upper_half = v.astype(jnp.bfloat16)
            lower_half = (v - upper_half.astype(jnp.float32)).astype(jnp.bfloat16)
            both = jnp.dot(
                jnp.concatenate([upper_half, lower_half], axis=1), move[...],
                preferred_element_type=jnp.float32,
            )
            rows = pl.ds(pl.multiple_of(x8 * 256, 256), 256)
            below[f, rows, :] = both[:, 0:128]
            above[f, rows, :] = both[:, 128:256]
        return 0

    def sweep_z(x, _):
        for j in range(4):
            row = at8(x * 32 + 8 * j)
            w = [prim[f, at8((x + 2) * 64 + (j + 2) * 8), :] for f in range(5)]
            left, right = [], []
            for f, v in enumerate(w):
                h = half_slope(v - below[f, row, :], above[f, row, :] - v)
                left.append(v + h)
                lower = v - h
                right.append(jnp.where(zed == 63, lower, pltpu.roll(lower, 127, 1)))
            high = face_flux(left, right, 2)
            wall = cell_flux(w, 2)
            for f in range(5):
                low = jnp.where(zed == 0, wall[f], pltpu.roll(high[f], 1, 1))
                acc[f, row, :] = high[f] - low
        return 0

    def halo_y(part):
        span = pl.ds(80 * part, 80)
        return [
            send(ys.at[0, span], yr.at[1, span], HALO + 2 * part, {"gy": k_dn}),
            send(ys.at[1, span], yr.at[0, span], HALO + 2 * part + 1, {"gy": k_up}),
        ]

    halo_x = [
        send(xs.at[0], xr.at[1], HALO + 8, {"gx": g_dn}),
        send(xs.at[1], xr.at[0], HALO + 9, {"gx": g_up}),
    ]

    def halo_copies(part):
        return halo_y(part) + (halo_x[:1] if part == 0 else halo_x[1:] if part == 3 else [])

    def send_halo(part):
        for f in range(5):
            for r in range(2):
                row = part * 80 + f * 16 + r * 8
                base = (2 + PART * part) * 64 + r * 8
                ys[0, row : row + 8, :] = prim[f, pl.ds(base + 16, 8, stride=64), :]
                ys[1, row : row + 8, :] = prim[f, pl.ds(base + 39, 8, stride=64), :]
                for side, at in ((0, 0), (1, 3)):
                    if part == at:
                        row, base = f * 64 + r * 32, (2 + 30 * side + r) * 64 + 16
                        xs[side, row : row + 32, :] = prim[f, base : base + 32, :]
        return halo_copies(part)

    def start_part(part):
        for c in rest[part]:
            c.wait_recv()
        first = part * PART
        assemble((1, 2, 3, 4), first, PART, 2)
        lax.fori_loop(first, first + PART, primitives, 0)
        for c in send_halo(part):
            c.start()
        neighbours_z(part, 0)
        lax.fori_loop(first, first + PART, sweep_z, 0)

    modes = lax.dot_general(
        bz[...], cons[0], (((1,), (1,)), ((), ())),
        precision=HIGHEST, preferred_element_type=jnp.float32,
    )
    for r in range(16):
        for c in range(8):
            spec_t[r, 8 * c : 8 * c + 8, :] = modes[8 * r : 8 * r + 8, 128 * c : 128 * c + 128]

    def a2a_copy(peer, source):
        return send(
            spec_t.at[pl.ds(2 * peer, 2)], spec_r.at[pl.ds(2 * source, 2)],
            A2A + peer, {"gx": peer}, A2A + source,
        )

    def start_a2a(o, _):
        a2a_copy((g + o) % NG, g).start()
        return 0

    lax.fori_loop(1, NG, start_a2a, 0)
    for c in rest[1]:
        c.start()
    spec_r[pl.ds(2 * g, 2)] = spec_t[pl.ds(2 * g, 2)]
    start_part(0)
    for c in rest[2]:
        c.start()
    start_part(1)

    def wait_a2a(o, _):
        source = (g + NG - o) % NG
        a2a_copy(source, source).wait_recv()
        return 0

    lax.fori_loop(1, NG, wait_a2a, 0)
    for c in rest[3]:
        c.start()

    def to_lines(r, _):
        for q in range(2):
            parts = [spec_r[r, pl.ds(4 * q + b, 8, stride=8), :] for b in range(4)]
            for i, v in enumerate(swap4(parts)):
                lines[at8(r * 32 + 8 * i), 128 * q : 128 * q + 128] = v
        return 0

    lax.fori_loop(0, 16, to_lines, 0)
    lined = lax.dot_general(
        lines[...], sf[...], (((0,), (0,)), ((), ())),
        precision=HIGHEST, preferred_element_type=jnp.float32,
    )
    for t in range(4):
        trans[t] = lined[:, 128 * t : 128 * t + 128]

    k_four, k_in = k // 4, k % 4
    lam, gain = tab[0], tab[1]
    lam2 = lam * lam
    lam4 = lam2 * lam2
    lam8 = lam4 * lam4
    lam16 = lam8 * lam8
    lam32 = lam16 * lam16
    lam64 = lam32 * lam32
    lam128 = lam64 * lam64

    def line_rows(y):
        return pl.ds((y % 4) * 8 + y // 4, 8, stride=32)

    def line(y):
        return jnp.concatenate([trans[t, line_rows(y), :] for t in range(4)], axis=1)

    def sums(i, carry):
        u, v = carry
        low, high = line(i), line(31 - i)
        held[i] = low
        return low + lam * u, high + lam * v

    zero = jnp.zeros((8, 512), jnp.float32)
    up_sum, down_sum = lax.fori_loop(0, 32, sums, (zero, zero))
    mom_z[k_in, 0:8, :] = up_sum
    mom_z[k_in, 8:16, :] = down_sum

    def mom_z_copy(peer, source):
        return send(
            mom_z.at[source], mom_z.at[source], MOM_Z + peer, {"gy": 4 * k_four + peer}, MOM_Z + source
        )

    def mom_y_copy(peer, source):
        return send(
            mom_y.at[source], mom_y.at[source], MOM_Y + peer, {"gy": 4 * peer + k_in}, MOM_Y + source
        )

    for o in range(1, 4):
        mom_z_copy((k_in + o) % 4, k_in).start()
    start_part(2)
    for o in range(1, 4):
        source = (k_in + 4 - o) % 4
        mom_z_copy(source, source).wait_recv()
    from_low, from_high, four_up, four_down = zero, zero, zero, zero
    power_low, power_high = zero + 1.0, zero + 1.0
    for i in range(4):
        ups, downs = mom_z[i, 0:8, :], mom_z[3 - i, 8:16, :]
        four_up = four_up * lam32 + ups
        four_down = four_down * lam32 + downs
        from_low = jnp.where(i < k_in, from_low * lam32 + ups, from_low)
        from_high = jnp.where(3 - i > k_in, from_high * lam32 + downs, from_high)
        power_low = jnp.where(i < k_in, power_low * lam32, power_low)
        power_high = jnp.where(3 - i > k_in, power_high * lam32, power_high)
    mom_y[k_four, 0:8, :] = four_up
    mom_y[k_four, 8:16, :] = four_down
    for o in range(1, 4):
        mom_y_copy((k_four + o) % 4, k_four).start()
    start_part(3)
    for o in range(1, 4):
        source = (k_four + 4 - o) % 4
        mom_y_copy(source, source).wait_recv()

    far_low, far_high, at_start, at_end = zero, zero, zero, zero
    far_power_low, far_power_high = zero + 1.0, zero + 1.0
    for i in range(4):
        ups, downs = mom_y[i, 0:8, :], mom_y[3 - i, 8:16, :]
        at_end = at_end * lam128 + ups
        at_start = at_start * lam128 + downs
        far_low = jnp.where(i < k_four, far_low * lam128 + ups, far_low)
        far_high = jnp.where(3 - i > k_four, far_high * lam128 + downs, far_high)
        far_power_low = jnp.where(i < k_four, far_power_low * lam128, far_power_low)
        far_power_high = jnp.where(3 - i > k_four, far_power_high * lam128, far_power_high)
    lam256 = lam128 * lam128
    whole = lam256 * lam256 * lam
    at_start, at_end = lam * at_start, lam * at_end
    scale = 1.0 / (1.0 - whole * whole)
    low_image = (at_start - whole * at_end) * scale * far_power_low
    high_image = (at_end - whole * at_start) * scale * far_power_high
    first_u = from_low + power_low * (far_low - low_image)
    first_v = from_high + power_high * (far_high - high_image)

    def downward(i, v):
        v = held[31 - i] + lam * v
        vsol[31 - i] = v
        return v

    lax.fori_loop(0, 32, downward, first_v)

    def upward(i, u):
        carried = lam * u
        f = held[i]
        value = gain * (carried + vsol[i])
        for t in range(4):
            trans[t, line_rows(i), :] = value[:, 128 * t : 128 * t + 128]
        return f + carried

    lax.fori_loop(0, 32, upward, first_u)
    lines[...] = lax.dot_general(
        si[...], jnp.concatenate([trans[t] for t in range(4)], axis=1), (((1,), (1,)), ((), ())),
        precision=HIGHEST, preferred_element_type=jnp.float32,
    )

    def from_lines(r, _):
        for q in range(2):
            parts = [lines[at8(r * 32 + 8 * i), 128 * q : 128 * q + 128] for i in range(4)]
            for b, v in enumerate(swap4(parts)):
                back_t[r, pl.ds(4 * q + b, 8, stride=8), :] = v
        return 0

    lax.fori_loop(0, 16, from_lines, 0)

    def back_copy(peer, source):
        return send(
            back_t.at[pl.ds(2 * peer, 2)], back_r.at[pl.ds(2 * source, 2)],
            BACK + peer, {"gx": peer}, BACK + source,
        )

    def start_back(o, _):
        back_copy((g + o) % NG, g).start()
        return 0

    lax.fori_loop(1, NG, start_back, 0)
    back_r[pl.ds(2 * g, 2)] = back_t[pl.ds(2 * g, 2)]


    def place_halo_x():
        for c in halo_x:
            c.wait_recv()
        for f in range(5):
            for r in range(2):
                for j in range(4):
                    row = f * 64 + r * 32 + j * 8
                    e = (j + 2) * 8

                    def plane(xx):
                        return prim[f, (xx + 2) * 64 + e : (xx + 2) * 64 + e + 8, :]

                    low = pltpu.roll(jnp.where(lane >= 64, xr[0, row : row + 8, :], plane(30 + r)), 64, 1)
                    low = jnp.where((lane < 64) & (g == 0), plane(0), low)
                    prim[f, r * 64 + e : r * 64 + e + 8, :] = low
                    high = pltpu.roll(jnp.where(lane < 64, xr[1, row : row + 8, :], plane(r)), 64, 1)
                    high = jnp.where((lane >= 64) & (g == NG - 1), plane(31), high)
                    prim[f, (34 + r) * 64 + e : (34 + r) * 64 + e + 8, :] = high

    def place_y(x, _):
        base = (x + 2) * 64
        for f in range(5):
            rows = [prim[f, at8(base + 16 + 8 * j), :] for j in range(4)]
            first = jnp.broadcast_to(rows[0][0:1, :], (8, 128))
            final = jnp.broadcast_to(rows[3][7:8, :], (8, 128))
            for r in range(2):
                row = (x // PART) * 80 + f * 16 + r * 8 + x % PART
                low = jnp.where(k == 0, first, jnp.broadcast_to(yr[0, pl.ds(row, 1), :], (8, 128)))
                prim[f, at8(base + 8 * r), :] = jnp.where(sub == 0, low, pltpu.roll(rows[2 + r], 1, 0))
                high = jnp.where(k == NK - 1, final, jnp.broadcast_to(yr[1, pl.ds(row, 1), :], (8, 128)))
                prim[f, at8(base + 48 + 8 * r), :] = jnp.where(sub == 7, high, pltpu.roll(rows[r], 7, 0))
        return 0

    def place_halo_y(part):
        for c in halo_y(part):
            c.wait_recv()
        lax.fori_loop(PART * part, PART * part + PART, place_y, 0)

    def sweep_row(cell, count, normal, target):
        before_left, before_flux = None, None
        for i in range(-1, count + 1):
            left, right = [], []
            for f in range(5):
                v = cell(f, i)
                h = half_slope(v - cell(f, i - 1), cell(f, i + 1) - v)
                left.append(v + h)
                right.append(v - h)
            if before_left is not None:
                flux = face_flux(before_left, right, normal)
                if before_flux is not None:
                    for f in range(5):
                        row = target(i - 1)
                        acc[f, row, :] = acc[f, row, :] + (flux[f] - before_flux[f])
                before_flux = flux
            before_left = left

    def hydro(part):
        def sweep_y(i, _):
            x = part * PART + i
            base = (x + 2) * 64 + 16
            sweep_row(
                lambda f, e: prim[f, at8(base + 8 * e), :], 4, 1, lambda e: at8(x * 32 + 8 * e)
            )
            return 0

        lax.fori_loop(0, PART, sweep_y, 0)

        def sweep_x(j, _):
            base = (part * PART + 2) * 64 + 16 + 8 * j
            sweep_row(
                lambda f, i: prim[f, at8(base + 64 * i), :], PART, 0,
                lambda i: at8((part * PART + i) * 32 + 8 * j),
            )
            return 0

        lax.fori_loop(0, 4, sweep_x, 0)

    def finish(part):
        def body(i, _):
            x = part * PART + i
            base = (x + 1) * 48 + 8
            new = [[None] * 4 for _ in range(4)]
            half = -0.5 * dt
            for j in range(4):
                ax = half * (pot[at8(base + 48 + 8 * j), :] - pot[at8(base - 48 + 8 * j), :])
                ay = half * (pot[at8(base + 8 + 8 * j), :] - pot[at8(base - 8 + 8 * j), :])
                az = half * potz[at8(x * 32 + 8 * j), :]
                u = [cons[f, at8(x * 32 + 8 * j), :] for f in range(5)]
                change = [acc[f, at8(x * 32 + 8 * j), :] for f in range(5)]
                for i3, a in enumerate((ax, ay, az)):
                    new[i3][j] = u[1 + i3] - dt * change[1 + i3] + u[0] * a
                new[3][j] = u[4] - dt * change[4] + (u[1] * ax + u[2] * ay + u[3] * az)
            for f in range(4):
                b0, b2, b1, b3 = swap4(new[f])
                for q, v in enumerate((b0, b1, b2, b3)):
                    nb[1 + q, 1 + f, x] = v
            return 0

        lax.fori_loop(0, PART, body, 0)

    def after_copies(part):
        fields, span = pl.ds(1, 4), pl.ds(part * PART, PART)
        return [
            send(nb.at[1, fields, span], nb.at[5, fields, span], AFTER + part, {"gy": k_dn}),
            send(nb.at[4, fields, span], nb.at[0, fields, span], AFTER + 4 + part, {"gy": k_up}),
        ]

    def emit(part):
        for c in after_copies(part):
            c.start()

    def deficit(x, total):
        for j in range(4):
            row = at8(x * 32 + 8 * j)
            density = cons[0, row, :] - dt * acc[0, row, :]
            total = total + (jnp.maximum(density, FLOOR) - density)
        return total

    def def_copy(peer, source):
        return send(defs.at[source], defs.at[source], DEF_Y + peer, {"gy": peer}, DEF_Y + source)

    def start_def(o, _):
        def_copy((k + o) % NK, k).start()
        return 0

    def wait_def(o, _):
        source = (k + NK - o) % NK
        def_copy(source, source).wait_recv()
        return 0

    def density_copies(part):
        span = pl.ds(part * PART, PART)
        return [
            send(nb.at[1, 0, span], nb.at[5, 0, span], DENSITY + part, {"gy": k_dn}),
            send(nb.at[4, 0, span], nb.at[0, 0, span], DENSITY + 4 + part, {"gy": k_up}),
        ]

    def finish_density(part):
        def body(i2, _):
            for i in range(2):
                x = part * PART + i2 * 2 + i
                new = []
                for j in range(4):
                    row = at8(x * 32 + 8 * j)
                    new.append(jnp.maximum(cons[0, row, :] - dt * acc[0, row, :], FLOOR))
                b0, b2, b1, b3 = swap4(new)
                for q, v in enumerate((b0, b1, b2, b3)):
                    nb[1 + q, 0, x] = v
            return 0

        lax.fori_loop(0, PART // 2, body, 0)
        for c in density_copies(part):
            c.start()

    place_halo_y(1)
    hydro(1)
    finish_density(1)
    place_halo_y(2)
    hydro(2)
    finish_density(2)
    place_halo_x()
    place_halo_y(3)
    hydro(3)
    finish_density(3)

    def wait_back(o, _):
        source = (g + NG - o) % NG
        back_copy(source, source).wait_recv()
        return 0

    lax.fori_loop(1, NG, wait_back, 0)
    both = lax.dot_general(
        jnp.concatenate(
            [
                jnp.concatenate([back_r[r, 8 * c : 8 * c + 8, :] for c in range(8)], axis=1)
                for r in range(16)
            ]
        ),
        bzi[...], (((0,), (0,)), ((), ())),
        precision=HIGHEST, preferred_element_type=jnp.float32,
    )
    pot0[...] = both[:, 0:128]
    potz[...] = both[:, 128:256]
    pxs[0] = pot0[0:32, :]
    pxs[1] = pot0[31 * 32 : 32 * 32, :]
    for q in range(4):
        pys[0, 8 * q : 8 * q + 8, :] = pot0[pl.ds(8 * q * 32, 8, stride=32), :]
        pys[1, 8 * q : 8 * q + 8, :] = pot0[pl.ds(8 * q * 32 + 31, 8, stride=32), :]
    phi_halo = [
        send(pxs.at[0], pxr.at[1], PHI, {"gx": g_dn}),
        send(pxs.at[1], pxr.at[0], PHI + 1, {"gx": g_up}),
        send(pys.at[0], pyr.at[1], PHI + 2, {"gy": k_dn}),
        send(pys.at[1], pyr.at[0], PHI + 3, {"gy": k_up}),
    ]
    for c in phi_halo:
        c.start()

    place_halo_y(0)
    hydro(0)
    defs[k] = lax.fori_loop(0, 32, deficit, jnp.zeros((8, 128), jnp.float32))
    lax.fori_loop(1, NK, start_def, 0)
    finish_density(0)
    for c in phi_halo:
        c.wait_recv()
    for j in range(4):
        low = pltpu.roll(
            jnp.where(lane >= 64, pxr[0, 8 * j : 8 * j + 8, :], pot0[31 * 32 + 8 * j : 31 * 32 + 8 * j + 8, :]), 64, 1
        )
        pot[8 + 8 * j : 16 + 8 * j, :] = jnp.where((lane < 64) & (g == 0), 0.0, low)
        high = pltpu.roll(jnp.where(lane < 64, pxr[1, 8 * j : 8 * j + 8, :], pot0[8 * j : 8 * j + 8, :]), 64, 1)
        pot[33 * 48 + 8 + 8 * j : 33 * 48 + 16 + 8 * j, :] = jnp.where((lane >= 64) & (g == NG - 1), 0.0, high)

    def place_pot(x, _):
        base = (x + 1) * 48
        rows = [pot0[at8(x * 32 + 8 * j), :] for j in range(4)]
        for j in range(4):
            pot[at8(base + 8 + 8 * j), :] = rows[j]
        low = jnp.where(k == 0, 0.0, jnp.broadcast_to(pyr[0, pl.ds(x, 1), :], (8, 128)))
        pot[at8(base), :] = jnp.where(sub == 0, low, pltpu.roll(rows[3], 1, 0))
        high = jnp.where(k == NK - 1, 0.0, jnp.broadcast_to(pyr[1, pl.ds(x, 1), :], (8, 128)))
        pot[at8(base + 40), :] = jnp.where(sub == 7, high, pltpu.roll(rows[0], 7, 0))
        return 0

    lax.fori_loop(0, 32, place_pot, 0)
    def finish_part(part):
        finish(part)
        emit(part)

    finish_part(1)
    finish_part(2)
    lax.fori_loop(1, NK, wait_def, 0)
    dgx[g] = jnp.sum(defs[...], axis=0)

    def dgx_copy(peer, source):
        return send(dgx.at[source], dgx.at[source], DEF_X + peer, {"gx": peer}, DEF_X + source)

    def start_dgx(o, _):
        dgx_copy((g + o) % NG, g).start()
        return 0

    def wait_dgx(o, _):
        source = (g + NG - o) % NG
        dgx_copy(source, source).wait_recv()
        return 0

    lax.fori_loop(1, NG, start_dgx, 0)
    for part in (0, 3):
        finish_part(part)
    lax.fori_loop(1, NG, wait_dgx, 0)
    added[0, 0] = jnp.sum(jnp.sum(dgx[...], axis=0)) * (1.0 / 512)

    halo = sum([halo_copies(part) for part in range(32 // PART)], [])
    for c in edges + sum(rest, []) + halo + phi_halo:
        c.wait_send()

    def sent_y(o, _):
        def_copy((k + o) % NK, k).wait_send()
        return 0

    def sent_x(o, _):
        peer = (g + o) % NG
        a2a_copy(peer, g).wait_send()
        back_copy(peer, g).wait_send()
        dgx_copy(peer, g).wait_send()
        return 0

    for o in range(1, 4):
        mom_z_copy((k_in + o) % 4, k_in).wait_send()
        mom_y_copy((k_four + o) % 4, k_four).wait_send()
    lax.fori_loop(1, NK, sent_y, 0)
    lax.fori_loop(1, NG, sent_x, 0)
    for part in range(32 // PART):
        for c in density_copies(part) + after_copies(part):
            c.wait()


def place_kernel(after, where, nb, out, tmp, ready, sem):
    g, k = where[0], where[1]
    begin = after[g, k]
    end = jnp.where(k < NK - 1, after[g, jnp.minimum(k + 1, NK - 1)], 4 * NK)
    lead, held = jnp.clip(begin - 4 * k, -1, 1), end - begin
    halves = [pl.ds(0, 16384), pl.ds(16384, 16384)]
    writes = [
        pltpu.make_async_copy(ready.at[f, :, h], out.at[f, :, h], sem.at[2 * f + i])
        for f in range(5)
        for i, h in enumerate(halves)
    ]
    for f in range(5):

        def body(x4, _):
            for i4 in range(4):
                x = x4 * 4 + i4
                for slot in range(6):
                    index = jnp.minimum(slot + lead + 1, 5)
                    v = jnp.where(slot < held, nb[index, f, x], 0.0)
                    tmp[i4, pl.ds(slot, 8, stride=8), :] = v
                for s in range(8):
                    ready[f, :, pl.ds(pl.multiple_of(x * 1024 + 128 * s, 128), 128)] = tmp[i4, 8 * s : 8 * s + 6, :]
            return 0

        for i in range(2):
            lax.fori_loop(4 * i, 4 * i + 4, body, 0)
            writes[2 * f + i].start()
    for c in writes:
        c.wait()


def per_device(consts, state_before, before_start, after_start, time_step):
    f32 = jnp.float32
    st = jnp.transpose(state_before, (1, 0, 2))
    any_spec = pl.BlockSpec(memory_space=pl.ANY)
    smem = pl.BlockSpec(memory_space=pltpu.SMEM)
    vmem = pl.BlockSpec(memory_space=pltpu.VMEM)
    block = (5, 32, 8, 128)

    def scratch(*shape):
        return pltpu.VMEM(shape, f32)

    nb, added = pl.pallas_call(
        step_kernel,
        out_shape=(pltpu.VMEM((6,) + block, f32), jax.ShapeDtypeStruct((1, 1), f32)),
        in_specs=[any_spec, smem, smem] + [any_spec] * 6,
        out_specs=(vmem, smem),
        scratch_shapes=[
            scratch(5, 6, 32768),
            scratch(4, 64, 128),
            scratch(6, *block),
            scratch(*block),
            scratch(*block),
            scratch(*block),
            scratch(5, 1024, 128),
            scratch(5, 36 * 64, 128),
            scratch(5, 1024, 128),
            scratch(5, 1024, 128), scratch(5, 1024, 128),
            scratch(34 * 48, 128),
            scratch(1024, 128),
            scratch(1024, 128),
            scratch(2, 320, 128), scratch(2, 320, 128), scratch(2, 320, 128), scratch(2, 320, 128),
            scratch(2, 32, 128), scratch(2, 32, 128), scratch(2, 32, 128), scratch(2, 32, 128),
            scratch(16, 64, 128),
            scratch(16, 64, 128),
            scratch(512, 256),
            scratch(4, 256, 128),
            scratch(32, 8, 512),
            scratch(32, 8, 512),
            scratch(16, 64, 128),
            scratch(16, 64, 128),
            scratch(4, 16, 512),
            scratch(4, 16, 512),
            scratch(16, 8, 128),
            scratch(8, 8, 128),
            scratch(128, 128), scratch(128, 256), scratch(512, 512), scratch(512, 512),
            scratch(2, 8, 512),
            pltpu.VMEM((256, 256), jnp.bfloat16),
            pltpu.SemaphoreType.DMA((11,)),
            pltpu.SemaphoreType.DMA((N_SEM,)),
            pltpu.SemaphoreType.DMA((N_SEM,)),
        ],
        compiler_params=pltpu.CompilerParams(
            collective_id=0, has_side_effects=True, vmem_limit_bytes=58 * 1024 * 1024
        ),
        name="step",
    )(st, before_start, time_step.reshape(1, 1), *consts)

    where = jnp.stack([lax.axis_index("gx"), lax.axis_index("gy")]).astype(jnp.int32)
    out = pl.pallas_call(
        place_kernel,
        out_shape=jax.ShapeDtypeStruct((5, 6, 32768), f32),
        in_specs=[smem, smem, vmem],
        out_specs=any_spec,
        scratch_shapes=[
            scratch(4, 64, 128), scratch(5, 6, 32768), pltpu.SemaphoreType.DMA((10,)),
        ],
        compiler_params=pltpu.CompilerParams(vmem_limit_bytes=32 * 1024 * 1024),
        name="place",
    )(after_start, where, nb)
    return jnp.transpose(out, (1, 0, 2)), added.reshape(())


def solution(mesh):
    consts = tables()

    def run(*args):
        return per_device([jnp.asarray(c) for c in consts[:-1]] + [jnp.asarray(consts[-1], jnp.bfloat16)], *args)

    placed = (P(("gx", "gy"), None, None), P(), P(), P())
    return jax.shard_map(
        run,
        mesh=mesh,
        in_specs=placed,
        out_specs=(P(("gx", "gy"), None, None), P()),
        check_vma=False,
    )
```

```python
import jax
import jax.numpy as jnp
import numpy as np
from jax import lax
from jax.experimental import pallas as pl
from jax.experimental.pallas import tpu as pltpu
from jax.sharding import PartitionSpec as P

GAMMA = 5.0 / 3.0
FLOOR = 0.25
MESH = pl.DeviceIdType.MESH
HIGHEST = lax.Precision.HIGHEST

NK, NG, PART = 16, 8, 8


def tables():
    def sine(n):
        i = np.arange(1, n + 1)
        return np.sin(np.pi * ((i[:, None] * i[None, :]) % (2 * (n + 1))) / (n + 1))

    sine_x, sine_z = sine(512), sine(64)
    forward = np.zeros((8, 2, 8, 2, 64))
    for u in range(2):
        forward[:, u, :, u, :] = sine_z.reshape(8, 8, 64)
    forward = forward.reshape(128, 128)
    backward = forward * (2.0 / 65)
    padded = np.pad(backward.reshape(128, 2, 64), ((0, 0), (0, 0), (1, 1)))
    slope = (padded[:, :, 2:] - padded[:, :, :-2]).reshape(128, 128)
    order = np.arange(512).reshape(8, 2, 8, 4).transpose(0, 1, 3, 2).reshape(512)
    ordered = sine_x[order]
    modes_x = 2 - 2 * np.cos(np.pi * np.arange(1, 513) / 513)
    modes_z = 2 - 2 * np.cos(np.pi * np.arange(1, 65) / 65)
    h = 0.5 * (modes_z[:, None] + modes_x[None, :])
    root = np.sqrt(h * (h + 2))
    lam = 1 / (1 + h + root)
    gain = -0.5 / root

    table = np.stack([lam.reshape(8, 8, 512), gain.reshape(8, 8, 512)], axis=1)
    cell = np.arange(128)
    down = (cell[:, None] == cell - (cell % 64 > 0)).astype(np.float32)
    up = (cell[:, None] == cell + (cell % 64 < 63)).astype(np.float32)
    f32 = np.float32
    return (
        (forward * (4.0 / 64)).astype(f32),
        np.concatenate([backward, slope], axis=1).astype(f32),
        ordered.astype(f32),
        (ordered * (2.0 / 513)).astype(f32),
        table.astype(f32),
        np.tile(np.concatenate([down, up], axis=1), (2, 1)),
    )


def lanes():
    return lax.broadcasted_iota(jnp.int32, (8, 128), 1)


def swap4(parts):
    group = lanes() // 32
    low, even = group < 2, group % 2 == 0

    def pick(order):
        return jnp.where(low, jnp.where(even, order[0], order[1]), jnp.where(even, order[2], order[3]))

    turned = []
    for r in range(4):
        mixed = pick([parts[(i + r) % 4] for i in range(4)])
        turned.append(pltpu.roll(mixed, 32 * r, 1) if r else mixed)
    return [pick([turned[(b - j) % 4] for b in range(4)]) for j in range(4)]


def half_slope(down, up):
    quarter = 0.25 * (down + up)
    low = jnp.minimum(jnp.maximum(down, up), 0.0)
    high = jnp.maximum(jnp.minimum(down, up), 0.0)
    return jnp.minimum(jnp.maximum(quarter, low), high)


def face_flux(left, right, normal):
    def side(w):
        rho, vx, vy, vz, p = w
        gp = GAMMA * p
        return gp * lax.rsqrt(gp * rho), 0.5 * (vx * vx + vy * vy + vz * vz)

    sound_l, half_l = side(left)
    sound_r, half_r = side(right)
    ul, ur = left[1 + normal], right[1 + normal]
    fast = jnp.maximum(jnp.maximum(ul + sound_l, ur + sound_r), 0.0)
    slow = jnp.minimum(jnp.minimum(ul - sound_l, ur - sound_r), 0.0)
    inverse = 1.0 / (fast - slow)
    a, b = fast * inverse, slow * inverse
    d = fast * b
    kl, kr = a * ul - d, d - b * ur
    gl, gr = left[0] * kl, right[0] * kr
    apl, bpr = a * left[4], b * right[4]
    out = [gl + gr]
    for i in range(3):
        term = gl * left[1 + i] + gr * right[1 + i]
        out.append(term + (apl - bpr) if i == normal else term)
    out.append(
        1.5 * (left[4] * kl + right[4] * kr) + (gl * half_l + gr * half_r) + (apl * ul - bpr * ur)
    )
    return out


def cell_flux(w, normal):
    rho, p, u = w[0], w[4], w[1 + normal]
    mass = rho * u
    out = [mass]
    for i in range(3):
        out.append(mass * w[1 + i] + p if i == normal else mass * w[1 + i])
    half = 0.5 * (w[1] * w[1] + w[2] * w[2] + w[3] * w[3])
    out.append(2.5 * p * u + mass * half)
    return out


def at8(row):
    return pl.ds(pl.multiple_of(row, 8), 8)


EDGE, REST, HALO, PHI, AFTER, A2A, BACK, MOM_Z, MOM_Y, DEF_Y, DEF_X, DENSITY, N_SEM = (
    0, 2, 10, 20, 24, 32, 40, 48, 52, 56, 72, 80, 88,
)


def step_kernel(
    st, before, dt_ref, bz_h, bzi_h, sf_h, si_h, tab_h, move_h,
    nb, added,
    raw, tmp, dense, tail, next_head, prev_tail, cons, prim, acc, below, above, pot, pot0, potz,
    xs, xr, ys, yr, pxs, pxr, pys, pyr,
    spec_t, spec_r, lines, trans, held, vsol, back_t, back_r, mom_z, mom_y, defs, dgx,
    bz, bzi, sf, si, tab, move, load_sem, ss, rs,
):
    g, k = lax.axis_index("gx"), lax.axis_index("gy")
    k_up, k_dn = (k + 1) % NK, (k + NK - 1) % NK
    g_up, g_dn = (g + 1) % NG, (g + NG - 1) % NG
    dt = dt_ref[0, 0]
    lane = lanes()
    sub = lax.broadcasted_iota(jnp.int32, (8, 128), 0)
    zed = lane % 64

    loads = [pltpu.make_async_copy(st.at[f], raw.at[f], load_sem.at[f]) for f in range(5)]
    consts = [(bz_h, bz), (sf_h, sf), (tab_h.at[g], tab), (si_h, si), (bzi_h, bzi), (move_h, move)]
    const_loads = [
        pltpu.make_async_copy(a, b, load_sem.at[5 + i]) for i, (a, b) in enumerate(consts)
    ]
    for c in loads + const_loads:
        c.start()

    barrier = pltpu.get_barrier_semaphore()

    def greet_y(o, _):
        pl.semaphore_signal(barrier, inc=1, device_id={"gy": (k + o) % NK}, device_id_type=MESH)
        return 0

    def greet_x(o, _):
        pl.semaphore_signal(barrier, inc=1, device_id={"gx": (g + o) % NG}, device_id_type=MESH)
        return 0

    lax.fori_loop(1, NK, greet_y, 0)
    lax.fori_loop(1, NG, greet_x, 0)

    def send(src, dst, sem, device, rsem=None):
        return pltpu.make_async_remote_copy(
            src_ref=src, dst_ref=dst, send_sem=ss.at[sem], recv_sem=rs.at[sem if rsem is None else rsem],
            device_id=device, device_id_type=MESH,
        )

    begin = before[g, k]
    end = jnp.where(k < NK - 1, before[g, jnp.minimum(k + 1, NK - 1)], 4 * NK)
    lead, trail = jnp.clip(begin - 4 * k, -1, 1), jnp.clip(end - 4 * (k + 1), -1, 1)
    last = jnp.clip(end - begin - 1, 0, 5)

    def spread(f):
        def body(x4, _):
            for i4 in range(4):
                x = x4 * 4 + i4
                v = raw[f, :, pl.ds(pl.multiple_of(x * 1024, 1024), 1024)]
                for s in range(8):
                    tmp[i4, 8 * s : 8 * s + 6, :] = v[:, 128 * s : 128 * s + 128]
                for slot in range(6):
                    dense[slot, f, x] = tmp[i4, pl.ds(slot, 8, stride=8), :]
            return 0

        lax.fori_loop(0, 8, body, 0)

        def tails(x4, _):
            for i4 in range(4):
                tail[f, x4 * 4 + i4] = dense[last, f, x4 * 4 + i4]
            return 0

        lax.fori_loop(0, 8, tails, 0)

    def assemble(fields, first, count, step):
        def body(i, _):
            for f in fields:
                for i4 in range(step):
                    x = first + i * step + i4
                    q0 = jnp.where(lead > 0, prev_tail[f, x], dense[jnp.maximum(-lead, 0), f, x])
                    q1 = dense[1 - lead, f, x]
                    q2 = dense[2 - lead, f, x]
                    q3 = jnp.where(trail < 0, next_head[f, x], dense[3 - lead, f, x])
                    for j, v in enumerate(swap4((q0, q2, q1, q3))):
                        cons[f, at8(x * 32 + 8 * j), :] = v
            return 0

        lax.fori_loop(0, count // step, body, 0)

    loads[0].wait()
    spread(0)
    pl.semaphore_wait(barrier, NK + NG - 2)
    edges = [
        send(dense.at[0, 0], next_head.at[0], EDGE, {"gy": k_dn}),
        send(tail.at[0], prev_tail.at[0], EDGE + 1, {"gy": k_up}),
    ]
    rest = [
        [
            send(dense.at[0, pl.ds(1, 4), span], next_head.at[pl.ds(1, 4), span], REST + 2 * i, {"gy": k_dn}),
            send(tail.at[pl.ds(1, 4), span], prev_tail.at[pl.ds(1, 4), span], REST + 2 * i + 1, {"gy": k_up}),
        ]
        for i, span in enumerate(pl.ds(PART * i, PART) for i in range(32 // PART))
    ]
    for c in edges:
        c.start()
    for f in range(1, 5):
        loads[f].wait()
        spread(f)
    for c in rest[0]:
        c.start()
    for c in edges:
        c.wait_recv()
    assemble((0,), 0, 32, 4)
    for c in const_loads:
        c.wait()

    def primitives(x, _):
        for j in range(4):
            rho, mx, my, mz, energy = [cons[f, at8(x * 32 + 8 * j), :] for f in range(5)]
            inverse = 1.0 / rho
            vx, vy, vz = mx * inverse, my * inverse, mz * inverse
            p = (GAMMA - 1.0) * (energy - 0.5 * rho * (vx * vx + vy * vy + vz * vz))
            for f, v in enumerate((rho, vx, vy, vz, p)):
                prim[f, at8((x + 2) * 64 + (j + 2) * 8), :] = v
        return 0

    def neighbours_z(x8, _):
        for f in range(5):
            v = jnp.concatenate(
                [prim[f, pl.ds(pl.multiple_of((x8 * 8 + i + 2) * 64 + 16, 16), 32), :] for i in range(8)]
            )
            upper_half = v.astype(jnp.bfloat16)
            lower_half = (v - upper_half.astype(jnp.float32)).astype(jnp.bfloat16)
            both = jnp.dot(
                jnp.concatenate([upper_half, lower_half], axis=1), move[...],
                preferred_element_type=jnp.float32,
            )
            rows = pl.ds(pl.multiple_of(x8 * 256, 256), 256)
            below[f, rows, :] = both[:, 0:128]
            above[f, rows, :] = both[:, 128:256]
        return 0

    def sweep_z(x, _):
        for j in range(4):
            row = at8(x * 32 + 8 * j)
            w = [prim[f, at8((x + 2) * 64 + (j + 2) * 8), :] for f in range(5)]
            left, right = [], []
            for f, v in enumerate(w):
                h = half_slope(v - below[f, row, :], above[f, row, :] - v)
                left.append(v + h)
                lower = v - h
                right.append(jnp.where(zed == 63, lower, pltpu.roll(lower, 127, 1)))
            high = face_flux(left, right, 2)
            wall = cell_flux(w, 2)
            for f in range(5):
                low = jnp.where(zed == 0, wall[f], pltpu.roll(high[f], 1, 1))
                acc[f, row, :] = high[f] - low
        return 0

    def halo_y(part):
        span = pl.ds(80 * part, 80)
        return [
            send(ys.at[0, span], yr.at[1, span], HALO + 2 * part, {"gy": k_dn}),
            send(ys.at[1, span], yr.at[0, span], HALO + 2 * part + 1, {"gy": k_up}),
        ]

    halo_x = [
        send(xs.at[0], xr.at[1], HALO + 8, {"gx": g_dn}),
        send(xs.at[1], xr.at[0], HALO + 9, {"gx": g_up}),
    ]

    def halo_copies(part):
        return halo_y(part) + (halo_x[:1] if part == 0 else halo_x[1:] if part == 3 else [])

    def send_halo(part):
        for f in range(5):
            for r in range(2):
                row = part * 80 + f * 16 + r * 8
                base = (2 + PART * part) * 64 + r * 8
                ys[0, row : row + 8, :] = prim[f, pl.ds(base + 16, 8, stride=64), :]
                ys[1, row : row + 8, :] = prim[f, pl.ds(base + 39, 8, stride=64), :]
                for side, at in ((0, 0), (1, 3)):
                    if part == at:
                        row, base = f * 64 + r * 32, (2 + 30 * side + r) * 64 + 16
                        xs[side, row : row + 32, :] = prim[f, base : base + 32, :]
        return halo_copies(part)

    def start_part(part):
        for c in rest[part]:
            c.wait_recv()
        first = part * PART
        assemble((1, 2, 3, 4), first, PART, 2)
        lax.fori_loop(first, first + PART, primitives, 0)
        for c in send_halo(part):
            c.start()
        neighbours_z(part, 0)
        lax.fori_loop(first, first + PART, sweep_z, 0)

    modes = lax.dot_general(
        bz[...], cons[0], (((1,), (1,)), ((), ())),
        precision=HIGHEST, preferred_element_type=jnp.float32,
    )
    for r in range(16):
        for c in range(8):
            spec_t[r, 8 * c : 8 * c + 8, :] = modes[8 * r : 8 * r + 8, 128 * c : 128 * c + 128]

    def a2a_copy(peer, source):
        return send(
            spec_t.at[pl.ds(2 * peer, 2)], spec_r.at[pl.ds(2 * source, 2)],
            A2A + peer, {"gx": peer}, A2A + source,
        )

    def start_a2a(o, _):
        a2a_copy((g + o) % NG, g).start()
        return 0

    lax.fori_loop(1, NG, start_a2a, 0)
    for c in rest[1]:
        c.start()
    spec_r[pl.ds(2 * g, 2)] = spec_t[pl.ds(2 * g, 2)]
    start_part(0)
    for c in rest[2]:
        c.start()
    start_part(1)

    def wait_a2a(o, _):
        source = (g + NG - o) % NG
        a2a_copy(source, source).wait_recv()
        return 0

    lax.fori_loop(1, NG, wait_a2a, 0)
    for c in rest[3]:
        c.start()

    def to_lines(r, _):
        for q in range(2):
            parts = [spec_r[r, pl.ds(4 * q + b, 8, stride=8), :] for b in range(4)]
            for i, v in enumerate(swap4(parts)):
                lines[at8(r * 32 + 8 * i), 128 * q : 128 * q + 128] = v
        return 0

    lax.fori_loop(0, 16, to_lines, 0, unroll=2)
    lined = lax.dot_general(
        lines[...], sf[...], (((0,), (0,)), ((), ())),
        precision=HIGHEST, preferred_element_type=jnp.float32,
    )
    for t in range(4):
        trans[t] = lined[:, 128 * t : 128 * t + 128]

    k_four, k_in = k // 4, k % 4
    lam, gain = tab[0], tab[1]
    lam2 = lam * lam
    lam4 = lam2 * lam2
    lam8 = lam4 * lam4
    lam16 = lam8 * lam8
    lam32 = lam16 * lam16
    lam64 = lam32 * lam32
    lam128 = lam64 * lam64

    def line_rows(y):
        return pl.ds((y % 4) * 8 + y // 4, 8, stride=32)

    def line(y):
        return jnp.concatenate([trans[t, line_rows(y), :] for t in range(4)], axis=1)

    def sum_up(i, u):
        held[i] = line(i)
        return held[i] + lam * u

    def sum_down(i, v):
        return held[31 - i] + lam * v

    zero = jnp.zeros((8, 512), jnp.float32)
    up_sum = lax.fori_loop(0, 32, sum_up, zero)
    down_sum = lax.fori_loop(0, 32, sum_down, zero)
    mom_z[k_in, 0:8, :] = up_sum
    mom_z[k_in, 8:16, :] = down_sum

    def mom_z_copy(peer, source):
        return send(
            mom_z.at[source], mom_z.at[source], MOM_Z + peer, {"gy": 4 * k_four + peer}, MOM_Z + source
        )

    def mom_y_copy(peer, source):
        return send(
            mom_y.at[source], mom_y.at[source], MOM_Y + peer, {"gy": 4 * peer + k_in}, MOM_Y + source
        )

    for o in range(1, 4):
        mom_z_copy((k_in + o) % 4, k_in).start()
    start_part(2)
    for o in range(1, 4):
        source = (k_in + 4 - o) % 4
        mom_z_copy(source, source).wait_recv()
    from_low, from_high, four_up, four_down = zero, zero, zero, zero
    power_low, power_high = zero + 1.0, zero + 1.0
    for i in range(4):
        ups, downs = mom_z[i, 0:8, :], mom_z[3 - i, 8:16, :]
        four_up = four_up * lam32 + ups
        four_down = four_down * lam32 + downs
        from_low = jnp.where(i < k_in, from_low * lam32 + ups, from_low)
        from_high = jnp.where(3 - i > k_in, from_high * lam32 + downs, from_high)
        power_low = jnp.where(i < k_in, power_low * lam32, power_low)
        power_high = jnp.where(3 - i > k_in, power_high * lam32, power_high)
    mom_y[k_four, 0:8, :] = four_up
    mom_y[k_four, 8:16, :] = four_down
    for o in range(1, 4):
        mom_y_copy((k_four + o) % 4, k_four).start()
    start_part(3)
    for o in range(1, 4):
        source = (k_four + 4 - o) % 4
        mom_y_copy(source, source).wait_recv()

    far_low, far_high, at_start, at_end = zero, zero, zero, zero
    far_power_low, far_power_high = zero + 1.0, zero + 1.0
    for i in range(4):
        ups, downs = mom_y[i, 0:8, :], mom_y[3 - i, 8:16, :]
        at_end = at_end * lam128 + ups
        at_start = at_start * lam128 + downs
        far_low = jnp.where(i < k_four, far_low * lam128 + ups, far_low)
        far_high = jnp.where(3 - i > k_four, far_high * lam128 + downs, far_high)
        far_power_low = jnp.where(i < k_four, far_power_low * lam128, far_power_low)
        far_power_high = jnp.where(3 - i > k_four, far_power_high * lam128, far_power_high)
    lam256 = lam128 * lam128
    whole = lam256 * lam256 * lam
    at_start, at_end = lam * at_start, lam * at_end
    scale = 1.0 / (1.0 - whole * whole)
    low_image = (at_start - whole * at_end) * scale * far_power_low
    high_image = (at_end - whole * at_start) * scale * far_power_high
    first_u = from_low + power_low * (far_low - low_image)
    first_v = from_high + power_high * (far_high - high_image)

    def downward(i, v):
        v = held[31 - i] + lam * v
        vsol[31 - i] = v
        return v

    lax.fori_loop(0, 32, downward, first_v)

    def upward(i, u):
        carried = lam * u
        f = held[i]
        value = gain * (carried + vsol[i])
        for t in range(4):
            trans[t, line_rows(i), :] = value[:, 128 * t : 128 * t + 128]
        return f + carried

    lax.fori_loop(0, 32, upward, first_u)
    lines[...] = lax.dot_general(
        si[...], jnp.concatenate([trans[t] for t in range(4)], axis=1), (((1,), (1,)), ((), ())),
        precision=HIGHEST, preferred_element_type=jnp.float32,
    )

    def from_lines(r, _):
        for q in range(2):
            parts = [lines[at8(r * 32 + 8 * i), 128 * q : 128 * q + 128] for i in range(4)]
            for b, v in enumerate(swap4(parts)):
                back_t[r, pl.ds(4 * q + b, 8, stride=8), :] = v
        return 0

    lax.fori_loop(0, 16, from_lines, 0, unroll=2)

    def back_copy(peer, source):
        return send(
            back_t.at[pl.ds(2 * peer, 2)], back_r.at[pl.ds(2 * source, 2)],
            BACK + peer, {"gx": peer}, BACK + source,
        )

    def start_back(o, _):
        back_copy((g + o) % NG, g).start()
        return 0

    lax.fori_loop(1, NG, start_back, 0)
    back_r[pl.ds(2 * g, 2)] = back_t[pl.ds(2 * g, 2)]


    def place_halo_x():
        for c in halo_x:
            c.wait_recv()
        for f in range(5):
            for r in range(2):
                for j in range(4):
                    row = f * 64 + r * 32 + j * 8
                    e = (j + 2) * 8

                    def plane(xx):
                        return prim[f, (xx + 2) * 64 + e : (xx + 2) * 64 + e + 8, :]

                    low = pltpu.roll(jnp.where(lane >= 64, xr[0, row : row + 8, :], plane(30 + r)), 64, 1)
                    low = jnp.where((lane < 64) & (g == 0), plane(0), low)
                    prim[f, r * 64 + e : r * 64 + e + 8, :] = low
                    high = pltpu.roll(jnp.where(lane < 64, xr[1, row : row + 8, :], plane(r)), 64, 1)
                    high = jnp.where((lane >= 64) & (g == NG - 1), plane(31), high)
                    prim[f, (34 + r) * 64 + e : (34 + r) * 64 + e + 8, :] = high

    def place_y(x, _):
        base = (x + 2) * 64
        for f in range(5):
            rows = [prim[f, at8(base + 16 + 8 * j), :] for j in range(4)]
            first = jnp.broadcast_to(rows[0][0:1, :], (8, 128))
            final = jnp.broadcast_to(rows[3][7:8, :], (8, 128))
            for r in range(2):
                row = (x // PART) * 80 + f * 16 + r * 8 + x % PART
                low = jnp.where(k == 0, first, jnp.broadcast_to(yr[0, pl.ds(row, 1), :], (8, 128)))
                prim[f, at8(base + 8 * r), :] = jnp.where(sub == 0, low, pltpu.roll(rows[2 + r], 1, 0))
                high = jnp.where(k == NK - 1, final, jnp.broadcast_to(yr[1, pl.ds(row, 1), :], (8, 128)))
                prim[f, at8(base + 48 + 8 * r), :] = jnp.where(sub == 7, high, pltpu.roll(rows[r], 7, 0))
        return 0

    def place_halo_y(part):
        for c in halo_y(part):
            c.wait_recv()
        lax.fori_loop(PART * part, PART * part + PART, place_y, 0)

    def sweep_row(cell, count, normal, target):
        before_left, before_flux = None, None
        for i in range(-1, count + 1):
            left, right = [], []
            for f in range(5):
                v = cell(f, i)
                h = half_slope(v - cell(f, i - 1), cell(f, i + 1) - v)
                left.append(v + h)
                right.append(v - h)
            if before_left is not None:
                flux = face_flux(before_left, right, normal)
                if before_flux is not None:
                    for f in range(5):
                        row = target(i - 1)
                        acc[f, row, :] = acc[f, row, :] + (flux[f] - before_flux[f])
                before_flux = flux
            before_left = left

    def hydro(part):
        def sweep_y(i, _):
            x = part * PART + i
            base = (x + 2) * 64 + 16
            sweep_row(
                lambda f, e: prim[f, at8(base + 8 * e), :], 4, 1, lambda e: at8(x * 32 + 8 * e)
            )
            return 0

        lax.fori_loop(0, PART, sweep_y, 0)

        def sweep_x(j, _):
            base = (part * PART + 2) * 64 + 16 + 8 * j
            sweep_row(
                lambda f, i: prim[f, at8(base + 64 * i), :], PART, 0,
                lambda i: at8((part * PART + i) * 32 + 8 * j),
            )
            return 0

        lax.fori_loop(0, 4, sweep_x, 0)

    def finish(part):
        def body(i, _):
            x = part * PART + i
            base = (x + 1) * 48 + 8
            new = [[None] * 4 for _ in range(4)]
            half = -0.5 * dt
            for j in range(4):
                ax = half * (pot[at8(base + 48 + 8 * j), :] - pot[at8(base - 48 + 8 * j), :])
                ay = half * (pot[at8(base + 8 + 8 * j), :] - pot[at8(base - 8 + 8 * j), :])
                az = half * potz[at8(x * 32 + 8 * j), :]
                u = [cons[f, at8(x * 32 + 8 * j), :] for f in range(5)]
                change = [acc[f, at8(x * 32 + 8 * j), :] for f in range(5)]
                for i3, a in enumerate((ax, ay, az)):
                    new[i3][j] = u[1 + i3] - dt * change[1 + i3] + u[0] * a
                new[3][j] = u[4] - dt * change[4] + (u[1] * ax + u[2] * ay + u[3] * az)
            for f in range(4):
                b0, b2, b1, b3 = swap4(new[f])
                for q, v in enumerate((b0, b1, b2, b3)):
                    nb[1 + q, 1 + f, x] = v
            return 0

        lax.fori_loop(0, PART, body, 0)

    def after_copies(part):
        fields, span = pl.ds(1, 4), pl.ds(part * PART, PART)
        return [
            send(nb.at[1, fields, span], nb.at[5, fields, span], AFTER + part, {"gy": k_dn}),
            send(nb.at[4, fields, span], nb.at[0, fields, span], AFTER + 4 + part, {"gy": k_up}),
        ]

    def emit(part):
        for c in after_copies(part):
            c.start()

    def deficit(x, total):
        for j in range(4):
            row = at8(x * 32 + 8 * j)
            density = cons[0, row, :] - dt * acc[0, row, :]
            total = total + (jnp.maximum(density, FLOOR) - density)
        return total

    def def_copy(peer, source):
        return send(defs.at[source], defs.at[source], DEF_Y + peer, {"gy": peer}, DEF_Y + source)

    def start_def(o, _):
        def_copy((k + o) % NK, k).start()
        return 0

    def wait_def(o, _):
        source = (k + NK - o) % NK
        def_copy(source, source).wait_recv()
        return 0

    def density_copies(part):
        span = pl.ds(part * PART, PART)
        return [
            send(nb.at[1, 0, span], nb.at[5, 0, span], DENSITY + part, {"gy": k_dn}),
            send(nb.at[4, 0, span], nb.at[0, 0, span], DENSITY + 4 + part, {"gy": k_up}),
        ]

    def finish_density(part):
        def body(i2, _):
            for i in range(2):
                x = part * PART + i2 * 2 + i
                new = []
                for j in range(4):
                    row = at8(x * 32 + 8 * j)
                    new.append(jnp.maximum(cons[0, row, :] - dt * acc[0, row, :], FLOOR))
                b0, b2, b1, b3 = swap4(new)
                for q, v in enumerate((b0, b1, b2, b3)):
                    nb[1 + q, 0, x] = v
            return 0

        lax.fori_loop(0, PART // 2, body, 0)
        for c in density_copies(part):
            c.start()

    place_halo_y(1)
    hydro(1)
    finish_density(1)
    place_halo_y(2)
    hydro(2)
    finish_density(2)
    place_halo_x()
    place_halo_y(3)
    hydro(3)
    finish_density(3)

    def wait_back(o, _):
        source = (g + NG - o) % NG
        back_copy(source, source).wait_recv()
        return 0

    lax.fori_loop(1, NG, wait_back, 0)
    both = lax.dot_general(
        jnp.concatenate(
            [
                jnp.concatenate([back_r[r, 8 * c : 8 * c + 8, :] for c in range(8)], axis=1)
                for r in range(16)
            ]
        ),
        bzi[...], (((0,), (0,)), ((), ())),
        precision=HIGHEST, preferred_element_type=jnp.float32,
    )
    pot0[...] = both[:, 0:128]
    potz[...] = both[:, 128:256]
    pxs[0] = pot0[0:32, :]
    pxs[1] = pot0[31 * 32 : 32 * 32, :]
    for q in range(4):
        pys[0, 8 * q : 8 * q + 8, :] = pot0[pl.ds(8 * q * 32, 8, stride=32), :]
        pys[1, 8 * q : 8 * q + 8, :] = pot0[pl.ds(8 * q * 32 + 31, 8, stride=32), :]
    phi_halo = [
        send(pxs.at[0], pxr.at[1], PHI, {"gx": g_dn}),
        send(pxs.at[1], pxr.at[0], PHI + 1, {"gx": g_up}),
        send(pys.at[0], pyr.at[1], PHI + 2, {"gy": k_dn}),
        send(pys.at[1], pyr.at[0], PHI + 3, {"gy": k_up}),
    ]
    for c in phi_halo:
        c.start()

    place_halo_y(0)
    hydro(0)
    defs[k] = lax.fori_loop(0, 32, deficit, jnp.zeros((8, 128), jnp.float32))
    lax.fori_loop(1, NK, start_def, 0)
    finish_density(0)
    for c in phi_halo:
        c.wait_recv()
    for j in range(4):
        low = pltpu.roll(
            jnp.where(lane >= 64, pxr[0, 8 * j : 8 * j + 8, :], pot0[31 * 32 + 8 * j : 31 * 32 + 8 * j + 8, :]), 64, 1
        )
        pot[8 + 8 * j : 16 + 8 * j, :] = jnp.where((lane < 64) & (g == 0), 0.0, low)
        high = pltpu.roll(jnp.where(lane < 64, pxr[1, 8 * j : 8 * j + 8, :], pot0[8 * j : 8 * j + 8, :]), 64, 1)
        pot[33 * 48 + 8 + 8 * j : 33 * 48 + 16 + 8 * j, :] = jnp.where((lane >= 64) & (g == NG - 1), 0.0, high)

    def place_pot(x, _):
        base = (x + 1) * 48
        rows = [pot0[at8(x * 32 + 8 * j), :] for j in range(4)]
        for j in range(4):
            pot[at8(base + 8 + 8 * j), :] = rows[j]
        low = jnp.where(k == 0, 0.0, jnp.broadcast_to(pyr[0, pl.ds(x, 1), :], (8, 128)))
        pot[at8(base), :] = jnp.where(sub == 0, low, pltpu.roll(rows[3], 1, 0))
        high = jnp.where(k == NK - 1, 0.0, jnp.broadcast_to(pyr[1, pl.ds(x, 1), :], (8, 128)))
        pot[at8(base + 40), :] = jnp.where(sub == 7, high, pltpu.roll(rows[0], 7, 0))
        return 0

    lax.fori_loop(0, 32, place_pot, 0)
    def finish_part(part):
        finish(part)
        emit(part)

    finish_part(1)
    finish_part(2)
    lax.fori_loop(1, NK, wait_def, 0)
    dgx[g] = jnp.sum(defs[...], axis=0)

    def dgx_copy(peer, source):
        return send(dgx.at[source], dgx.at[source], DEF_X + peer, {"gx": peer}, DEF_X + source)

    def start_dgx(o, _):
        dgx_copy((g + o) % NG, g).start()
        return 0

    def wait_dgx(o, _):
        source = (g + NG - o) % NG
        dgx_copy(source, source).wait_recv()
        return 0

    lax.fori_loop(1, NG, start_dgx, 0)
    for part in (0, 3):
        finish_part(part)
    lax.fori_loop(1, NG, wait_dgx, 0)
    added[0, 0] = jnp.sum(jnp.sum(dgx[...], axis=0)) * (1.0 / 512)

    halo = sum([halo_copies(part) for part in range(32 // PART)], [])
    for c in edges + sum(rest, []) + halo + phi_halo:
        c.wait_send()

    def sent_y(o, _):
        def_copy((k + o) % NK, k).wait_send()
        return 0

    def sent_x(o, _):
        peer = (g + o) % NG
        a2a_copy(peer, g).wait_send()
        back_copy(peer, g).wait_send()
        dgx_copy(peer, g).wait_send()
        return 0

    for o in range(1, 4):
        mom_z_copy((k_in + o) % 4, k_in).wait_send()
        mom_y_copy((k_four + o) % 4, k_four).wait_send()
    lax.fori_loop(1, NK, sent_y, 0)
    lax.fori_loop(1, NG, sent_x, 0)
    for part in range(32 // PART):
        for c in density_copies(part) + after_copies(part):
            c.wait()


def place_kernel(after, where, nb, out, tmp, ready, sem):
    g, k = where[0], where[1]
    begin = after[g, k]
    end = jnp.where(k < NK - 1, after[g, jnp.minimum(k + 1, NK - 1)], 4 * NK)
    lead, held = jnp.clip(begin - 4 * k, -1, 1), end - begin
    halves = [pl.ds(0, 16384), pl.ds(16384, 16384)]
    writes = [
        pltpu.make_async_copy(ready.at[f, :, h], out.at[f, :, h], sem.at[2 * f + i])
        for f in range(5)
        for i, h in enumerate(halves)
    ]
    for f in range(5):

        def body(x4, _):
            for i4 in range(4):
                x = x4 * 4 + i4
                for slot in range(6):
                    index = jnp.minimum(slot + lead + 1, 5)
                    v = jnp.where(slot < held, nb[index, f, x], 0.0)
                    tmp[i4, pl.ds(slot, 8, stride=8), :] = v
                for s in range(8):
                    ready[f, :, pl.ds(pl.multiple_of(x * 1024 + 128 * s, 128), 128)] = tmp[i4, 8 * s : 8 * s + 6, :]
            return 0

        for i in range(2):
            lax.fori_loop(4 * i, 4 * i + 4, body, 0)
            writes[2 * f + i].start()
    for c in writes:
        c.wait()


def per_device(consts, state_before, before_start, after_start, time_step):
    f32 = jnp.float32
    st = jnp.transpose(state_before, (1, 0, 2))
    any_spec = pl.BlockSpec(memory_space=pl.ANY)
    smem = pl.BlockSpec(memory_space=pltpu.SMEM)
    vmem = pl.BlockSpec(memory_space=pltpu.VMEM)
    block = (5, 32, 8, 128)

    def scratch(*shape):
        return pltpu.VMEM(shape, f32)

    nb, added = pl.pallas_call(
        step_kernel,
        out_shape=(pltpu.VMEM((6,) + block, f32), jax.ShapeDtypeStruct((1, 1), f32)),
        in_specs=[any_spec, smem, smem] + [any_spec] * 6,
        out_specs=(vmem, smem),
        scratch_shapes=[
            scratch(5, 6, 32768),
            scratch(4, 64, 128),
            scratch(6, *block),
            scratch(*block),
            scratch(*block),
            scratch(*block),
            scratch(5, 1024, 128),
            scratch(5, 36 * 64, 128),
            scratch(5, 1024, 128),
            scratch(5, 1024, 128), scratch(5, 1024, 128),
            scratch(34 * 48, 128),
            scratch(1024, 128),
            scratch(1024, 128),
            scratch(2, 320, 128), scratch(2, 320, 128), scratch(2, 320, 128), scratch(2, 320, 128),
            scratch(2, 32, 128), scratch(2, 32, 128), scratch(2, 32, 128), scratch(2, 32, 128),
            scratch(16, 64, 128),
            scratch(16, 64, 128),
            scratch(512, 256),
            scratch(4, 256, 128),
            scratch(32, 8, 512),
            scratch(32, 8, 512),
            scratch(16, 64, 128),
            scratch(16, 64, 128),
            scratch(4, 16, 512),
            scratch(4, 16, 512),
            scratch(16, 8, 128),
            scratch(8, 8, 128),
            scratch(128, 128), scratch(128, 256), scratch(512, 512), scratch(512, 512),
            scratch(2, 8, 512),
            pltpu.VMEM((256, 256), jnp.bfloat16),
            pltpu.SemaphoreType.DMA((11,)),
            pltpu.SemaphoreType.DMA((N_SEM,)),
            pltpu.SemaphoreType.DMA((N_SEM,)),
        ],
        compiler_params=pltpu.CompilerParams(
            collective_id=0, has_side_effects=True, vmem_limit_bytes=58 * 1024 * 1024
        ),
        name="step",
    )(st, before_start, time_step.reshape(1, 1), *consts)

    where = jnp.stack([lax.axis_index("gx"), lax.axis_index("gy")]).astype(jnp.int32)
    out = pl.pallas_call(
        place_kernel,
        out_shape=jax.ShapeDtypeStruct((5, 6, 32768), f32),
        in_specs=[smem, smem, vmem],
        out_specs=any_spec,
        scratch_shapes=[
            scratch(4, 64, 128), scratch(5, 6, 32768), pltpu.SemaphoreType.DMA((10,)),
        ],
        compiler_params=pltpu.CompilerParams(vmem_limit_bytes=32 * 1024 * 1024),
        name="place",
    )(after_start, where, nb)
    return jnp.transpose(out, (1, 0, 2)), added.reshape(())


def solution(mesh):
    consts = tables()

    def run(*args):
        return per_device([jnp.asarray(c) for c in consts[:-1]] + [jnp.asarray(consts[-1], jnp.bfloat16)], *args)

    placed = (P(("gx", "gy"), None, None), P(), P(), P())
    return jax.shard_map(
        run,
        mesh=mesh,
        in_specs=placed,
        out_specs=(P(("gx", "gy"), None, None), P()),
        check_vma=False,
    )
```
